256 devices in a mesh: chain: 64 (over z, y, core), col: 4 (over x).
Axes of the slice: x: 4, y: 4, z: 8, core: 2. Of those that a mesh axis runs over, the one named last changes fastest.
Arguments:
- rhs: bfloat16 [4, 64, 32, 128], P(None, 'chain'), may hold values from -6 to 6
- pattern: int32 [4, 64, 24], P(None, 'chain', 'col'), may hold values from 0 to 255, as said below
- factor: bfloat16 [4, 64, 24, 128, 128], P(None, 'chain', 'col'), may hold values from -0.1875 to 0.1875
- inverse: bfloat16 [4, 64, 128, 128], P(None, 'chain'), as said below
- level_size: int32 [6], replicated, may hold values from 1 to 64, 256 in all
Outputs:
- half_solved: bfloat16 [4, 64, 32, 128], P(None, 'chain')
- solved: bfloat16 [4, 64, 32, 128], P(None, 'chain')
The draws below stay inside these ranges and needn't reach their ends.
Inputs may be any that keep to these rules, and one draw needn't show every extreme that they name: Among the pattern entries held by one index of chain and one index of col (all 4 of its block rows), at most 2 name block rows on any one index of chain (block row mod 64); in every such group exactly 2 name block rows on one index of chain that is common to all groups of that index of col. A block row may name a block row more than once. `inverse`: each block is lower triangular with a diagonal between 0.3 and 2.
All inputs are finite; a program needn't handle non-finite values.
Results may differ from the reference program's by a relative error of at most 0.013.
Values may be sent and summed in bfloat16 or wider, within the bound.
No kernel may reach another device: no remote copies, remote signals or barrier semaphores. Data moves between devices by JAX's collectives and lax.ppermute only.
A program may use at most 64 MiB of HBM per device.

```python
import math
import jax
import jax.numpy as jnp
import numpy as np
from jax import lax

BLOCK = 128
NNZ = 24
PROBES = 32
ROWS_DEV = 4
LEVELS = 6
BLOCK_ROWS = 256
CAP = 2
N_CHAIN = 64
N_COL = 4


def draw_pattern(key, part):
    entries = NNZ // N_COL
    count = ROWS_DEV * entries
    runs = (count + CAP - 1) // CAP
    key_first = jax.random.fold_in(key, 21)
    key_perm = jax.random.fold_in(key, 22)
    key_base = jax.random.fold_in(key, 23)
    first = jax.random.randint(key_first, (N_COL,), 0, N_CHAIN, dtype=jnp.int32)
    group_keys = jax.random.split(key_perm, N_CHAIN * N_COL)
    others = jax.vmap(lambda single: jax.random.permutation(single, N_CHAIN - 1))(group_keys)
    others = others.astype(jnp.int32).reshape(N_CHAIN, N_COL, N_CHAIN - 1)
    firsts = jnp.broadcast_to(first[None, :, None], (N_CHAIN, N_COL, 1))
    order = jnp.concatenate([firsts, (firsts + 1 + others) % N_CHAIN], axis=2)
    positions = jnp.arange(count, dtype=jnp.int32)
    run_ids = positions // CAP
    lane = order[:, :, run_ids]
    base = jax.random.randint(key_base, (N_CHAIN, N_COL, runs), 0, ROWS_DEV, dtype=jnp.int32)
    quotient = (base[:, :, run_ids] + (positions % CAP)[None, None, :]) % ROWS_DEV
    column = quotient * N_CHAIN + lane
    column = column.reshape(N_CHAIN, N_COL, ROWS_DEV, entries).transpose(2, 0, 1, 3)
    return column.reshape(ROWS_DEV, N_CHAIN, NNZ).astype(jnp.int32)


def draw_inverse(key, part):
    key_diag = jax.random.fold_in(key, 11)
    key_low = jax.random.fold_in(key, 12)
    diagonal = jax.random.uniform(key_diag, (ROWS_DEV, N_CHAIN, BLOCK), jnp.float32, 0.5, 1.5)
    lower = jax.random.normal(key_low, (ROWS_DEV, N_CHAIN, BLOCK, BLOCK), jnp.float32)
    lower = jnp.tril(lower, -1) * (0.6 / jnp.sqrt(BLOCK * 1.0))
    eye = jnp.eye(BLOCK, dtype=jnp.float32)
    return (lower + diagonal[..., None] * eye).astype(jnp.bfloat16)


def level_of(key, extent, shards, smallest, largest):
    def one(axis_at, blocks):
        steps = jax.random.uniform(jax.random.fold_in(jax.random.fold_in(key, 6), axis_at), (blocks,), jnp.float32, smallest / len(shards), largest / len(shards))
        return jnp.repeat(jnp.exp(steps), extent[axis_at] // blocks).reshape((-1,) + (1,) * (len(extent) - axis_at - 1))

    level = one(*shards[0])
    for cut in shards[1:]:
        level = level * one(*cut)
    return level


def split_up(number_of, total, bound, lean):
    weights = [(1 << 20) // math.isqrt(grade ** lean) + 1 for grade in range(2, number_of + 1)]
    spare, counts = total - bound - (number_of - 1), [1] * (number_of - 1)
    while spare > 0:
        movable = [i for i in range(number_of - 1) if counts[i] < bound]
        whole, remaining = sum([weights[i] for i in movable]), spare
        for i in movable:
            extra = min(bound - counts[i], max(1, remaining * weights[i] // whole), spare)
            counts[i] = counts[i] + extra
            spare = spare - extra
    return np.array([bound] + counts)


def uneven(own_key, amount, total, most, slope):
    if amount == 2:
        one = jax.random.randint(own_key, (), max(1, total - most), min(most, total - 1) + 1)
        return jnp.stack([one, total - one])
    sizes = jnp.asarray(split_up(amount, total, most, slope), jnp.int32)
    couples = (amount - 1) // 2
    donor, taker = sizes[1:1 + 2 * couples:2], sizes[2:2 + 2 * couples:2]
    margin = jnp.minimum(donor - 1, most - taker)
    passed = jax.random.randint(jax.random.fold_in(own_key, 1), (couples,), 0, 1 << 20) % (margin + 1)
    sizes = sizes.at[1:1 + 2 * couples:2].set(donor - passed).at[2:2 + 2 * couples:2].set(taker + passed)
    return sizes[jax.random.permutation(jax.random.fold_in(own_key, 2), amount)]


def scatter_about(stream_key, shape, width, limit, cuts=(), held_as=jnp.bfloat16):
    result = width * jax.random.normal(stream_key, shape, jnp.float32)
    if cuts:
        result = result * level_of(stream_key, shape, cuts, -0.22, 0.18)
    return jnp.clip(result, -limit, limit).astype(held_as)


def setup_inputs(seed: int = 0) -> dict:
    seeds = jax.random.split(jax.random.key(seed), 6)
    rhs = scatter_about(seeds[0], (ROWS_DEV, N_CHAIN, PROBES, BLOCK), 1.0, 6.0, ((1, 64),))
    pattern = draw_pattern(jax.random.fold_in(seeds[5], 71), 0)
    factor = scatter_about(seeds[2], (ROWS_DEV, N_CHAIN, NNZ, BLOCK, BLOCK), (BLOCK * NNZ // 3) ** -0.5, 0.1875, ((1, 64), (2, 4)))
    inverse = draw_inverse(jax.random.fold_in(seeds[5], 71), 0)
    level_size = uneven(seeds[4], LEVELS, BLOCK_ROWS, N_CHAIN, 0).astype(jnp.int32)
    return {"rhs": rhs, "pattern": pattern, "factor": factor, "inverse": inverse, "level_size": level_size}


def level_index(positions, ends):
    return jnp.sum((positions[..., None] >= ends).astype(jnp.int32), axis=-1)


def reference(rhs, pattern, factor, inverse, level_size):
    total = ROWS_DEV * N_CHAIN
    right = rhs.reshape(total, PROBES, BLOCK)
    columns = pattern.reshape(total, NNZ).astype(jnp.int32)
    blocks = factor.reshape(total, NNZ, BLOCK, BLOCK)
    inverse_rows = inverse.reshape(total, BLOCK, BLOCK)
    ends = jnp.cumsum(level_size).astype(jnp.int32)
    row_level = level_index(jnp.arange(total, dtype=jnp.int32), ends)
    keep = level_index(columns, ends) < row_level[:, None]

    def forward(store, row_id):
        chosen = jnp.where(keep[row_id][:, None, None], store[columns[row_id]], 0).astype(jnp.float32)
        partial_value = jnp.einsum("jpb,jcb->pc", chosen, blocks[row_id].astype(jnp.float32), precision=lax.Precision.HIGHEST)
        rest = (right[row_id].astype(jnp.float32) - partial_value).astype(jnp.bfloat16)
        segment = jnp.dot(rest, inverse_rows[row_id].T, preferred_element_type=jnp.float32).astype(jnp.bfloat16)
        return store.at[row_id].set(segment), None

    store, _ = lax.scan(forward, jnp.zeros((total, PROBES, BLOCK), jnp.bfloat16), jnp.arange(total, dtype=jnp.int32))

    def backward(accum, row_id):
        rest = (store[row_id].astype(jnp.float32) - accum[row_id]).astype(jnp.bfloat16)
        segment = jnp.dot(rest, inverse_rows[row_id], preferred_element_type=jnp.float32).astype(jnp.bfloat16)
        terms = jnp.einsum("pc,jcb->jpb", segment.astype(jnp.float32), blocks[row_id].astype(jnp.float32), precision=lax.Precision.HIGHEST)
        terms = jnp.where(keep[row_id][:, None, None], terms, 0.0)
        accum = accum.at[columns[row_id]].add(terms)
        return accum, segment

    _, solved = lax.scan(backward, jnp.zeros((total, PROBES, BLOCK), jnp.float32), jnp.arange(total, dtype=jnp.int32), reverse=True)
    return store.reshape(rhs.shape), solved.reshape(rhs.shape)
```

```python
import functools
import jax
import jax.numpy as jnp
from jax import lax
from jax.experimental import pallas as pl
from jax.experimental.pallas import tpu as pltpu
from jax.sharding import PartitionSpec as P

BF16 = jnp.bfloat16
F32 = jnp.float32
NT = (((1,), (1,)), ((), ()))
NN = (((1,), (0,)), ((), ()))


def locate(level, sizes, lanes, rows):
    lane = lax.axis_index("chain")
    start = jnp.int32(0)
    for k in range(level):
        start = start + sizes[k]
    slot = (start - lane + (lanes - 1)) // lanes
    live = (slot < rows) & (slot * lanes + lane < start + sizes[level])
    return jnp.minimum(slot, rows - 1), live


def start_all(copies):
    for c in copies:
        c.start()


def wait_all(copies):
    for c in copies:
        c.wait()


def factor_copies(cols, entries, slot, fac, fbuf, sems, base):
    return [
        pltpu.make_async_copy(
            fac.at[q, pl.ds(slot * entries, entries)],
            fbuf.at[pl.ds(q * entries, entries)],
            sems.at[base + q],
        )
        for q in range(cols)
    ]


def wide(fbuf, total):
    return jnp.concatenate([fbuf[j] for j in range(total)], axis=1)


def half_segment(level, lanes, total, slot, index, rest, inv, fbuf, store):
    if level > 0:
        chosen = jnp.concatenate(
            [
                store[jnp.minimum(index[slot * total + j], level * lanes)]
                for j in range(total)
            ],
            axis=1,
        )
        summed = lax.dot_general(
            chosen, wide(fbuf, total), NT, preferred_element_type=F32
        )
        rest = (rest.astype(F32) - summed).astype(BF16)
    return lax.dot_general(rest, inv, NT, preferred_element_type=F32).astype(BF16)


def forward_first(lanes, rows, sizes, right, inverse, out, rbuf, ibuf, sems):
    slot, _ = locate(0, sizes, lanes, rows)
    copies = [
        pltpu.make_async_copy(right.at[slot], rbuf, sems.at[0]),
        pltpu.make_async_copy(inverse.at[slot], ibuf, sems.at[1]),
    ]
    start_all(copies)
    wait_all(copies)
    segment = half_segment(0, lanes, 0, slot, None, rbuf[...], ibuf[...], None, None)
    out[...] = jnp.broadcast_to(segment[None], out.shape)


def forward_level(level, lanes, rows, cols, entries, *refs):
    sizes, index, right, inverse, fac = refs[:5]
    earlier = refs[5 : 5 + level]
    out, rbuf, ibuf, fbuf, store, sems = refs[5 + level :]
    total = cols * entries
    slot, _ = locate(level, sizes, lanes, rows)
    copies = [
        pltpu.make_async_copy(right.at[slot], rbuf, sems.at[0]),
        pltpu.make_async_copy(inverse.at[slot], ibuf, sems.at[1]),
    ]
    copies += [
        pltpu.make_async_copy(
            earlier[k], store.at[pl.ds(k * lanes, lanes)], sems.at[2 + k]
        )
        for k in range(level)
    ]
    copies += factor_copies(cols, entries, slot, fac, fbuf, sems, 2 + level)
    start_all(copies)
    store[level * lanes] = jnp.zeros(store.shape[1:], BF16)
    wait_all(copies)
    segment = half_segment(
        level, lanes, total, slot, index, rbuf[...], ibuf[...], fbuf, store
    )
    out[...] = jnp.broadcast_to(segment[None], out.shape)


def add_terms(level, lanes, total, slot, live, index, segment, fbuf, acc):
    segment = jnp.where(live, segment.astype(F32), 0.0).astype(BF16)
    terms = lax.dot_general(segment, wide(fbuf, total), NN, preferred_element_type=F32)
    width = segment.shape[1]
    for j in range(total):
        at = jnp.minimum(index[slot * total + j], level * lanes)
        acc[at] = acc[at] + terms[:, j * width : (j + 1) * width]


def turn_level(level, lanes, rows, cols, entries, *refs):
    sizes, index, right, inverse, fac = refs[:5]
    earlier = refs[5 : 5 + level]
    half, solved, kept, out, rbuf, ibuf, fbuf, store, acc, sems = refs[5 + level :]
    total = cols * entries
    slot, live = locate(level, sizes, lanes, rows)
    copies = [
        pltpu.make_async_copy(right.at[slot], rbuf, sems.at[0]),
        pltpu.make_async_copy(inverse.at[slot], ibuf, sems.at[1]),
    ]
    copies += [
        pltpu.make_async_copy(
            earlier[k], store.at[pl.ds(k * lanes, lanes)], sems.at[2 + k]
        )
        for k in range(level)
    ]
    copies += factor_copies(cols, entries, slot, fac, fbuf, sems, 2 + level)
    start_all(copies)
    store[level * lanes] = jnp.zeros(store.shape[1:], BF16)
    acc[...] = jnp.zeros(acc.shape, F32)
    wait_all(copies)
    segment = half_segment(
        level, lanes, total, slot, index, rbuf[...], ibuf[...], fbuf, store
    )
    half[...] = segment
    segment = lax.dot_general(
        segment, ibuf[...], NN, preferred_element_type=F32
    ).astype(BF16)
    solved[...] = segment
    add_terms(level, lanes, total, slot, live, index, segment, fbuf, acc)
    below = (level - 1) * lanes
    save = pltpu.make_async_copy(acc.at[pl.ds(0, below)], kept, sems.at[0])
    save.start()
    out[...] = acc[pl.ds(below, lanes)].astype(BF16)
    save.wait()


def backward_level(level, lanes, rows, cols, entries, *refs):
    sizes, index, inverse, fac, fronts, arrived, pending = refs[:7]
    refs = refs[7:]
    solved, refs = refs[0], refs[1:]
    kept = None
    if level > 1:
        kept, refs = refs[0], refs[1:]
    out, hbuf, ibuf, fbuf, tbuf, acc, sems = refs
    total = cols * entries
    slot, live = locate(level, sizes, lanes, rows)
    first = [
        pltpu.make_async_copy(arrived, tbuf, sems.at[0]),
        pltpu.make_async_copy(inverse.at[slot], ibuf, sems.at[1]),
        pltpu.make_async_copy(
            fronts.at[lax.axis_index("chain")], hbuf, sems.at[2]
        ),
    ]
    later = factor_copies(cols, entries, slot, fac, fbuf, sems, 3)
    later.append(
        pltpu.make_async_copy(
            pending, acc.at[pl.ds(0, level * lanes)], sems.at[3 + cols]
        )
    )
    start_all(first + later)
    wait_all(first)
    summed = jnp.sum(tbuf[...].astype(F32), axis=0)
    rest = (hbuf[...].astype(F32) - summed).astype(BF16)
    segment = lax.dot_general(rest, ibuf[...], NN, preferred_element_type=F32).astype(
        BF16
    )
    solved[...] = segment
    wait_all(later)
    add_terms(level, lanes, total, slot, live, index, segment, fbuf, acc)
    below = (level - 1) * lanes
    if kept is not None:
        save = pltpu.make_async_copy(acc.at[pl.ds(0, below)], kept, sems.at[0])
        save.start()
    out[...] = acc[pl.ds(below, lanes)].astype(BF16)
    if kept is not None:
        save.wait()


def finish(levels, lanes, rows, cols, *refs):
    sizes, inverse, arrived = refs[:3]
    fronts = refs[3 : 3 + levels - 1]
    refs = refs[3 + levels - 1 :]
    half_last = refs[0]
    done = refs[1:levels]
    out, hbuf, sbuf, ibuf, tbuf, sems = refs[levels:]
    lane = lax.axis_index("chain")
    slot, _ = locate(0, sizes, lanes, rows)
    first = [
        pltpu.make_async_copy(arrived, tbuf, sems.at[0]),
        pltpu.make_async_copy(inverse.at[slot], ibuf, sems.at[1]),
    ]
    first += [
        pltpu.make_async_copy(fronts[k].at[lane], hbuf.at[k], sems.at[2 + k])
        for k in range(levels - 1)
    ]
    first.append(
        pltpu.make_async_copy(half_last, hbuf.at[levels - 1], sems.at[1 + levels])
    )
    first += [
        pltpu.make_async_copy(done[k - 1], sbuf.at[k], sems.at[1 + levels + k])
        for k in range(1, levels)
    ]
    start_all(first)
    wait_all(first)
    summed = jnp.sum(tbuf[...].astype(F32), axis=0)
    rest = (hbuf[0].astype(F32) - summed).astype(BF16)
    sbuf[0] = lax.dot_general(rest, ibuf[...], NN, preferred_element_type=F32).astype(
        BF16
    )
    for r in range(rows):
        row = r * lanes + lane
        end = jnp.int32(0)
        level = jnp.int32(0)
        for k in range(levels):
            end = end + sizes[k]
            level = level + (row >= end).astype(jnp.int32)
        h, s = hbuf[level], sbuf[level]
        for q in range(cols):
            out[q, r] = h
            out[q, rows + r] = s


def per_device(rhs, pattern, factor, inverse, level_size):
    lanes = lax.axis_size("chain")
    cols = lax.axis_size("col")
    lane = lax.axis_index("chain")
    rows, _, probes, width = rhs.shape
    entries = pattern.shape[2]
    levels = level_size.shape[0]
    share = probes // cols
    total = cols * entries
    inverse = inverse[:, 0]
    right = lax.dynamic_index_in_dim(
        rhs.reshape(rows, cols, share, width), lax.axis_index("col"), 1, keepdims=False
    )

    smem = pl.BlockSpec(memory_space=pltpu.SMEM)
    hbm = pl.BlockSpec(memory_space=pl.ANY)
    vmem = pl.BlockSpec(memory_space=pltpu.VMEM)
    segment_shape = jax.ShapeDtypeStruct((share, width), BF16)
    front_shape = jax.ShapeDtypeStruct((lanes, share, width), BF16)
    params = pltpu.CompilerParams(vmem_limit_bytes=12 * 1024 * 1024)
    rbuf = pltpu.VMEM((share, width), BF16)
    ibuf = pltpu.VMEM((width, width), BF16)
    fbuf = pltpu.VMEM((total, width, width), BF16)

    def exchange(x):
        return lax.all_to_all(x, "chain", 0, 0, tiled=True)

    codes = jnp.pad(
        pattern.reshape(1, 1, rows * entries).astype(BF16),
        ((0, 0), (0, width - 1), (0, width - rows * entries)),
    )
    fac = lax.all_gather(
        jnp.concatenate([factor.reshape(rows * entries, width, width), codes]), "col"
    )
    columns = fac[:, rows * entries, 0, : rows * entries].astype(jnp.int32)
    columns = columns.reshape(cols, rows, entries).transpose(1, 0, 2)
    own_rows = jnp.arange(rows, dtype=jnp.int32) * lanes + lane
    own_level = jnp.zeros_like(own_rows)
    level = jnp.zeros_like(columns)
    end = jnp.int32(0)
    for k in range(levels):
        end = end + level_size[k]
        own_level += (own_rows >= end).astype(jnp.int32)
        level += (columns >= end).astype(jnp.int32)
    index = jnp.where(
        level < own_level[:, None, None],
        level * lanes + columns % lanes,
        levels * lanes,
    ).reshape(rows * total)

    first = pl.pallas_call(
        functools.partial(forward_first, lanes, rows),
        out_shape=front_shape,
        in_specs=[smem, hbm, hbm],
        out_specs=vmem,
        scratch_shapes=[rbuf, ibuf, pltpu.SemaphoreType.DMA((2,))],
        compiler_params=params,
        name="forward_first",
    )(level_size, right, inverse)
    fronts = [exchange(first)]
    for k in range(1, levels - 1):
        mine = pl.pallas_call(
            functools.partial(forward_level, k, lanes, rows, cols, entries),
            out_shape=front_shape,
            in_specs=[smem, smem, hbm, hbm, hbm] + [hbm] * k,
            out_specs=vmem,
            scratch_shapes=[
                rbuf,
                ibuf,
                fbuf,
                pltpu.VMEM((k * lanes + 1, share, width), BF16),
                pltpu.SemaphoreType.DMA((2 + k + cols,)),
            ],
            compiler_params=params,
            name=f"forward_level_{k}",
        )(level_size, index, right, inverse, fac, *fronts)
        fronts.append(exchange(mine))

    last = levels - 1
    half_last, solved, pending, terms = pl.pallas_call(
        functools.partial(turn_level, last, lanes, rows, cols, entries),
        out_shape=(
            segment_shape,
            segment_shape,
            jax.ShapeDtypeStruct(((last - 1) * lanes, share, width), F32),
            front_shape,
        ),
        in_specs=[smem, smem, hbm, hbm, hbm] + [hbm] * last,
        out_specs=(vmem, vmem, hbm, vmem),
        scratch_shapes=[
            rbuf,
            ibuf,
            fbuf,
            pltpu.VMEM((last * lanes + 1, share, width), BF16),
            pltpu.VMEM((last * lanes + 1, share, width), F32),
            pltpu.SemaphoreType.DMA((2 + last + cols,)),
        ],
        compiler_params=params,
        name="turn_level",
    )(level_size, index, right, inverse, fac, *fronts)
    done = [solved]
    for k in range(last - 1, 0, -1):
        arrived = exchange(terms)
        outs = [segment_shape]
        specs = [vmem]
        if k > 1:
            outs.append(jax.ShapeDtypeStruct(((k - 1) * lanes, share, width), F32))
            specs.append(hbm)
        got = pl.pallas_call(
            functools.partial(backward_level, k, lanes, rows, cols, entries),
            out_shape=(*outs, front_shape),
            in_specs=[smem, smem] + [hbm] * 5,
            out_specs=(*specs, vmem),
            scratch_shapes=[
                rbuf,
                ibuf,
                fbuf,
                pltpu.VMEM((lanes, share, width), BF16),
                pltpu.VMEM((k * lanes + 1, share, width), F32),
                pltpu.SemaphoreType.DMA((4 + cols,)),
            ],
            compiler_params=params,
            name=f"backward_level_{k}",
        )(level_size, index, inverse, fac, fronts[k], arrived, pending)
        solved, terms = got[0], got[-1]
        pending = got[1] if k > 1 else None
        done.insert(0, solved)
    arrived = exchange(terms)
    shares = pl.pallas_call(
        functools.partial(finish, levels, lanes, rows, cols),
        out_shape=jax.ShapeDtypeStruct((cols, 2 * rows, share, width), BF16),
        in_specs=[smem] + [hbm] * (2 + 2 * levels - 1),
        out_specs=vmem,
        scratch_shapes=[
            pltpu.VMEM((levels, share, width), BF16),
            pltpu.VMEM((levels, share, width), BF16),
            ibuf,
            pltpu.VMEM((lanes, share, width), BF16),
            pltpu.SemaphoreType.DMA((2 + 2 * levels,)),
        ],
        compiler_params=params,
        name="finish",
    )(level_size, inverse, arrived, *fronts, half_last, *done)
    whole = lax.all_to_all(shares, "col", 0, 0, tiled=True)
    whole = whole.transpose(1, 0, 2, 3).reshape(2, rows, 1, probes, width)
    return whole[0], whole[1]


def solution(mesh):
    return jax.shard_map(
        per_device,
        mesh=mesh,
        in_specs=(
            P(None, "chain", None, None),
            P(None, "chain", "col"),
            P(None, "chain", "col", None, None),
            P(None, "chain", None, None),
            P(),
        ),
        out_specs=(P(None, "chain", None, None), P(None, "chain", None, None)),
        check_vma=False,
    )
```

```python
import functools
import jax
import jax.numpy as jnp
from jax import lax
from jax.experimental import pallas as pl
from jax.experimental.pallas import tpu as pltpu
from jax.sharding import PartitionSpec as P

BF16 = jnp.bfloat16
F32 = jnp.float32
NT = (((1,), (1,)), ((), ()))
NN = (((1,), (0,)), ((), ()))
CODE_ROWS = 16


class Plan:
    def __init__(self, lanes, cols, rows, entries, share, width, levels):
        self.lanes, self.cols, self.rows, self.entries = lanes, cols, rows, entries
        self.share, self.width, self.levels = share, width, levels
        self.near = (rows + 1) // 2

    def slots(self, level):
        return max(0, self.rows - (self.levels - level)), min(level, self.rows - 1)


def locate(plan, level, sizes):
    lane = lax.axis_index("chain")
    start = jnp.int32(0)
    for k in range(level):
        start = start + sizes[k]
    slot = (start - lane + (plan.lanes - 1)) // plan.lanes
    live = (slot < plan.rows) & (
        slot * plan.lanes + lane < start + sizes[level]
    )
    low, high = plan.slots(level)
    return jnp.clip(slot, low, high), live


def block_at(plan, ref, slot, entry):
    at = pl.multiple_of((slot * plan.entries + entry) * plan.width, plan.width)
    return ref[pl.ds(at, plan.width), :]


def by_source(plan, level, slot, near, far, run):
    low, high = plan.slots(level)
    col = lax.axis_index("col")

    def near_entries():
        for s in range(plan.cols):
            for e in range(plan.entries):
                yield (
                    functools.partial(block_at, plan, near[s], slot, e),
                    (s * plan.rows + slot, e),
                )

    def far_entries():
        for q in range(plan.cols):
            s = lax.rem(col - q + plan.cols, plan.cols)
            for e in range(plan.entries):
                yield (
                    functools.partial(block_at, plan, far.at[q], slot - plan.near, e),
                    (s * plan.rows + slot, e),
                )

    if high < plan.near:
        run(list(near_entries()))
    elif low >= plan.near:
        run(list(far_entries()))
    else:

        @pl.when(slot < plan.near)
        def _():
            run(list(near_entries()))

        @pl.when(slot >= plan.near)
        def _():
            run(list(far_entries()))


def gather_store(plan, level, earlier, store):
    for k in range(level):
        store[pl.ds(k * plan.lanes, plan.lanes)] = earlier[k][...]
    store[level * plan.lanes] = jnp.zeros(store.shape[1:], BF16)


def half_segment(plan, level, slot, table, right, inverse, near, far, store, sums):
    def run(entries):
        chosen = jnp.concatenate(
            [store[jnp.minimum(table[at], level * plan.lanes)] for _, at in entries],
            axis=1,
        )
        weights = jnp.concatenate([load() for load, _ in entries], axis=1)
        sums[...] = lax.dot_general(chosen, weights, NT, preferred_element_type=F32)

    by_source(plan, level, slot, near, far, run)
    rest = right[slot, lax.axis_index("col")].astype(F32) - sums[...]
    return lax.dot_general(
        rest.astype(BF16), inverse[slot], NT, preferred_element_type=F32
    ).astype(BF16)


def add_terms(plan, level, slot, live, table, segment, near, far, acc):
    segment = jnp.where(live, segment.astype(F32), 0.0).astype(BF16)

    def run(entries):
        weights = jnp.concatenate([load() for load, _ in entries], axis=1)
        terms = lax.dot_general(segment, weights, NN, preferred_element_type=F32)
        for j, (_, place) in enumerate(entries):
            at = jnp.minimum(table[place], level * plan.lanes)
            acc[at] = acc[at] + terms[:, j * plan.width : (j + 1) * plan.width]

    by_source(plan, level, slot, near, far, run)


def forward_first(plan, *refs):
    pattern, factor, right, inverse, out, near, far, wide, code, sems = refs
    split = plan.near * plan.entries * plan.width
    left = plan.rows * plan.entries * plan.width - split
    copies = [
        pltpu.make_async_copy(
            factor.at[pl.ds(0, split)], near.at[pl.ds(0, split)], sems.at[0]
        ),
        pltpu.make_async_copy(factor.at[pl.ds(split, left)], far, sems.at[1]),
    ]
    for c in copies:
        c.start()
    wide[...] = jnp.zeros(wide.shape, F32)
    wide[pl.ds(0, plan.rows), pl.ds(0, plan.entries)] = pattern[:, 0, :].astype(F32)
    code[...] = wide[...].astype(BF16)
    last = pltpu.make_async_copy(code, near.at[pl.ds(split, CODE_ROWS)], sems.at[2])
    last.start()
    segment = lax.dot_general(
        right[0, lax.axis_index("col")], inverse[0], NT, preferred_element_type=F32
    ).astype(BF16)
    out[...] = jnp.broadcast_to(segment[None], out.shape)
    for c in copies:
        c.wait()
    last.wait()


def fill_table(plan, sizes, near, table):
    split = plan.near * plan.entries * plan.width
    lane = lax.axis_index("chain")
    columns = jnp.concatenate(
        [
            near[s][pl.ds(split, CODE_ROWS), :].astype(F32)[: plan.rows]
            for s in range(plan.cols)
        ],
        axis=0,
    ).astype(jnp.int32)
    places = lax.broadcasted_iota(jnp.int32, columns.shape, 0)
    own = lax.rem(places, plan.rows) * plan.lanes + lane
    level = jnp.zeros_like(columns)
    own_level = jnp.zeros_like(columns)
    end = jnp.int32(0)
    for k in range(plan.levels):
        end = end + sizes[k]
        level = level + (columns >= end).astype(jnp.int32)
        own_level = own_level + (own >= end).astype(jnp.int32)
    table[...] = jnp.where(
        level < own_level,
        level * plan.lanes + lax.rem(columns, plan.lanes),
        plan.levels * plan.lanes,
    )


def forward_second(plan, *refs):
    sizes, right, inverse, front = refs[:4]
    near = refs[4 : 4 + plan.cols]
    out, table, local, store, sums, sem = refs[4 + plan.cols :]
    fill_table(plan, sizes, near, table)
    copy = pltpu.make_async_copy(table, local, sem)
    copy.start()
    slot, _ = locate(plan, 1, sizes)
    gather_store(plan, 1, [front], store)
    copy.wait()
    segment = half_segment(
        plan, 1, slot, local, right, inverse, near, None, store, sums
    )
    out[...] = jnp.broadcast_to(segment[None], out.shape)


def forward_level(plan, level, *refs):
    sizes, table, right, inverse, far = refs[:5]
    near = refs[5 : 5 + plan.cols]
    earlier = refs[5 + plan.cols : 5 + plan.cols + level]
    out, store, sums = refs[5 + plan.cols + level :]
    slot, _ = locate(plan, level, sizes)
    gather_store(plan, level, earlier, store)
    segment = half_segment(
        plan, level, slot, table, right, inverse, near, far, store, sums
    )
    out[...] = jnp.broadcast_to(segment[None], out.shape)


def turn_level(plan, level, *refs):
    sizes, table, right, inverse, far = refs[:5]
    near = refs[5 : 5 + plan.cols]
    earlier = refs[5 + plan.cols : 5 + plan.cols + level]
    half, solved, acc, out, store, sums = refs[5 + plan.cols + level :]
    slot, live = locate(plan, level, sizes)
    gather_store(plan, level, earlier, store)
    acc[...] = jnp.zeros(acc.shape, F32)
    segment = half_segment(
        plan, level, slot, table, right, inverse, near, far, store, sums
    )
    half[...] = segment
    segment = lax.dot_general(
        segment, inverse[slot], NN, preferred_element_type=F32
    ).astype(BF16)
    solved[...] = segment
    add_terms(plan, level, slot, live, table, segment, near, far, acc)
    out[...] = acc[pl.ds((level - 1) * plan.lanes, plan.lanes)].astype(BF16)


def solve_back(slot, half, inverse, arrived):
    summed = jnp.sum(arrived[...].astype(F32), axis=0)
    rest = (half.astype(F32) - summed).astype(BF16)
    return lax.dot_general(
        rest, inverse[slot], NN, preferred_element_type=F32
    ).astype(BF16)


def backward_level(plan, level, *refs):
    sizes, table, inverse, front, arrived, _, far = refs[:7]
    near = refs[7 : 7 + plan.cols]
    solved, acc, out = refs[7 + plan.cols :]
    slot, live = locate(plan, level, sizes)
    segment = solve_back(slot, front[lax.axis_index("chain")], inverse, arrived)
    solved[...] = segment
    add_terms(plan, level, slot, live, table, segment, near, far, acc)
    out[...] = acc[pl.ds((level - 1) * plan.lanes, plan.lanes)].astype(BF16)


def finish(plan, *refs):
    levels = plan.levels
    sizes, inverse, arrived = refs[:3]
    fronts = refs[3 : 2 + levels]
    half_last = refs[2 + levels]
    done = refs[3 + levels : 2 + 2 * levels]
    out, hbuf, sbuf = refs[2 + 2 * levels :]
    lane = lax.axis_index("chain")
    for k in range(levels - 1):
        hbuf[k] = fronts[k][lane]
        sbuf[k + 1] = done[k][...]
    hbuf[levels - 1] = half_last[...]
    sbuf[0] = solve_back(0, hbuf[0], inverse, arrived)
    for r in range(plan.rows):
        row = r * plan.lanes + lane
        end = jnp.int32(0)
        level = jnp.int32(0)
        for k in range(levels):
            end = end + sizes[k]
            level = level + (row >= end).astype(jnp.int32)
        h, s = hbuf[level], sbuf[level]
        for q in range(plan.cols):
            out[q, r] = h
            out[q, plan.rows + r] = s


def per_device(rhs, pattern, factor, inverse, level_size):
    lanes = lax.axis_size("chain")
    cols = lax.axis_size("col")
    rows, _, probes, width = rhs.shape
    entries = pattern.shape[2]
    levels = level_size.shape[0]
    share = probes // cols
    plan = Plan(lanes, cols, rows, entries, share, width, levels)
    split = plan.near * entries * width
    left = rows * entries * width - split

    smem = pl.BlockSpec(memory_space=pltpu.SMEM)
    hbm = pl.BlockSpec(memory_space=pl.ANY)
    vmem = pl.BlockSpec(memory_space=pltpu.VMEM)
    segment_shape = pltpu.VMEM((share, width), BF16)
    front_shape = pltpu.VMEM((lanes, share, width), BF16)
    params = pltpu.CompilerParams(vmem_limit_bytes=12 * 1024 * 1024)
    sums = pltpu.VMEM((share, width), F32)

    def held(x):
        return pltpu.with_memory_space_constraint(x, pltpu.VMEM)

    def store(level):
        return pltpu.VMEM((level * lanes + 1, share, width), BF16)

    def exchange(x):
        return held(lax.all_to_all(x, "chain", 0, 0, tiled=True))

    inverse = held(inverse.reshape(rows, width, width))
    right = held(rhs.reshape(rows, cols, share, width))

    first, own, rest = pl.pallas_call(
        functools.partial(forward_first, plan),
        out_shape=(
            front_shape,
            pltpu.VMEM((split + CODE_ROWS, width), BF16),
            jax.ShapeDtypeStruct((left, width), BF16),
        ),
        in_specs=[vmem, hbm, vmem, vmem],
        out_specs=(vmem, vmem, hbm),
        scratch_shapes=[
            pltpu.VMEM((CODE_ROWS, width), F32),
            pltpu.VMEM((CODE_ROWS, width), BF16),
            pltpu.SemaphoreType.DMA((3,)),
        ],
        compiler_params=params,
        name="forward_first",
    )(pattern, factor.reshape(rows * entries * width, width), right, inverse)
    near = [held(own)] + [
        held(lax.ppermute(own, "col", [(i, (i + s) % cols) for i in range(cols)]))
        for s in range(1, cols)
    ]
    far = held(lax.all_gather(rest, "col"))
    fronts = [exchange(first)]

    mine, table = pl.pallas_call(
        functools.partial(forward_second, plan),
        out_shape=(front_shape, pltpu.VMEM((cols * rows, width), jnp.int32)),
        in_specs=[smem] + [vmem] * (3 + cols),
        out_specs=(vmem, vmem),
        scratch_shapes=[
            pltpu.SMEM((cols * rows, width), jnp.int32),
            store(1),
            sums,
            pltpu.SemaphoreType.DMA,
        ],
        compiler_params=params,
        name="forward_second",
    )(level_size, right, inverse, fronts[0], *near)
    fronts.append(exchange(mine))
    for k in range(2, levels - 1):
        mine = pl.pallas_call(
            functools.partial(forward_level, plan, k),
            out_shape=front_shape,
            in_specs=[smem, smem] + [vmem] * (3 + cols + k),
            out_specs=vmem,
            scratch_shapes=[store(k), sums],
            compiler_params=params,
            name=f"forward_level_{k}",
        )(level_size, table, right, inverse, far, *near, *fronts)
        fronts.append(exchange(mine))

    last = levels - 1
    acc_shape = pltpu.VMEM((last * lanes + 1, share, width), F32)
    half_last, solved, acc, terms = pl.pallas_call(
        functools.partial(turn_level, plan, last),
        out_shape=(segment_shape, segment_shape, acc_shape, front_shape),
        in_specs=[smem, smem] + [vmem] * (3 + cols + last),
        out_specs=(vmem,) * 4,
        scratch_shapes=[store(last), sums],
        compiler_params=params,
        name="turn_level",
    )(level_size, table, right, inverse, far, *near, *fronts)
    done = [held(solved)]
    for k in range(last - 1, 0, -1):
        solved, acc, terms = pl.pallas_call(
            functools.partial(backward_level, plan, k),
            out_shape=(segment_shape, acc_shape, front_shape),
            in_specs=[smem, smem] + [vmem] * (5 + cols),
            out_specs=(vmem,) * 3,
            input_output_aliases={5: 1},
            compiler_params=params,
            name=f"backward_level_{k}",
        )(
            level_size,
            table,
            inverse,
            fronts[k],
            exchange(terms),
            held(acc),
            far,
            *near,
        )
        done.insert(0, held(solved))
    shares = pl.pallas_call(
        functools.partial(finish, plan),
        out_shape=pltpu.VMEM((cols, 2 * rows, share, width), BF16),
        in_specs=[smem] + [vmem] * (1 + 2 * levels),
        out_specs=vmem,
        scratch_shapes=[
            pltpu.VMEM((levels, share, width), BF16),
            pltpu.VMEM((levels, share, width), BF16),
        ],
        compiler_params=params,
        name="finish",
    )(level_size, inverse, exchange(terms), *fronts, held(half_last), *done)
    whole = lax.all_to_all(shares, "col", 0, 0, tiled=True)
    whole = whole.transpose(1, 0, 2, 3).reshape(2, rows, 1, probes, width)
    return whole[0], whole[1]


def solution(mesh):
    return jax.shard_map(
        per_device,
        mesh=mesh,
        in_specs=(
            P(None, "chain", None, None),
            P(None, "chain", "col"),
            P(None, "chain", "col", None, None),
            P(None, "chain", None, None),
            P(),
        ),
        out_specs=(P(None, "chain", None, None), P(None, "chain", None, None)),
        check_vma=False,
    )
```

```python
import functools
import jax
import jax.numpy as jnp
from jax import lax
from jax.experimental import pallas as pl
from jax.experimental.pallas import tpu as pltpu
from jax.sharding import PartitionSpec as P

BF16 = jnp.bfloat16
F32 = jnp.float32
NT = (((1,), (1,)), ((), ()))
NN = (((1,), (0,)), ((), ()))
CODE_ROWS = 16
TABLE_ROWS = 8


class Plan:
    def __init__(self, lanes, cols, rows, entries, share, width, levels):
        self.lanes, self.cols, self.rows, self.entries = lanes, cols, rows, entries
        self.share, self.width, self.levels = share, width, levels
        self.deep = entries * width
        self.near = range(1, min(3, levels))
        self.far = range(min(3, levels), levels)

    def slots(self, level):
        return max(0, self.rows - (self.levels - level)), min(level, self.rows - 1)


def locate(plan, level, sizes):
    lane = lax.axis_index("chain")
    start = jnp.int32(0)
    for k in range(level):
        start = start + sizes[k]
    slot = (start - lane + (plan.lanes - 1)) // plan.lanes
    live = (slot < plan.rows) & (slot * plan.lanes + lane < start + sizes[level])
    low, high = plan.slots(level)
    return jnp.clip(slot, low, high), live


def factor_row(plan, factor, level, sizes):
    slot, _ = locate(plan, level, sizes)
    return factor.at[pl.ds(pl.multiple_of(slot * plan.deep, plan.deep), plan.deep)]


def weights_of(plan, level, sources):
    base = (level - (plan.near if level in plan.near else plan.far)[0]) * plan.deep
    return jnp.concatenate(
        [
            source[base + e * plan.width : base + (e + 1) * plan.width, :]
            for source in sources
            for e in range(plan.entries)
        ],
        axis=1,
    )


def places_of(plan, level, table):
    return [
        table[s * TABLE_ROWS + level, e]
        for s in range(plan.cols)
        for e in range(plan.entries)
    ]


def gather_store(plan, level, earlier, store):
    for k in range(level):
        store[pl.ds(k * plan.lanes, plan.lanes)] = earlier[k][...]
    store[level * plan.lanes] = jnp.zeros(store.shape[1:], BF16)


def half_segment(plan, level, table, right, inverse, sources, store):
    chosen = jnp.concatenate([store[at] for at in places_of(plan, level, table)], axis=1)
    weights = weights_of(plan, level, sources)
    summed = lax.dot_general(chosen, weights, NT, preferred_element_type=F32)
    rest = (right[level].astype(F32) - summed).astype(BF16)
    return lax.dot_general(
        rest, inverse[level], NT, preferred_element_type=F32
    ).astype(BF16)


def add_terms(plan, level, live, table, segment, sources, acc):
    segment = jnp.where(live, segment.astype(F32), 0.0).astype(BF16)
    weights = weights_of(plan, level, sources)
    terms = lax.dot_general(segment, weights, NN, preferred_element_type=F32)
    for j, at in enumerate(places_of(plan, level, table)):
        acc[at] = acc[at] + terms[:, j * plan.width : (j + 1) * plan.width]


def forward_first(plan, *refs):
    sizes, pattern, factor, right, inverse = refs[:5]
    out, near, rights, inverses, pats, wide, code, sems = refs[5:]
    col = lax.axis_index("col")
    slots = [locate(plan, k, sizes)[0] for k in range(plan.levels)]
    pick = pltpu.make_async_copy(pattern, pats, sems.at[0])
    pick.start()
    small = []
    for k in range(plan.levels):
        at = 1 + 2 * k
        small.append(
            pltpu.make_async_copy(inverse.at[slots[k]], inverses.at[k], sems.at[at])
        )
        small.append(
            pltpu.make_async_copy(
                right.at[slots[k], col], rights.at[k], sems.at[at + 1]
            )
        )
    for c in small:
        c.start()
    large = [
        pltpu.make_async_copy(
            factor_row(plan, factor, k, sizes),
            near.at[pl.ds(i * plan.deep, plan.deep)],
            sems.at[1 + 2 * plan.levels + i],
        )
        for i, k in enumerate(plan.near)
    ]
    for c in large:
        c.start()
    wide[...] = jnp.zeros(wide.shape, F32)
    pick.wait()
    for k in range(1, plan.levels):
        wide[pl.ds(k, 1), pl.ds(0, plan.entries)] = pats[slots[k]].astype(F32)
    code[...] = wide[...].astype(BF16)
    last = pltpu.make_async_copy(
        code,
        near.at[pl.ds(len(plan.near) * plan.deep, CODE_ROWS)],
        sems.at[1 + 2 * plan.levels + len(plan.near)],
    )
    last.start()
    small[0].wait()
    small[1].wait()
    segment = lax.dot_general(
        rights[0], inverses[0], NT, preferred_element_type=F32
    ).astype(BF16)
    out[...] = jnp.broadcast_to(segment[None], out.shape)
    for c in small[2:] + large:
        c.wait()
    last.wait()


def fill_table(plan, sizes, near, table):
    split = len(plan.near) * plan.deep
    columns = jnp.concatenate(
        [
            near[s][split : split + CODE_ROWS, :].astype(F32)[:TABLE_ROWS]
            for s in range(plan.cols)
        ],
        axis=0,
    ).astype(jnp.int32)
    own_level = lax.rem(lax.broadcasted_iota(jnp.int32, columns.shape, 0), TABLE_ROWS)
    level = jnp.zeros_like(columns)
    end = jnp.int32(0)
    for k in range(plan.levels):
        end = end + sizes[k]
        level = level + (columns >= end).astype(jnp.int32)
    table[...] = jnp.where(
        level < own_level,
        level * plan.lanes + lax.rem(columns, plan.lanes),
        own_level * plan.lanes,
    )


def forward_second(plan, *refs):
    sizes, factor, right, inverse, front = refs[:5]
    near = refs[5 : 5 + plan.cols]
    out, table, far, local, store, sems = refs[5 + plan.cols :]
    copies = [
        pltpu.make_async_copy(
            factor_row(plan, factor, k, sizes),
            far.at[pl.ds(i * plan.deep, plan.deep)],
            sems.at[1 + i],
        )
        for i, k in enumerate(plan.far)
    ]
    for c in copies:
        c.start()
    fill_table(plan, sizes, near, table)
    copy = pltpu.make_async_copy(table, local, sems.at[0])
    copy.start()
    gather_store(plan, 1, [front], store)
    copy.wait()
    segment = half_segment(plan, 1, local, right, inverse, near, store)
    out[...] = jnp.broadcast_to(segment[None], out.shape)
    for c in copies:
        c.wait()


def forward_level(plan, level, *refs):
    table, right, inverse = refs[:3]
    sources = refs[3 : 3 + plan.cols]
    earlier = refs[3 + plan.cols : 3 + plan.cols + level]
    out, store = refs[3 + plan.cols + level :]
    gather_store(plan, level, earlier, store)
    segment = half_segment(plan, level, table, right, inverse, sources, store)
    out[...] = jnp.broadcast_to(segment[None], out.shape)


def turn_level(plan, level, *refs):
    sizes, table, right, inverse = refs[:4]
    sources = refs[4 : 4 + plan.cols]
    earlier = refs[4 + plan.cols : 4 + plan.cols + level]
    half, solved, acc, out, store = refs[4 + plan.cols + level :]
    _, live = locate(plan, level, sizes)
    gather_store(plan, level, earlier, store)
    acc[...] = jnp.zeros(acc.shape, F32)
    segment = half_segment(plan, level, table, right, inverse, sources, store)
    half[...] = segment
    segment = lax.dot_general(
        segment, inverse[level], NN, preferred_element_type=F32
    ).astype(BF16)
    solved[...] = segment
    add_terms(plan, level, live, table, segment, sources, acc)
    out[...] = acc[pl.ds((level - 1) * plan.lanes, plan.lanes)].astype(BF16)


def solve_back(half, inverse, arrived):
    summed = jnp.sum(arrived[...].astype(F32), axis=0)
    rest = (half.astype(F32) - summed).astype(BF16)
    return lax.dot_general(rest, inverse, NN, preferred_element_type=F32).astype(BF16)


def backward_level(plan, level, *refs):
    sizes, table, inverse, front, arrived, _ = refs[:6]
    sources = refs[6 : 6 + plan.cols]
    solved, acc, out = refs[6 + plan.cols :]
    _, live = locate(plan, level, sizes)
    segment = solve_back(front[lax.axis_index("chain")], inverse[level], arrived)
    solved[...] = segment
    add_terms(plan, level, live, table, segment, sources, acc)
    out[...] = acc[pl.ds((level - 1) * plan.lanes, plan.lanes)].astype(BF16)


def finish(plan, *refs):
    levels = plan.levels
    sizes, inverse, arrived = refs[:3]
    fronts = refs[3 : 2 + levels]
    half_last = refs[2 + levels]
    done = refs[3 + levels : 2 + 2 * levels]
    out, hbuf, sbuf = refs[2 + 2 * levels :]
    lane = lax.axis_index("chain")
    for k in range(levels - 1):
        hbuf[k] = fronts[k][lane]
        sbuf[k + 1] = done[k][...]
    hbuf[levels - 1] = half_last[...]
    sbuf[0] = solve_back(hbuf[0], inverse[0], arrived)
    for r in range(plan.rows):
        row = r * plan.lanes + lane
        end = jnp.int32(0)
        level = jnp.int32(0)
        for k in range(levels):
            end = end + sizes[k]
            level = level + (row >= end).astype(jnp.int32)
        h, s = hbuf[level], sbuf[level]
        for q in range(plan.cols):
            out[q, r] = h
            out[q, plan.rows + r] = s


def per_device(rhs, pattern, factor, inverse, level_size):
    lanes = lax.axis_size("chain")
    cols = lax.axis_size("col")
    rows, _, probes, width = rhs.shape
    entries = pattern.shape[2]
    levels = level_size.shape[0]
    share = probes // cols
    plan = Plan(lanes, cols, rows, entries, share, width, levels)

    smem = pl.BlockSpec(memory_space=pltpu.SMEM)
    hbm = pl.BlockSpec(memory_space=pltpu.HBM)
    vmem = pl.BlockSpec(memory_space=pltpu.VMEM)
    segment_shape = pltpu.VMEM((share, width), BF16)
    front_shape = pltpu.VMEM((lanes, share, width), BF16)
    params = pltpu.CompilerParams(vmem_limit_bytes=12 * 1024 * 1024)

    def far_off(x):
        return pltpu.with_memory_space_constraint(x, pltpu.HBM)

    def held(x):
        return pltpu.with_memory_space_constraint(x, pltpu.VMEM)

    def store(level):
        return pltpu.VMEM((level * lanes + 1, share, width), BF16)

    def exchange(x):
        return held(lax.all_to_all(x, "chain", 0, 0, tiled=True))

    def around(x):
        return [held(x)] + [
            held(lax.ppermute(x, "col", [(i, (i + s) % cols) for i in range(cols)]))
            for s in range(1, cols)
        ]

    factor = far_off(factor.reshape(rows * plan.entries * width, width))
    first, own, rights, inverses = pl.pallas_call(
        functools.partial(forward_first, plan),
        out_shape=(
            front_shape,
            pltpu.VMEM((len(plan.near) * plan.deep + CODE_ROWS, width), BF16),
            pltpu.VMEM((levels, share, width), BF16),
            pltpu.VMEM((levels, width, width), BF16),
        ),
        in_specs=[smem, hbm, hbm, hbm, hbm],
        out_specs=(vmem,) * 4,
        scratch_shapes=[
            pltpu.VMEM((rows, 1, entries), jnp.int32),
            pltpu.VMEM((CODE_ROWS, width), F32),
            pltpu.VMEM((CODE_ROWS, width), BF16),
            pltpu.SemaphoreType.DMA((2 + 2 * levels + len(plan.near),)),
        ],
        compiler_params=params,
        name="forward_first",
    )(
        level_size,
        far_off(pattern),
        factor,
        far_off(rhs.reshape(rows, cols, share, width)),
        far_off(inverse.reshape(rows, width, width)),
    )
    rights, inverses = held(rights), held(inverses)
    near = around(own)
    fronts = [exchange(first)]

    mine, table, own = pl.pallas_call(
        functools.partial(forward_second, plan),
        out_shape=(
            front_shape,
            pltpu.VMEM((cols * TABLE_ROWS, width), jnp.int32),
            pltpu.VMEM((len(plan.far) * plan.deep, width), BF16),
        ),
        in_specs=[smem, hbm] + [vmem] * (3 + cols),
        out_specs=(vmem,) * 3,
        scratch_shapes=[
            pltpu.SMEM((cols * TABLE_ROWS, width), jnp.int32),
            store(1),
            pltpu.SemaphoreType.DMA((1 + len(plan.far),)),
        ],
        compiler_params=params,
        name="forward_second",
    )(level_size, factor, rights, inverses, fronts[0], *near)
    far = around(own)
    fronts.append(exchange(mine))

    def sources(level):
        return near if level in plan.near else far

    for k in range(2, levels - 1):
        mine = pl.pallas_call(
            functools.partial(forward_level, plan, k),
            out_shape=front_shape,
            in_specs=[smem] + [vmem] * (2 + cols + k),
            out_specs=vmem,
            scratch_shapes=[store(k)],
            compiler_params=params,
            name=f"forward_level_{k}",
        )(table, rights, inverses, *sources(k), *fronts)
        fronts.append(exchange(mine))

    last = levels - 1
    acc_shape = pltpu.VMEM((last * lanes + 1, share, width), F32)
    half_last, solved, acc, terms = pl.pallas_call(
        functools.partial(turn_level, plan, last),
        out_shape=(segment_shape, segment_shape, acc_shape, front_shape),
        in_specs=[smem, smem] + [vmem] * (2 + cols + last),
        out_specs=(vmem,) * 4,
        scratch_shapes=[store(last)],
        compiler_params=params,
        name="turn_level",
    )(level_size, table, rights, inverses, *sources(last), *fronts)
    done = [held(solved)]
    for k in range(last - 1, 0, -1):
        solved, acc, terms = pl.pallas_call(
            functools.partial(backward_level, plan, k),
            out_shape=(segment_shape, acc_shape, front_shape),
            in_specs=[smem, smem] + [vmem] * (4 + cols),
            out_specs=(vmem,) * 3,
            input_output_aliases={5: 1},
            compiler_params=params,
            name=f"backward_level_{k}",
        )(
            level_size,
            table,
            inverses,
            fronts[k],
            exchange(terms),
            held(acc),
            *sources(k),
        )
        done.insert(0, held(solved))
    shares = pl.pallas_call(
        functools.partial(finish, plan),
        out_shape=pltpu.VMEM((cols, 2 * rows, share, width), BF16),
        in_specs=[smem] + [vmem] * (1 + 2 * levels),
        out_specs=vmem,
        scratch_shapes=[
            pltpu.VMEM((levels, share, width), BF16),
            pltpu.VMEM((levels, share, width), BF16),
        ],
        compiler_params=params,
        name="finish",
    )(level_size, inverses, exchange(terms), *fronts, held(half_last), *done)
    whole = lax.all_to_all(shares, "col", 0, 0, tiled=True)
    whole = whole.transpose(1, 0, 2, 3).reshape(2, rows, 1, probes, width)
    return whole[0], whole[1]


def solution(mesh):
    return jax.shard_map(
        per_device,
        mesh=mesh,
        in_specs=(
            P(None, "chain", None, None),
            P(None, "chain", "col"),
            P(None, "chain", "col", None, None),
            P(None, "chain", None, None),
            P(),
        ),
        out_specs=(P(None, "chain", None, None), P(None, "chain", None, None)),
        check_vma=False,
    )
```

```python
import functools
import jax
import jax.numpy as jnp
from jax import lax
from jax.experimental import pallas as pl
from jax.experimental.pallas import tpu as pltpu
from jax.sharding import PartitionSpec as P

BF16 = jnp.bfloat16
F32 = jnp.float32
NT = (((1,), (1,)), ((), ()))
NN = (((1,), (0,)), ((), ()))
CODE_ROWS = 16
TABLE_ROWS = 8


class Plan:
    def __init__(self, lanes, cols, rows, entries, share, width, levels):
        self.lanes, self.cols, self.rows, self.entries = lanes, cols, rows, entries
        self.share, self.width, self.levels = share, width, levels
        self.deep = entries * width
        self.near = range(1, min(3, levels))
        self.far = range(min(3, levels), levels)

    def slots(self, level):
        return max(0, self.rows - (self.levels - level)), min(level, self.rows - 1)


def locate(plan, level, sizes):
    lane = lax.axis_index("chain")
    start = jnp.int32(0)
    for k in range(level):
        start = start + sizes[k]
    slot = (start - lane + (plan.lanes - 1)) // plan.lanes
    live = (slot < plan.rows) & (slot * plan.lanes + lane < start + sizes[level])
    low, high = plan.slots(level)
    return jnp.clip(slot, low, high), live


def factor_row(plan, factor, level, sizes):
    slot, _ = locate(plan, level, sizes)
    return factor.at[pl.ds(pl.multiple_of(slot * plan.deep, plan.deep), plan.deep)]


def weights_of(plan, level, sources):
    base = (level - (plan.near if level in plan.near else plan.far)[0]) * plan.deep
    return jnp.concatenate(
        [
            source[base + e * plan.width : base + (e + 1) * plan.width, :]
            for source in sources
            for e in range(plan.entries)
        ],
        axis=1,
    )


def places_of(plan, level, table):
    return [
        table[level, s * plan.entries + e]
        for s in range(plan.cols)
        for e in range(plan.entries)
    ]


def gather_store(plan, level, earlier, store):
    for k in range(level):
        store[pl.ds(k * plan.lanes, plan.lanes)] = earlier[k][...]
    store[level * plan.lanes] = jnp.zeros(store.shape[1:], BF16)


def half_segment(plan, level, table, right, inverse, sources, store):
    chosen = jnp.concatenate([store[at] for at in places_of(plan, level, table)], axis=1)
    weights = weights_of(plan, level, sources)
    summed = lax.dot_general(chosen, weights, NT, preferred_element_type=F32)
    rest = (right[level].astype(F32) - summed).astype(BF16)
    return lax.dot_general(
        rest, inverse[level], NT, preferred_element_type=F32
    ).astype(BF16)


def add_terms(plan, level, table, segment, sources, acc):
    weights = weights_of(plan, level, sources)
    terms = lax.dot_general(segment, weights, NN, preferred_element_type=F32)
    for j, at in enumerate(places_of(plan, level, table)):
        acc[at] = acc[at] + terms[:, j * plan.width : (j + 1) * plan.width]


def forward_first(plan, *refs):
    sizes, pattern, factor, right, inverse = refs[:5]
    out, near, rights, inverses, pats, wide, code, sems = refs[5:]
    col = lax.axis_index("col")
    slots = [locate(plan, k, sizes)[0] for k in range(plan.levels)]
    pick = pltpu.make_async_copy(pattern, pats, sems.at[0])
    pick.start()
    small = []
    for k in range(plan.levels):
        at = 1 + 2 * k
        small.append(
            pltpu.make_async_copy(inverse.at[slots[k]], inverses.at[k], sems.at[at])
        )
        small.append(
            pltpu.make_async_copy(
                right.at[slots[k], col], rights.at[k], sems.at[at + 1]
            )
        )
    for c in small:
        c.start()
    large = [
        pltpu.make_async_copy(
            factor_row(plan, factor, k, sizes),
            near.at[pl.ds(i * plan.deep, plan.deep)],
            sems.at[1 + 2 * plan.levels + i],
        )
        for i, k in enumerate(plan.near)
    ]
    for c in large:
        c.start()
    wide[...] = jnp.zeros(wide.shape, F32)
    pick.wait()
    for k in range(1, plan.levels):
        wide[pl.ds(k, 1), pl.ds(0, plan.entries)] = pats[slots[k]].astype(F32)
    code[...] = wide[...].astype(BF16)
    last = pltpu.make_async_copy(
        code,
        near.at[pl.ds(len(plan.near) * plan.deep, CODE_ROWS)],
        sems.at[1 + 2 * plan.levels + len(plan.near)],
    )
    last.start()
    small[0].wait()
    small[1].wait()
    segment = lax.dot_general(
        rights[0], inverses[0], NT, preferred_element_type=F32
    ).astype(BF16)
    out[...] = jnp.broadcast_to(segment[None], out.shape)
    for c in small[2:] + large:
        c.wait()
    last.wait()


def fill_table(plan, sizes, near, table):
    split = len(plan.near) * plan.deep
    shape = (TABLE_ROWS, plan.width)
    row_level = lax.broadcasted_iota(jnp.int32, shape, 0)
    entry = lax.broadcasted_iota(jnp.int32, shape, 1)
    alive = jnp.zeros(shape, jnp.int32)
    ends = []
    for k in range(plan.levels):
        ends.append((ends[-1] if ends else 0) + sizes[k])
        live = locate(plan, k, sizes)[1].astype(jnp.int32)
        alive = alive + jnp.where(row_level == k, live, 0)
    total = jnp.zeros(shape, jnp.int32)
    for s in range(plan.cols):
        columns = near[s][split : split + CODE_ROWS, :].astype(F32)[:TABLE_ROWS]
        columns = columns.astype(jnp.int32)
        level = jnp.zeros(shape, jnp.int32)
        for end in ends:
            level = level + (columns >= end).astype(jnp.int32)
        place = jnp.where(
            (level < row_level) & (alive > 0),
            level * plan.lanes + lax.rem(columns, plan.lanes),
            row_level * plan.lanes,
        )
        place = jnp.where(entry < plan.entries, place, 0)
        total = total + (pltpu.roll(place, s * plan.entries, 1) if s else place)
    table[...] = total


def forward_second(plan, *refs):
    sizes, factor, right, inverse, front = refs[:5]
    near = refs[5 : 5 + plan.cols]
    out, table, far, local, store, sems = refs[5 + plan.cols :]
    copies = [
        pltpu.make_async_copy(
            factor_row(plan, factor, k, sizes),
            far.at[pl.ds(i * plan.deep, plan.deep)],
            sems.at[1 + i],
        )
        for i, k in enumerate(plan.far)
    ]
    for c in copies:
        c.start()
    fill_table(plan, sizes, near, table)
    copy = pltpu.make_async_copy(table, local, sems.at[0])
    copy.start()
    gather_store(plan, 1, [front], store)
    copy.wait()
    segment = half_segment(plan, 1, local, right, inverse, near, store)
    out[...] = jnp.broadcast_to(segment[None], out.shape)
    for c in copies:
        c.wait()


def forward_level(plan, level, *refs):
    table, right, inverse = refs[:3]
    sources = refs[3 : 3 + plan.cols]
    earlier = refs[3 + plan.cols : 3 + plan.cols + level]
    out, store = refs[3 + plan.cols + level :]
    gather_store(plan, level, earlier, store)
    segment = half_segment(plan, level, table, right, inverse, sources, store)
    out[...] = jnp.broadcast_to(segment[None], out.shape)


def turn_level(plan, level, *refs):
    table, right, inverse = refs[:3]
    sources = refs[3 : 3 + plan.cols]
    earlier = refs[3 + plan.cols : 3 + plan.cols + level]
    half, solved, acc, out, store = refs[3 + plan.cols + level :]
    gather_store(plan, level, earlier, store)
    acc[...] = jnp.zeros(acc.shape, F32)
    segment = half_segment(plan, level, table, right, inverse, sources, store)
    half[...] = segment
    segment = lax.dot_general(
        segment, inverse[level], NN, preferred_element_type=F32
    ).astype(BF16)
    solved[...] = segment
    add_terms(plan, level, table, segment, sources, acc)
    out[...] = acc[pl.ds((level - 1) * plan.lanes, plan.lanes)].astype(BF16)


def solve_back(half, inverse, arrived):
    summed = jnp.sum(arrived[...].astype(F32), axis=0)
    rest = (half.astype(F32) - summed).astype(BF16)
    return lax.dot_general(rest, inverse, NN, preferred_element_type=F32).astype(BF16)


def backward_level(plan, level, *refs):
    table, inverse, front, arrived, _ = refs[:5]
    sources = refs[5 : 5 + plan.cols]
    solved, acc, out = refs[5 + plan.cols :]
    segment = solve_back(front[lax.axis_index("chain")], inverse[level], arrived)
    solved[...] = segment
    add_terms(plan, level, table, segment, sources, acc)
    out[...] = acc[pl.ds((level - 1) * plan.lanes, plan.lanes)].astype(BF16)


def finish(plan, *refs):
    levels = plan.levels
    sizes, inverse, arrived = refs[:3]
    fronts = refs[3 : 2 + levels]
    half_last = refs[2 + levels]
    done = refs[3 + levels : 2 + 2 * levels]
    out, hbuf, sbuf = refs[2 + 2 * levels :]
    lane = lax.axis_index("chain")
    for k in range(levels - 1):
        hbuf[k] = fronts[k][lane]
        sbuf[k + 1] = done[k][...]
    hbuf[levels - 1] = half_last[...]
    sbuf[0] = solve_back(hbuf[0], inverse[0], arrived)
    for r in range(plan.rows):
        row = r * plan.lanes + lane
        end = jnp.int32(0)
        level = jnp.int32(0)
        for k in range(levels):
            end = end + sizes[k]
            level = level + (row >= end).astype(jnp.int32)
        h, s = hbuf[level], sbuf[level]
        for q in range(plan.cols):
            out[q, r] = h
            out[q, plan.rows + r] = s


def per_device(rhs, pattern, factor, inverse, level_size):
    lanes = lax.axis_size("chain")
    cols = lax.axis_size("col")
    rows, _, probes, width = rhs.shape
    entries = pattern.shape[2]
    levels = level_size.shape[0]
    share = probes // cols
    plan = Plan(lanes, cols, rows, entries, share, width, levels)

    smem = pl.BlockSpec(memory_space=pltpu.SMEM)
    hbm = pl.BlockSpec(memory_space=pltpu.HBM)
    vmem = pl.BlockSpec(memory_space=pltpu.VMEM)
    segment_shape = pltpu.VMEM((share, width), BF16)
    front_shape = pltpu.VMEM((lanes, share, width), BF16)
    params = pltpu.CompilerParams(vmem_limit_bytes=12 * 1024 * 1024)

    def far_off(x):
        return pltpu.with_memory_space_constraint(x, pltpu.HBM)

    def held(x):
        return pltpu.with_memory_space_constraint(x, pltpu.VMEM)

    def store(level):
        return pltpu.VMEM((level * lanes + 1, share, width), BF16)

    def exchange(x):
        return held(lax.all_to_all(x, "chain", 0, 0, tiled=True))

    def around(x):
        return [held(x)] + [
            held(lax.ppermute(x, "col", [(i, (i + s) % cols) for i in range(cols)]))
            for s in range(1, cols)
        ]

    factor = far_off(factor.reshape(rows * plan.entries * width, width))
    first, own, rights, inverses = pl.pallas_call(
        functools.partial(forward_first, plan),
        out_shape=(
            front_shape,
            pltpu.VMEM((len(plan.near) * plan.deep + CODE_ROWS, width), BF16),
            pltpu.VMEM((levels, share, width), BF16),
            pltpu.VMEM((levels, width, width), BF16),
        ),
        in_specs=[smem, hbm, hbm, hbm, hbm],
        out_specs=(vmem,) * 4,
        scratch_shapes=[
            pltpu.VMEM((rows, 1, entries), jnp.int32),
            pltpu.VMEM((CODE_ROWS, width), F32),
            pltpu.VMEM((CODE_ROWS, width), BF16),
            pltpu.SemaphoreType.DMA((2 + 2 * levels + len(plan.near),)),
        ],
        compiler_params=params,
        name="forward_first",
    )(
        level_size,
        far_off(pattern),
        factor,
        far_off(rhs.reshape(rows, cols, share, width)),
        far_off(inverse.reshape(rows, width, width)),
    )
    rights, inverses = held(rights), held(inverses)
    near = around(own)
    fronts = [exchange(first)]

    mine, table, own = pl.pallas_call(
        functools.partial(forward_second, plan),
        out_shape=(
            front_shape,
            pltpu.VMEM((TABLE_ROWS, width), jnp.int32),
            pltpu.VMEM((len(plan.far) * plan.deep, width), BF16),
        ),
        in_specs=[smem, hbm] + [vmem] * (3 + cols),
        out_specs=(vmem,) * 3,
        scratch_shapes=[
            pltpu.SMEM((TABLE_ROWS, width), jnp.int32),
            store(1),
            pltpu.SemaphoreType.DMA((1 + len(plan.far),)),
        ],
        compiler_params=params,
        name="forward_second",
    )(level_size, factor, rights, inverses, fronts[0], *near)
    far = around(own)
    fronts.append(exchange(mine))

    def sources(level):
        return near if level in plan.near else far

    for k in range(2, levels - 1):
        mine = pl.pallas_call(
            functools.partial(forward_level, plan, k),
            out_shape=front_shape,
            in_specs=[smem] + [vmem] * (2 + cols + k),
            out_specs=vmem,
            scratch_shapes=[store(k)],
            compiler_params=params,
            name=f"forward_level_{k}",
        )(table, rights, inverses, *sources(k), *fronts)
        fronts.append(exchange(mine))

    last = levels - 1
    acc_shape = pltpu.VMEM((last * lanes + 1, share, width), F32)
    half_last, solved, acc, terms = pl.pallas_call(
        functools.partial(turn_level, plan, last),
        out_shape=(segment_shape, segment_shape, acc_shape, front_shape),
        in_specs=[smem] + [vmem] * (2 + cols + last),
        out_specs=(vmem,) * 4,
        scratch_shapes=[store(last)],
        compiler_params=params,
        name="turn_level",
    )(table, rights, inverses, *sources(last), *fronts)
    done = [held(solved)]
    for k in range(last - 1, 0, -1):
        solved, acc, terms = pl.pallas_call(
            functools.partial(backward_level, plan, k),
            out_shape=(segment_shape, acc_shape, front_shape),
            in_specs=[smem] + [vmem] * (4 + cols),
            out_specs=(vmem,) * 3,
            input_output_aliases={4: 1},
            compiler_params=params,
            name=f"backward_level_{k}",
        )(
            table,
            inverses,
            fronts[k],
            exchange(terms),
            held(acc),
            *sources(k),
        )
        done.insert(0, held(solved))
    shares = pl.pallas_call(
        functools.partial(finish, plan),
        out_shape=pltpu.VMEM((cols, 2 * rows, share, width), BF16),
        in_specs=[smem] + [vmem] * (1 + 2 * levels),
        out_specs=vmem,
        scratch_shapes=[
            pltpu.VMEM((levels, share, width), BF16),
            pltpu.VMEM((levels, share, width), BF16),
        ],
        compiler_params=params,
        name="finish",
    )(level_size, inverses, exchange(terms), *fronts, held(half_last), *done)
    whole = lax.all_to_all(shares, "col", 0, 0, tiled=True)
    whole = whole.transpose(1, 0, 2, 3).reshape(2, rows, 1, probes, width)
    return whole[0], whole[1]


def solution(mesh):
    return jax.shard_map(
        per_device,
        mesh=mesh,
        in_specs=(
            P(None, "chain", None, None),
            P(None, "chain", "col"),
            P(None, "chain", "col", None, None),
            P(None, "chain", None, None),
            P(),
        ),
        out_specs=(P(None, "chain", None, None), P(None, "chain", None, None)),
        check_vma=False,
    )
```

```python
import functools
import jax
import jax.numpy as jnp
from jax import lax
from jax.experimental import pallas as pl
from jax.experimental.pallas import tpu as pltpu
from jax.sharding import PartitionSpec as P

BF16 = jnp.bfloat16
F32 = jnp.float32
NT = (((1,), (1,)), ((), ()))
NN = (((1,), (0,)), ((), ()))
CODE_ROWS = 16
TABLE_ROWS = 8


class Plan:
    def __init__(self, lanes, cols, rows, entries, share, width, levels):
        self.lanes, self.cols, self.rows, self.entries = lanes, cols, rows, entries
        self.share, self.width, self.levels = share, width, levels
        self.deep = entries * width
        self.near = range(1, min(3, levels))
        self.far = range(min(3, levels), levels)

    def slots(self, level):
        return max(0, self.rows - (self.levels - level)), min(level, self.rows - 1)


def locate(plan, level, sizes):
    lane = lax.axis_index("chain")
    start = jnp.int32(0)
    for k in range(level):
        start = start + sizes[k]
    slot = (start - lane + (plan.lanes - 1)) // plan.lanes
    live = (slot < plan.rows) & (slot * plan.lanes + lane < start + sizes[level])
    low, high = plan.slots(level)
    return jnp.clip(slot, low, high), live


def factor_row(plan, factor, level, sizes):
    slot, _ = locate(plan, level, sizes)
    return factor.at[pl.ds(pl.multiple_of(slot * plan.deep, plan.deep), plan.deep)]


def weights_of(plan, level, sources):
    base = (level - (plan.near if level in plan.near else plan.far)[0]) * plan.deep
    return jnp.concatenate(
        [
            source[base + e * plan.width : base + (e + 1) * plan.width, :]
            for source in sources
            for e in range(plan.entries)
        ],
        axis=1,
    )


def places_of(plan, level, table):
    return [
        table[level, s * plan.entries + e]
        for s in range(plan.cols)
        for e in range(plan.entries)
    ]


def gather_store(plan, level, earlier, store):
    for k in range(level):
        store[pl.ds(k * plan.lanes, plan.lanes)] = earlier[k][...]
    store[level * plan.lanes] = jnp.zeros(store.shape[1:], BF16)


def half_segment(plan, level, table, right, inverse, sources, store):
    chosen = jnp.concatenate([store[at] for at in places_of(plan, level, table)], axis=1)
    weights = weights_of(plan, level, sources)
    summed = lax.dot_general(chosen, weights, NT, preferred_element_type=F32)
    rest = (right[level].astype(F32) - summed).astype(BF16)
    return lax.dot_general(
        rest, inverse[level], NT, preferred_element_type=F32
    ).astype(BF16)


def add_terms(plan, level, table, segment, sources, acc):
    weights = weights_of(plan, level, sources)
    terms = lax.dot_general(segment, weights, NN, preferred_element_type=F32)
    for j, at in enumerate(places_of(plan, level, table)):
        acc[at] = acc[at] + terms[:, j * plan.width : (j + 1) * plan.width]


def forward_first(plan, *refs):
    level_size, pattern, factor, right, inverse = refs[:5]
    out, near, rights, inverses, sizes, pats, wide, code, sems = refs[5:]
    col = lax.axis_index("col")
    pick = pltpu.make_async_copy(pattern, pats, sems.at[0])
    learn = pltpu.make_async_copy(
        level_size, sizes, sems.at[2 + 2 * plan.levels + len(plan.near)]
    )
    learn.start()
    pick.start()

    def pair(level, slot):
        at = 1 + 2 * level
        return [
            pltpu.make_async_copy(inverse.at[slot], inverses.at[level], sems.at[at]),
            pltpu.make_async_copy(
                right.at[slot, col], rights.at[level], sems.at[at + 1]
            ),
        ]

    small = pair(0, 0)
    for c in small:
        c.start()
    wide[...] = jnp.zeros(wide.shape, F32)
    learn.wait()
    slots = [locate(plan, k, sizes)[0] for k in range(plan.levels)]
    large = [
        pltpu.make_async_copy(
            factor_row(plan, factor, k, sizes),
            near.at[pl.ds(i * plan.deep, plan.deep)],
            sems.at[1 + 2 * plan.levels + i],
        )
        for i, k in enumerate(plan.near)
    ]
    for c in large:
        c.start()
    for k in range(1, plan.levels):
        more = pair(k, slots[k])
        for c in more:
            c.start()
        small += more
    pick.wait()
    for k in range(1, plan.levels):
        wide[pl.ds(k, 1), pl.ds(0, plan.entries)] = pats[slots[k]].astype(F32)
    code[...] = wide[...].astype(BF16)
    last = pltpu.make_async_copy(
        code,
        near.at[pl.ds(len(plan.near) * plan.deep, CODE_ROWS)],
        sems.at[1 + 2 * plan.levels + len(plan.near)],
    )
    last.start()
    small[0].wait()
    small[1].wait()
    segment = lax.dot_general(
        rights[0], inverses[0], NT, preferred_element_type=F32
    ).astype(BF16)
    out[...] = jnp.broadcast_to(segment[None], out.shape)
    for c in small[2:] + large:
        c.wait()
    last.wait()


def fill_table(plan, sizes, near, table):
    split = len(plan.near) * plan.deep
    shape = (TABLE_ROWS, plan.width)
    row_level = lax.broadcasted_iota(jnp.int32, shape, 0)
    entry = lax.broadcasted_iota(jnp.int32, shape, 1)
    alive = jnp.zeros(shape, jnp.int32)
    ends = []
    for k in range(plan.levels):
        ends.append((ends[-1] if ends else 0) + sizes[k])
        live = locate(plan, k, sizes)[1].astype(jnp.int32)
        alive = alive + jnp.where(row_level == k, live, 0)
    total = jnp.zeros(shape, jnp.int32)
    for s in range(plan.cols):
        columns = near[s][split : split + CODE_ROWS, :].astype(F32)[:TABLE_ROWS]
        columns = columns.astype(jnp.int32)
        level = jnp.zeros(shape, jnp.int32)
        for end in ends:
            level = level + (columns >= end).astype(jnp.int32)
        place = jnp.where(
            (level < row_level) & (alive > 0),
            level * plan.lanes + lax.rem(columns, plan.lanes),
            row_level * plan.lanes,
        )
        place = jnp.where(entry < plan.entries, place, 0)
        total = total + (pltpu.roll(place, s * plan.entries, 1) if s else place)
    own = entry * plan.lanes + lax.axis_index("chain")
    own_level = jnp.zeros(shape, jnp.int32)
    for end in ends:
        own_level = own_level + (own >= end).astype(jnp.int32)
    table[...] = jnp.where(row_level == TABLE_ROWS - 1, own_level, total)


def forward_second(plan, *refs):
    sizes, factor, right, inverse, front = refs[:5]
    near = refs[5 : 5 + plan.cols]
    out, table, far, draft, store, sems = refs[5 + plan.cols :]
    copies = [
        pltpu.make_async_copy(
            factor_row(plan, factor, k, sizes),
            far.at[pl.ds(i * plan.deep, plan.deep)],
            sems.at[1 + i],
        )
        for i, k in enumerate(plan.far)
    ]
    for c in copies:
        c.start()
    fill_table(plan, sizes, near, draft)
    copy = pltpu.make_async_copy(draft, table, sems.at[0])
    copy.start()
    gather_store(plan, 1, [front], store)
    copy.wait()
    segment = half_segment(plan, 1, table, right, inverse, near, store)
    out[...] = jnp.broadcast_to(segment[None], out.shape)
    for c in copies:
        c.wait()


def forward_level(plan, level, *refs):
    table, right, inverse = refs[:3]
    sources = refs[3 : 3 + plan.cols]
    earlier = refs[3 + plan.cols : 3 + plan.cols + level]
    out, store = refs[3 + plan.cols + level :]
    gather_store(plan, level, earlier, store)
    segment = half_segment(plan, level, table, right, inverse, sources, store)
    out[...] = jnp.broadcast_to(segment[None], out.shape)


def turn_level(plan, level, *refs):
    table, right, inverse = refs[:3]
    sources = refs[3 : 3 + plan.cols]
    earlier = refs[3 + plan.cols : 3 + plan.cols + level]
    half, solved, acc, out, store = refs[3 + plan.cols + level :]
    gather_store(plan, level, earlier, store)
    acc[...] = jnp.zeros(acc.shape, F32)
    segment = half_segment(plan, level, table, right, inverse, sources, store)
    half[...] = segment
    segment = lax.dot_general(
        segment, inverse[level], NN, preferred_element_type=F32
    ).astype(BF16)
    solved[...] = segment
    add_terms(plan, level, table, segment, sources, acc)
    out[...] = acc[pl.ds((level - 1) * plan.lanes, plan.lanes)].astype(BF16)


def solve_back(half, inverse, arrived):
    summed = jnp.sum(arrived[...].astype(F32), axis=0)
    rest = (half.astype(F32) - summed).astype(BF16)
    return lax.dot_general(rest, inverse, NN, preferred_element_type=F32).astype(BF16)


def backward_level(plan, level, *refs):
    table, inverse, front, arrived, _ = refs[:5]
    sources = refs[5 : 5 + plan.cols]
    solved, acc, out = refs[5 + plan.cols :]
    segment = solve_back(front[lax.axis_index("chain")], inverse[level], arrived)
    solved[...] = segment
    add_terms(plan, level, table, segment, sources, acc)
    out[...] = acc[pl.ds((level - 1) * plan.lanes, plan.lanes)].astype(BF16)


def finish(plan, *refs):
    levels = plan.levels
    table, inverse, arrived = refs[:3]
    fronts = refs[3 : 2 + levels]
    half_last = refs[2 + levels]
    done = refs[3 + levels : 2 + 2 * levels]
    out, hbuf, sbuf = refs[2 + 2 * levels :]
    lane = lax.axis_index("chain")
    for k in range(levels - 1):
        hbuf[k] = fronts[k][lane]
        sbuf[k + 1] = done[k][...]
    hbuf[levels - 1] = half_last[...]
    sbuf[0] = solve_back(hbuf[0], inverse[0], arrived)
    for r in range(plan.rows):
        level = table[TABLE_ROWS - 1, r]
        h, s = hbuf[level], sbuf[level]
        for q in range(plan.cols):
            out[q, r] = h
            out[q, plan.rows + r] = s


def per_device(rhs, pattern, factor, inverse, level_size):
    lanes = lax.axis_size("chain")
    cols = lax.axis_size("col")
    rows, _, probes, width = rhs.shape
    entries = pattern.shape[2]
    levels = level_size.shape[0]
    share = probes // cols
    plan = Plan(lanes, cols, rows, entries, share, width, levels)

    smem = pl.BlockSpec(memory_space=pltpu.SMEM)
    hbm = pl.BlockSpec(memory_space=pltpu.HBM)
    vmem = pl.BlockSpec(memory_space=pltpu.VMEM)
    segment_shape = pltpu.VMEM((share, width), BF16)
    front_shape = pltpu.VMEM((lanes, share, width), BF16)
    params = pltpu.CompilerParams(vmem_limit_bytes=12 * 1024 * 1024)

    def far_off(x):
        return pltpu.with_memory_space_constraint(x, pltpu.HBM)

    def held(x):
        return pltpu.with_memory_space_constraint(x, pltpu.VMEM)

    def scalars(x):
        return pltpu.with_memory_space_constraint(x, pltpu.SMEM)

    def store(level):
        return pltpu.VMEM((level * lanes + 1, share, width), BF16)

    def exchange(x):
        return held(lax.all_to_all(x, "chain", 0, 0, tiled=True))

    def around(x):
        return [held(x)] + [
            held(lax.ppermute(x, "col", [(i, (i + s) % cols) for i in range(cols)]))
            for s in range(1, cols)
        ]

    factor = far_off(factor.reshape(rows * plan.entries * width, width))
    first, own, rights, inverses, sizes = pl.pallas_call(
        functools.partial(forward_first, plan),
        out_shape=(
            front_shape,
            pltpu.VMEM((len(plan.near) * plan.deep + CODE_ROWS, width), BF16),
            pltpu.VMEM((levels, share, width), BF16),
            pltpu.VMEM((levels, width, width), BF16),
            pltpu.SMEM((levels,), jnp.int32),
        ),
        in_specs=[hbm] * 5,
        out_specs=(vmem,) * 4 + (smem,),
        scratch_shapes=[
            pltpu.VMEM((rows, 1, entries), jnp.int32),
            pltpu.VMEM((CODE_ROWS, width), F32),
            pltpu.VMEM((CODE_ROWS, width), BF16),
            pltpu.SemaphoreType.DMA((3 + 2 * levels + len(plan.near),)),
        ],
        compiler_params=params,
        name="forward_first",
    )(
        far_off(level_size),
        far_off(pattern),
        factor,
        far_off(rhs.reshape(rows, cols, share, width)),
        far_off(inverse.reshape(rows, width, width)),
    )
    rights, inverses, sizes = held(rights), held(inverses), scalars(sizes)
    near = around(own)
    fronts = [exchange(first)]

    mine, table, own = pl.pallas_call(
        functools.partial(forward_second, plan),
        out_shape=(
            front_shape,
            pltpu.SMEM((TABLE_ROWS, width), jnp.int32),
            pltpu.VMEM((len(plan.far) * plan.deep, width), BF16),
        ),
        in_specs=[smem, hbm] + [vmem] * (3 + cols),
        out_specs=(vmem, smem, vmem),
        scratch_shapes=[
            pltpu.VMEM((TABLE_ROWS, width), jnp.int32),
            store(1),
            pltpu.SemaphoreType.DMA((1 + len(plan.far),)),
        ],
        compiler_params=params,
        name="forward_second",
    )(sizes, factor, rights, inverses, fronts[0], *near)
    table = scalars(table)
    far = around(own)
    fronts.append(exchange(mine))

    def sources(level):
        return near if level in plan.near else far

    for k in range(2, levels - 1):
        mine = pl.pallas_call(
            functools.partial(forward_level, plan, k),
            out_shape=front_shape,
            in_specs=[smem] + [vmem] * (2 + cols + k),
            out_specs=vmem,
            scratch_shapes=[store(k)],
            compiler_params=params,
            name=f"forward_level_{k}",
        )(table, rights, inverses, *sources(k), *fronts)
        fronts.append(exchange(mine))

    last = levels - 1
    acc_shape = pltpu.VMEM((last * lanes + 1, share, width), F32)
    half_last, solved, acc, terms = pl.pallas_call(
        functools.partial(turn_level, plan, last),
        out_shape=(segment_shape, segment_shape, acc_shape, front_shape),
        in_specs=[smem] + [vmem] * (2 + cols + last),
        out_specs=(vmem,) * 4,
        scratch_shapes=[store(last)],
        compiler_params=params,
        name="turn_level",
    )(table, rights, inverses, *sources(last), *fronts)
    done = [held(solved)]
    for k in range(last - 1, 0, -1):
        solved, acc, terms = pl.pallas_call(
            functools.partial(backward_level, plan, k),
            out_shape=(segment_shape, acc_shape, front_shape),
            in_specs=[smem] + [vmem] * (4 + cols),
            out_specs=(vmem,) * 3,
            input_output_aliases={4: 1},
            compiler_params=params,
            name=f"backward_level_{k}",
        )(
            table,
            inverses,
            fronts[k],
            exchange(terms),
            held(acc),
            *sources(k),
        )
        done.insert(0, held(solved))
    shares = pl.pallas_call(
        functools.partial(finish, plan),
        out_shape=pltpu.VMEM((cols, 2 * rows, share, width), BF16),
        in_specs=[smem] + [vmem] * (1 + 2 * levels),
        out_specs=vmem,
        scratch_shapes=[
            pltpu.VMEM((levels, share, width), BF16),
            pltpu.VMEM((levels, share, width), BF16),
        ],
        compiler_params=params,
        name="finish",
    )(table, inverses, exchange(terms), *fronts, held(half_last), *done)
    whole = lax.all_to_all(shares, "col", 0, 0, tiled=True)
    whole = whole.transpose(1, 0, 2, 3).reshape(2, rows, 1, probes, width)
    return whole[0], whole[1]


def solution(mesh):
    return jax.shard_map(
        per_device,
        mesh=mesh,
        in_specs=(
            P(None, "chain", None, None),
            P(None, "chain", "col"),
            P(None, "chain", "col", None, None),
            P(None, "chain", None, None),
            P(),
        ),
        out_specs=(P(None, "chain", None, None), P(None, "chain", None, None)),
        check_vma=False,
    )
```

```python
import functools
import jax
import jax.numpy as jnp
from jax import lax
from jax.experimental import pallas as pl
from jax.experimental.pallas import tpu as pltpu
from jax.sharding import PartitionSpec as P

BF16 = jnp.bfloat16
F32 = jnp.float32
NT = (((1,), (1,)), ((), ()))
NN = (((1,), (0,)), ((), ()))
CODE_ROWS = 16
TABLE_ROWS = 8


class Plan:
    def __init__(self, lanes, cols, rows, entries, share, width, levels):
        self.lanes, self.cols, self.rows, self.entries = lanes, cols, rows, entries
        self.share, self.width, self.levels = share, width, levels
        self.deep = entries * width
        self.near = range(1, min(3, levels))
        self.far = range(min(3, levels), levels)

    def slots(self, level):
        return max(0, self.rows - (self.levels - level)), min(level, self.rows - 1)


def locate(plan, level, sizes):
    lane = lax.axis_index("chain")
    start = jnp.int32(0)
    for k in range(level):
        start = start + sizes[k]
    slot = (start - lane + (plan.lanes - 1)) // plan.lanes
    live = (slot < plan.rows) & (slot * plan.lanes + lane < start + sizes[level])
    low, high = plan.slots(level)
    return jnp.clip(slot, low, high), live


def factor_row(plan, factor, level, sizes):
    slot, _ = locate(plan, level, sizes)
    return factor.at[pl.ds(pl.multiple_of(slot * plan.deep, plan.deep), plan.deep)]


def weights_of(plan, level, sources):
    base = (level - (plan.near if level in plan.near else plan.far)[0]) * plan.deep
    return jnp.concatenate(
        [
            source[base + e * plan.width : base + (e + 1) * plan.width, :]
            for source in sources
            for e in range(plan.entries)
        ],
        axis=1,
    )


def places_of(plan, level, table):
    return [
        table[level, s * plan.entries + e]
        for s in range(plan.cols)
        for e in range(plan.entries)
    ]


def gather_store(plan, level, earlier, store):
    for k in range(level):
        store[pl.ds(k * plan.lanes, plan.lanes)] = earlier[k][...]
    store[level * plan.lanes] = jnp.zeros(store.shape[1:], BF16)


def half_segment(plan, level, table, right, inverse, sources, store):
    chosen = jnp.concatenate([store[at] for at in places_of(plan, level, table)], axis=1)
    weights = weights_of(plan, level, sources)
    summed = lax.dot_general(chosen, weights, NT, preferred_element_type=F32)
    rest = (right[level].astype(F32) - summed).astype(BF16)
    return lax.dot_general(
        rest, inverse[level], NT, preferred_element_type=F32
    ).astype(BF16)


def add_terms(plan, level, table, segment, sources, acc):
    weights = weights_of(plan, level, sources)
    terms = lax.dot_general(segment, weights, NN, preferred_element_type=F32)
    for j, at in enumerate(places_of(plan, level, table)):
        acc[at] = acc[at] + terms[:, j * plan.width : (j + 1) * plan.width]


def forward_first(plan, *refs):
    level_size, pattern, factor, right, inverse = refs[:5]
    out, near, rights, inverses, sizes, pats, wide, code, sems = refs[5:]
    col = lax.axis_index("col")
    pick = pltpu.make_async_copy(pattern, pats, sems.at[0])
    learn = pltpu.make_async_copy(
        level_size, sizes, sems.at[2 + 2 * plan.levels + len(plan.near)]
    )
    learn.start()
    pick.start()

    def pair(level, slot):
        at = 1 + 2 * level
        return [
            pltpu.make_async_copy(inverse.at[slot], inverses.at[level], sems.at[at]),
            pltpu.make_async_copy(
                right.at[slot, col], rights.at[level], sems.at[at + 1]
            ),
        ]

    small = pair(0, 0)
    for c in small:
        c.start()
    wide[...] = jnp.zeros(wide.shape, F32)
    learn.wait()
    slots = [locate(plan, k, sizes)[0] for k in range(plan.levels)]
    large = [
        pltpu.make_async_copy(
            factor_row(plan, factor, k, sizes),
            near.at[pl.ds(i * plan.deep, plan.deep)],
            sems.at[1 + 2 * plan.levels + i],
        )
        for i, k in enumerate(plan.near)
    ]
    for c in large:
        c.start()
    for k in range(1, plan.levels):
        more = pair(k, slots[k])
        for c in more:
            c.start()
        small += more
    pick.wait()
    for k in range(1, plan.levels):
        wide[pl.ds(k, 1), pl.ds(0, plan.entries)] = pats[slots[k]].astype(F32)
    code[...] = wide[...].astype(BF16)
    last = pltpu.make_async_copy(
        code,
        near.at[pl.ds(len(plan.near) * plan.deep, CODE_ROWS)],
        sems.at[1 + 2 * plan.levels + len(plan.near)],
    )
    last.start()
    small[0].wait()
    small[1].wait()
    segment = lax.dot_general(
        rights[0], inverses[0], NT, preferred_element_type=F32
    ).astype(BF16)
    out[...] = jnp.broadcast_to(segment[None], out.shape)
    for c in small[2:] + large:
        c.wait()
    last.wait()


def fill_table(plan, sizes, near, table):
    split = len(plan.near) * plan.deep
    shape = (TABLE_ROWS, plan.width)
    row_level = lax.broadcasted_iota(jnp.int32, shape, 0)
    entry = lax.broadcasted_iota(jnp.int32, shape, 1)
    alive = jnp.zeros(shape, jnp.int32)
    ends = []
    for k in range(plan.levels):
        ends.append((ends[-1] if ends else 0) + sizes[k])
        live = locate(plan, k, sizes)[1].astype(jnp.int32)
        alive = alive + jnp.where(row_level == k, live, 0)
    total = jnp.zeros(shape, jnp.int32)
    for s in range(plan.cols):
        columns = near[s][split : split + CODE_ROWS, :].astype(F32)[:TABLE_ROWS]
        columns = columns.astype(jnp.int32)
        level = jnp.zeros(shape, jnp.int32)
        for end in ends:
            level = level + (columns >= end).astype(jnp.int32)
        place = jnp.where(
            (level < row_level) & (alive > 0),
            level * plan.lanes + lax.rem(columns, plan.lanes),
            row_level * plan.lanes,
        )
        place = jnp.where(entry < plan.entries, place, 0)
        total = total + (pltpu.roll(place, s * plan.entries, 1) if s else place)
    own = entry * plan.lanes + lax.axis_index("chain")
    own_level = jnp.zeros(shape, jnp.int32)
    for end in ends:
        own_level = own_level + (own >= end).astype(jnp.int32)
    table[...] = jnp.where(row_level == TABLE_ROWS - 1, own_level, total)


def forward_second(plan, *refs):
    sizes, factor, right, inverse, front = refs[:5]
    near = refs[5 : 5 + plan.cols]
    out, table, far, draft, store, sems = refs[5 + plan.cols :]
    copies = [
        pltpu.make_async_copy(
            factor_row(plan, factor, k, sizes),
            far.at[pl.ds(i * plan.deep, plan.deep)],
            sems.at[1 + i],
        )
        for i, k in enumerate(plan.far)
    ]
    for c in copies:
        c.start()
    fill_table(plan, sizes, near, draft)
    copy = pltpu.make_async_copy(draft, table, sems.at[0])
    copy.start()
    gather_store(plan, 1, [front], store)
    copy.wait()
    segment = half_segment(plan, 1, table, right, inverse, near, store)
    out[...] = jnp.broadcast_to(segment[None], out.shape)
    for c in copies:
        c.wait()


def forward_level(plan, level, *refs):
    table, right, inverse = refs[:3]
    sources = refs[3 : 3 + plan.cols]
    earlier = refs[3 + plan.cols : 3 + plan.cols + level]
    out, store = refs[3 + plan.cols + level :]
    gather_store(plan, level, earlier, store)
    segment = half_segment(plan, level, table, right, inverse, sources, store)
    out[...] = jnp.broadcast_to(segment[None], out.shape)


def turn_level(plan, level, *refs):
    table, right, inverse = refs[:3]
    sources = refs[3 : 3 + plan.cols]
    earlier = refs[3 + plan.cols : 3 + plan.cols + level]
    half, solved, acc, out, store = refs[3 + plan.cols + level :]
    gather_store(plan, level, earlier, store)
    acc[...] = jnp.zeros(acc.shape, F32)
    segment = half_segment(plan, level, table, right, inverse, sources, store)
    half[...] = segment
    segment = lax.dot_general(
        segment, inverse[level], NN, preferred_element_type=F32
    ).astype(BF16)
    solved[...] = segment
    add_terms(plan, level, table, segment, sources, acc)
    out[...] = acc[pl.ds((level - 1) * plan.lanes, plan.lanes)].astype(BF16)


def solve_back(half, inverse, arrived):
    summed = jnp.sum(arrived[...].astype(F32), axis=0)
    rest = (half.astype(F32) - summed).astype(BF16)
    return lax.dot_general(rest, inverse, NN, preferred_element_type=F32).astype(BF16)


def backward_level(plan, level, *refs):
    table, inverse, front, arrived, _ = refs[:5]
    sources = refs[5 : 5 + plan.cols]
    solved, acc, out = refs[5 + plan.cols :]
    segment = solve_back(front[lax.axis_index("chain")], inverse[level], arrived)
    solved[...] = segment
    add_terms(plan, level, table, segment, sources, acc)
    out[...] = acc[pl.ds((level - 1) * plan.lanes, plan.lanes)].astype(BF16)


def finish(plan, *refs):
    levels = plan.levels
    table, inverse, arrived = refs[:3]
    fronts = refs[3 : 2 + levels]
    half_last = refs[2 + levels]
    done = refs[3 + levels : 2 + 2 * levels]
    out, hbuf, sbuf = refs[2 + 2 * levels :]
    lane = lax.axis_index("chain")
    for k in range(levels - 1):
        hbuf[k] = fronts[k][lane]
        sbuf[k + 1] = done[k][...]
    hbuf[levels - 1] = half_last[...]
    sbuf[0] = solve_back(hbuf[0], inverse[0], arrived)
    for r in range(plan.rows):
        level = table[TABLE_ROWS - 1, r]
        h, s = hbuf[level], sbuf[level]
        for q in range(plan.cols):
            out[q, r] = h
            out[q, plan.rows + r] = s


def per_device(rhs, pattern, factor, inverse, level_size):
    lanes = lax.axis_size("chain")
    cols = lax.axis_size("col")
    rows, _, probes, width = rhs.shape
    entries = pattern.shape[2]
    levels = level_size.shape[0]
    share = probes // cols
    plan = Plan(lanes, cols, rows, entries, share, width, levels)

    smem = pl.BlockSpec(memory_space=pltpu.SMEM)
    hbm = pl.BlockSpec(memory_space=pltpu.HBM)
    vmem = pl.BlockSpec(memory_space=pltpu.VMEM)
    segment_shape = pltpu.VMEM((share, width), BF16)
    front_shape = pltpu.VMEM((lanes, share, width), BF16)
    params = pltpu.CompilerParams(vmem_limit_bytes=12 * 1024 * 1024)

    def far_off(x):
        return pltpu.with_memory_space_constraint(x, pltpu.HBM)

    def held(x):
        return pltpu.with_memory_space_constraint(x, pltpu.VMEM)

    def scalars(x):
        return pltpu.with_memory_space_constraint(x, pltpu.SMEM)

    def store(level):
        return pltpu.VMEM((level * lanes + 1, share, width), BF16)

    def exchange(x):
        return held(lax.all_to_all(x, "chain", 0, 0, tiled=True))

    def around(x):
        return [held(x)] + [
            held(lax.ppermute(x, "col", [(i, i ^ s) for i in range(cols)]))
            for s in (1, 3, 2)
        ]

    factor = far_off(factor.reshape(rows * plan.entries * width, width))
    first, own, rights, inverses, sizes = pl.pallas_call(
        functools.partial(forward_first, plan),
        out_shape=(
            front_shape,
            pltpu.VMEM((len(plan.near) * plan.deep + CODE_ROWS, width), BF16),
            pltpu.VMEM((levels, share, width), BF16),
            pltpu.VMEM((levels, width, width), BF16),
            pltpu.SMEM((levels,), jnp.int32),
        ),
        in_specs=[hbm] * 5,
        out_specs=(vmem,) * 4 + (smem,),
        scratch_shapes=[
            pltpu.VMEM((rows, 1, entries), jnp.int32),
            pltpu.VMEM((CODE_ROWS, width), F32),
            pltpu.VMEM((CODE_ROWS, width), BF16),
            pltpu.SemaphoreType.DMA((3 + 2 * levels + len(plan.near),)),
        ],
        compiler_params=params,
        name="forward_first",
    )(
        far_off(level_size),
        far_off(pattern),
        factor,
        far_off(rhs.reshape(rows, cols, share, width)),
        far_off(inverse.reshape(rows, width, width)),
    )
    rights, inverses, sizes = held(rights), held(inverses), scalars(sizes)
    near = around(own)
    fronts = [exchange(first)]

    mine, table, own = pl.pallas_call(
        functools.partial(forward_second, plan),
        out_shape=(
            front_shape,
            pltpu.SMEM((TABLE_ROWS, width), jnp.int32),
            pltpu.VMEM((len(plan.far) * plan.deep, width), BF16),
        ),
        in_specs=[smem, hbm] + [vmem] * (3 + cols),
        out_specs=(vmem, smem, vmem),
        scratch_shapes=[
            pltpu.VMEM((TABLE_ROWS, width), jnp.int32),
            store(1),
            pltpu.SemaphoreType.DMA((1 + len(plan.far),)),
        ],
        compiler_params=params,
        name="forward_second",
    )(sizes, factor, rights, inverses, fronts[0], *near)
    table = scalars(table)
    far = around(own)
    fronts.append(exchange(mine))

    def sources(level):
        return near if level in plan.near else far

    for k in range(2, levels - 1):
        mine = pl.pallas_call(
            functools.partial(forward_level, plan, k),
            out_shape=front_shape,
            in_specs=[smem] + [vmem] * (2 + cols + k),
            out_specs=vmem,
            scratch_shapes=[store(k)],
            compiler_params=params,
            name=f"forward_level_{k}",
        )(table, rights, inverses, *sources(k), *fronts)
        fronts.append(exchange(mine))

    last = levels - 1
    acc_shape = pltpu.VMEM((last * lanes + 1, share, width), F32)
    half_last, solved, acc, terms = pl.pallas_call(
        functools.partial(turn_level, plan, last),
        out_shape=(segment_shape, segment_shape, acc_shape, front_shape),
        in_specs=[smem] + [vmem] * (2 + cols + last),
        out_specs=(vmem,) * 4,
        scratch_shapes=[store(last)],
        compiler_params=params,
        name="turn_level",
    )(table, rights, inverses, *sources(last), *fronts)
    done = [held(solved)]
    for k in range(last - 1, 0, -1):
        solved, acc, terms = pl.pallas_call(
            functools.partial(backward_level, plan, k),
            out_shape=(segment_shape, acc_shape, front_shape),
            in_specs=[smem] + [vmem] * (4 + cols),
            out_specs=(vmem,) * 3,
            input_output_aliases={4: 1},
            compiler_params=params,
            name=f"backward_level_{k}",
        )(
            table,
            inverses,
            fronts[k],
            exchange(terms),
            held(acc),
            *sources(k),
        )
        done.insert(0, held(solved))
    shares = pl.pallas_call(
        functools.partial(finish, plan),
        out_shape=pltpu.VMEM((cols, 2 * rows, share, width), BF16),
        in_specs=[smem] + [vmem] * (1 + 2 * levels),
        out_specs=vmem,
        scratch_shapes=[
            pltpu.VMEM((levels, share, width), BF16),
            pltpu.VMEM((levels, share, width), BF16),
        ],
        compiler_params=params,
        name="finish",
    )(table, inverses, exchange(terms), *fronts, held(half_last), *done)
    whole = lax.all_to_all(shares, "col", 0, 0, tiled=True)
    whole = whole.transpose(1, 0, 2, 3).reshape(2, rows, 1, probes, width)
    return whole[0], whole[1]


def solution(mesh):
    return jax.shard_map(
        per_device,
        mesh=mesh,
        in_specs=(
            P(None, "chain", None, None),
            P(None, "chain", "col"),
            P(None, "chain", "col", None, None),
            P(None, "chain", None, None),
            P(),
        ),
        out_specs=(P(None, "chain", None, None), P(None, "chain", None, None)),
        check_vma=False,
    )
```

```python
import functools
import jax
import jax.numpy as jnp
from jax import lax
from jax.experimental import pallas as pl
from jax.experimental.pallas import tpu as pltpu
from jax.sharding import PartitionSpec as P

BF16 = jnp.bfloat16
F32 = jnp.float32
NT = (((1,), (1,)), ((), ()))
NN = (((1,), (0,)), ((), ()))
CODE_ROWS = 16
TABLE_ROWS = 8


class Plan:
    def __init__(self, lanes, cols, rows, entries, share, width, levels):
        self.lanes, self.cols, self.rows, self.entries = lanes, cols, rows, entries
        self.share, self.width, self.levels = share, width, levels
        self.deep = entries * width
        self.near = range(1, min(3, levels))
        self.far = range(min(3, levels), levels)

    def slots(self, level):
        return max(0, self.rows - (self.levels - level)), min(level, self.rows - 1)


def locate(plan, level, sizes):
    lane = lax.axis_index("chain")
    start = jnp.int32(0)
    for k in range(level):
        start = start + sizes[k]
    slot = (start - lane + (plan.lanes - 1)) // plan.lanes
    live = (slot < plan.rows) & (slot * plan.lanes + lane < start + sizes[level])
    low, high = plan.slots(level)
    return jnp.clip(slot, low, high), live


def weights_of(plan, level, sources):
    base = (level - (plan.near if level in plan.near else plan.far)[0]) * plan.deep
    return jnp.concatenate(
        [
            source[base + e * plan.width : base + (e + 1) * plan.width, :]
            for source in sources
            for e in range(plan.entries)
        ],
        axis=1,
    )


def places_of(plan, level, table):
    return [
        table[level, s * plan.entries + e]
        for s in range(plan.cols)
        for e in range(plan.entries)
    ]


def gather_store(plan, level, earlier, store):
    for k in range(level):
        store[pl.ds(k * plan.lanes, plan.lanes)] = earlier[k][...]
    store[level * plan.lanes] = jnp.zeros(store.shape[1:], BF16)


def half_segment(plan, level, table, right, inverse, sources, store):
    chosen = jnp.concatenate([store[at] for at in places_of(plan, level, table)], axis=1)
    weights = weights_of(plan, level, sources)
    summed = lax.dot_general(chosen, weights, NT, preferred_element_type=F32)
    rest = (right[level].astype(F32) - summed).astype(BF16)
    return lax.dot_general(
        rest, inverse[level], NT, preferred_element_type=F32
    ).astype(BF16)


def add_terms(plan, level, table, segment, sources, acc):
    weights = weights_of(plan, level, sources)
    terms = lax.dot_general(segment, weights, NN, preferred_element_type=F32)
    for j, at in enumerate(places_of(plan, level, table)):
        acc[at] = acc[at] + terms[:, j * plan.width : (j + 1) * plan.width]


def forward_first(plan, *refs):
    level_size, pattern, factor, right, inverse = refs[:5]
    out, near, far, rights, inverses, sizes = refs[5:11]
    pats, blocks, sides, diagonal, wide, sems = refs[11:]
    col = lax.axis_index("col")
    loads = [
        (level_size, sizes),
        (inverse, diagonal),
        (right.at[:, col], sides),
        (factor, blocks),
        (pattern, pats),
    ]
    copies = [
        pltpu.make_async_copy(source, target, sems.at[i])
        for i, (source, target) in enumerate(loads)
    ]
    for c in copies:
        c.start()
    wide[...] = jnp.zeros(wide.shape, F32)
    copies[0].wait()
    slots = [locate(plan, k, sizes)[0] for k in range(plan.levels)]
    copies[1].wait()
    copies[2].wait()
    segment = lax.dot_general(
        sides[0], diagonal[0], NT, preferred_element_type=F32
    ).astype(BF16)
    out[...] = jnp.broadcast_to(segment[None], out.shape)
    for k in range(plan.levels):
        rights[k] = sides[slots[k]]
        inverses[k] = diagonal[slots[k]]
    copies[3].wait()
    copies[4].wait()
    for target, levels in ((near, plan.near), (far, plan.far)):
        for i, k in enumerate(levels):
            at = pl.multiple_of(slots[k] * plan.deep, plan.deep)
            target[pl.ds(i * plan.deep, plan.deep), :] = blocks[
                pl.ds(at, plan.deep), :
            ]
    for k in range(1, plan.levels):
        wide[pl.ds(k, 1), pl.ds(0, plan.entries)] = pats[slots[k]].astype(F32)
    near[pl.ds(len(plan.near) * plan.deep, CODE_ROWS), :] = wide[...].astype(BF16)


def fill_table(plan, sizes, near, table):
    split = len(plan.near) * plan.deep
    shape = (TABLE_ROWS, plan.width)
    row_level = lax.broadcasted_iota(jnp.int32, shape, 0)
    entry = lax.broadcasted_iota(jnp.int32, shape, 1)
    alive = jnp.zeros(shape, jnp.int32)
    ends = []
    for k in range(plan.levels):
        ends.append((ends[-1] if ends else 0) + sizes[k])
        live = locate(plan, k, sizes)[1].astype(jnp.int32)
        alive = alive + jnp.where(row_level == k, live, 0)
    total = jnp.zeros(shape, jnp.int32)
    for s in range(plan.cols):
        columns = near[s][split : split + CODE_ROWS, :].astype(F32)[:TABLE_ROWS]
        columns = columns.astype(jnp.int32)
        level = jnp.zeros(shape, jnp.int32)
        for end in ends:
            level = level + (columns >= end).astype(jnp.int32)
        place = jnp.where(
            (level < row_level) & (alive > 0),
            level * plan.lanes + lax.rem(columns, plan.lanes),
            row_level * plan.lanes,
        )
        place = jnp.where(entry < plan.entries, place, 0)
        total = total + (pltpu.roll(place, s * plan.entries, 1) if s else place)
    own = entry * plan.lanes + lax.axis_index("chain")
    own_level = jnp.zeros(shape, jnp.int32)
    for end in ends:
        own_level = own_level + (own >= end).astype(jnp.int32)
    table[...] = jnp.where(row_level == TABLE_ROWS - 1, own_level, total)


def after(far, segment, same):
    pass


def forward_second(plan, *refs):
    sizes, right, inverse, front = refs[:4]
    near = refs[4 : 4 + plan.cols]
    out, table, draft, store, sem = refs[4 + plan.cols :]
    fill_table(plan, sizes, near, draft)
    copy = pltpu.make_async_copy(draft, table, sem)
    copy.start()
    gather_store(plan, 1, [front], store)
    copy.wait()
    segment = half_segment(plan, 1, table, right, inverse, near, store)
    out[...] = jnp.broadcast_to(segment[None], out.shape)


def forward_level(plan, level, *refs):
    table, right, inverse = refs[:3]
    sources = refs[3 : 3 + plan.cols]
    earlier = refs[3 + plan.cols : 3 + plan.cols + level]
    out, store = refs[3 + plan.cols + level :]
    gather_store(plan, level, earlier, store)
    segment = half_segment(plan, level, table, right, inverse, sources, store)
    out[...] = jnp.broadcast_to(segment[None], out.shape)


def turn_level(plan, level, *refs):
    table, right, inverse = refs[:3]
    sources = refs[3 : 3 + plan.cols]
    earlier = refs[3 + plan.cols : 3 + plan.cols + level]
    half, solved, acc, out, store = refs[3 + plan.cols + level :]
    gather_store(plan, level, earlier, store)
    acc[...] = jnp.zeros(acc.shape, F32)
    segment = half_segment(plan, level, table, right, inverse, sources, store)
    half[...] = segment
    segment = lax.dot_general(
        segment, inverse[level], NN, preferred_element_type=F32
    ).astype(BF16)
    solved[...] = segment
    add_terms(plan, level, table, segment, sources, acc)
    out[...] = acc[pl.ds((level - 1) * plan.lanes, plan.lanes)].astype(BF16)


def solve_back(half, inverse, arrived):
    summed = jnp.sum(arrived[...].astype(F32), axis=0)
    rest = (half.astype(F32) - summed).astype(BF16)
    return lax.dot_general(rest, inverse, NN, preferred_element_type=F32).astype(BF16)


def backward_level(plan, level, *refs):
    table, inverse, front, arrived, _ = refs[:5]
    sources = refs[5 : 5 + plan.cols]
    solved, acc, out = refs[5 + plan.cols :]
    segment = solve_back(front[lax.axis_index("chain")], inverse[level], arrived)
    solved[...] = segment
    add_terms(plan, level, table, segment, sources, acc)
    out[...] = acc[pl.ds((level - 1) * plan.lanes, plan.lanes)].astype(BF16)


def finish(plan, *refs):
    levels = plan.levels
    table, inverse, arrived = refs[:3]
    fronts = refs[3 : 2 + levels]
    half_last = refs[2 + levels]
    done = refs[3 + levels : 2 + 2 * levels]
    out, hbuf, sbuf = refs[2 + 2 * levels :]
    lane = lax.axis_index("chain")
    for k in range(levels - 1):
        hbuf[k] = fronts[k][lane]
        sbuf[k + 1] = done[k][...]
    hbuf[levels - 1] = half_last[...]
    sbuf[0] = solve_back(hbuf[0], inverse[0], arrived)
    for r in range(plan.rows):
        level = table[TABLE_ROWS - 1, r]
        h, s = hbuf[level], sbuf[level]
        for q in range(plan.cols):
            out[q, r] = h
            out[q, plan.rows + r] = s


def per_device(rhs, pattern, factor, inverse, level_size):
    lanes = lax.axis_size("chain")
    cols = lax.axis_size("col")
    rows, _, probes, width = rhs.shape
    entries = pattern.shape[2]
    levels = level_size.shape[0]
    share = probes // cols
    plan = Plan(lanes, cols, rows, entries, share, width, levels)

    smem = pl.BlockSpec(memory_space=pltpu.SMEM)
    hbm = pl.BlockSpec(memory_space=pltpu.HBM)
    vmem = pl.BlockSpec(memory_space=pltpu.VMEM)
    segment_shape = pltpu.VMEM((share, width), BF16)
    front_shape = pltpu.VMEM((lanes, share, width), BF16)
    params = pltpu.CompilerParams(vmem_limit_bytes=12 * 1024 * 1024)

    def far_off(x):
        return pltpu.with_memory_space_constraint(x, pltpu.HBM)

    def held(x):
        return pltpu.with_memory_space_constraint(x, pltpu.VMEM)

    def scalars(x):
        return pltpu.with_memory_space_constraint(x, pltpu.SMEM)

    def store(level):
        return pltpu.VMEM((level * lanes + 1, share, width), BF16)

    def exchange(x):
        return held(lax.all_to_all(x, "chain", 0, 0, tiled=True))

    def around(x):
        return [held(x)] + [
            held(lax.ppermute(x, "col", [(i, i ^ s) for i in range(cols)]))
            for s in (1, 3, 2)
        ]

    factor = far_off(factor.reshape(rows * plan.entries * width, width))
    far_shape = pltpu.VMEM((len(plan.far) * plan.deep, width), BF16)
    first, own, later, rights, inverses, sizes = pl.pallas_call(
        functools.partial(forward_first, plan),
        out_shape=(
            front_shape,
            pltpu.VMEM((len(plan.near) * plan.deep + CODE_ROWS, width), BF16),
            far_shape,
            pltpu.VMEM((levels, share, width), BF16),
            pltpu.VMEM((levels, width, width), BF16),
            pltpu.SMEM((levels,), jnp.int32),
        ),
        in_specs=[hbm] * 5,
        out_specs=(vmem,) * 5 + (smem,),
        scratch_shapes=[
            pltpu.VMEM((rows, 1, entries), jnp.int32),
            pltpu.VMEM((rows * plan.deep, width), BF16),
            pltpu.VMEM((rows, share, width), BF16),
            pltpu.VMEM((rows, width, width), BF16),
            pltpu.VMEM((CODE_ROWS, width), F32),
            pltpu.SemaphoreType.DMA((5,)),
        ],
        compiler_params=params,
        name="forward_first",
    )(
        far_off(level_size),
        far_off(pattern),
        factor,
        far_off(rhs.reshape(rows, cols, share, width)),
        far_off(inverse.reshape(rows, width, width)),
    )
    rights, inverses, sizes = held(rights), held(inverses), scalars(sizes)
    near = around(own)
    fronts = [exchange(first)]
    mine, table = pl.pallas_call(
        functools.partial(forward_second, plan),
        out_shape=(
            front_shape,
            pltpu.SMEM((TABLE_ROWS, width), jnp.int32),
        ),
        in_specs=[smem] + [vmem] * (3 + cols),
        out_specs=(vmem, smem),
        scratch_shapes=[
            pltpu.VMEM((TABLE_ROWS, width), jnp.int32),
            store(1),
            pltpu.SemaphoreType.DMA,
        ],
        compiler_params=params,
        name="forward_second",
    )(sizes, rights, inverses, fronts[0], *near)
    table = scalars(table)
    later = pl.pallas_call(
        after,
        out_shape=far_shape,
        in_specs=[vmem, vmem],
        out_specs=vmem,
        input_output_aliases={0: 0},
        compiler_params=params,
        name="after",
    )(held(later), held(mine))
    far = around(later)
    fronts.append(exchange(mine))

    def sources(level):
        return near if level in plan.near else far

    for k in range(2, levels - 1):
        mine = pl.pallas_call(
            functools.partial(forward_level, plan, k),
            out_shape=front_shape,
            in_specs=[smem] + [vmem] * (2 + cols + k),
            out_specs=vmem,
            scratch_shapes=[store(k)],
            compiler_params=params,
            name=f"forward_level_{k}",
        )(table, rights, inverses, *sources(k), *fronts)
        fronts.append(exchange(mine))

    last = levels - 1
    acc_shape = pltpu.VMEM((last * lanes + 1, share, width), F32)
    half_last, solved, acc, terms = pl.pallas_call(
        functools.partial(turn_level, plan, last),
        out_shape=(segment_shape, segment_shape, acc_shape, front_shape),
        in_specs=[smem] + [vmem] * (2 + cols + last),
        out_specs=(vmem,) * 4,
        scratch_shapes=[store(last)],
        compiler_params=params,
        name="turn_level",
    )(table, rights, inverses, *sources(last), *fronts)
    done = [held(solved)]
    for k in range(last - 1, 0, -1):
        solved, acc, terms = pl.pallas_call(
            functools.partial(backward_level, plan, k),
            out_shape=(segment_shape, acc_shape, front_shape),
            in_specs=[smem] + [vmem] * (4 + cols),
            out_specs=(vmem,) * 3,
            input_output_aliases={4: 1},
            compiler_params=params,
            name=f"backward_level_{k}",
        )(
            table,
            inverses,
            fronts[k],
            exchange(terms),
            held(acc),
            *sources(k),
        )
        done.insert(0, held(solved))
    shares = pl.pallas_call(
        functools.partial(finish, plan),
        out_shape=pltpu.VMEM((cols, 2 * rows, share, width), BF16),
        in_specs=[smem] + [vmem] * (1 + 2 * levels),
        out_specs=vmem,
        scratch_shapes=[
            pltpu.VMEM((levels, share, width), BF16),
            pltpu.VMEM((levels, share, width), BF16),
        ],
        compiler_params=params,
        name="finish",
    )(table, inverses, exchange(terms), *fronts, held(half_last), *done)
    whole = lax.all_to_all(shares, "col", 0, 0, tiled=True)
    whole = whole.transpose(1, 0, 2, 3).reshape(2, rows, 1, probes, width)
    return whole[0], whole[1]


def solution(mesh):
    return jax.shard_map(
        per_device,
        mesh=mesh,
        in_specs=(
            P(None, "chain", None, None),
            P(None, "chain", "col"),
            P(None, "chain", "col", None, None),
            P(None, "chain", None, None),
            P(),
        ),
        out_specs=(P(None, "chain", None, None), P(None, "chain", None, None)),
        check_vma=False,
    )
```

```python
import functools
import jax
import jax.numpy as jnp
from jax import lax
from jax.experimental import pallas as pl
from jax.experimental.pallas import tpu as pltpu
from jax.sharding import PartitionSpec as P

BF16 = jnp.bfloat16
F32 = jnp.float32
NT = (((1,), (1,)), ((), ()))
NN = (((1,), (0,)), ((), ()))
CODE_ROWS = 16
TABLE_ROWS = 8
PAIR = 2


class Plan:
    def __init__(self, lanes, cols, rows, entries, share, width, levels):
        self.lanes, self.cols, self.rows, self.entries = lanes, cols, rows, entries
        self.share, self.width, self.levels = share, width, levels
        self.deep = entries * width
        self.near = range(1, min(3, levels))
        self.far = range(min(3, levels), levels)

    def slots(self, level):
        return max(0, self.rows - (self.levels - level)), min(level, self.rows - 1)


def locate(plan, level, sizes):
    lane = lax.axis_index("chain")
    start = jnp.int32(0)
    for k in range(level):
        start = start + sizes[k]
    slot = (start - lane + (plan.lanes - 1)) // plan.lanes
    live = (slot < plan.rows) & (slot * plan.lanes + lane < start + sizes[level])
    low, high = plan.slots(level)
    return jnp.clip(slot, low, high), live


def weights_of(plan, level, sources):
    base = (level - (plan.near if level in plan.near else plan.far)[0]) * plan.deep
    return jnp.concatenate(
        [
            source[base + e * plan.width : base + (e + 1) * plan.width, :]
            for source in sources
            for e in range(plan.entries)
        ],
        axis=1,
    )


def places_of(plan, level, table):
    return [
        table[level, s * plan.entries + e]
        for s in range(plan.cols)
        for e in range(plan.entries)
    ]


def gather_store(plan, level, earlier, store):
    part = plan.lanes // PAIR
    for k in range(PAIR * level):
        store[pl.ds(k * part, part)] = earlier[k][...]
    store[level * plan.lanes] = jnp.zeros(store.shape[1:], BF16)


def half_segment(plan, level, table, right, inverse, sources, store):
    chosen = jnp.concatenate([store[at] for at in places_of(plan, level, table)], axis=1)
    weights = weights_of(plan, level, sources)
    summed = lax.dot_general(chosen, weights, NT, preferred_element_type=F32)
    rest = (right[level].astype(F32) - summed).astype(BF16)
    return lax.dot_general(
        rest, inverse[level], NT, preferred_element_type=F32
    ).astype(BF16)


def add_terms(plan, level, table, segment, sources, acc):
    weights = weights_of(plan, level, sources)
    terms = lax.dot_general(segment, weights, NN, preferred_element_type=F32)
    for j, at in enumerate(places_of(plan, level, table)):
        acc[at] = acc[at] + terms[:, j * plan.width : (j + 1) * plan.width]


def give_terms(plan, level, acc, out):
    core = lax.rem(lax.axis_index("chain"), PAIR)
    part = plan.lanes // PAIR
    for i in range(PAIR):
        at = level * plan.lanes + i * part
        out[:, core ^ i] = acc[pl.ds(at, part)].astype(BF16)


def forward_first(plan, *refs):
    level_size, pattern, factor, right, inverse = refs[:5]
    out, near, far, rights, inverses, sizes = refs[5:11]
    pats, blocks, sides, diagonal, wide, sems = refs[11:]
    col = lax.axis_index("col")
    loads = [
        (level_size, sizes),
        (inverse, diagonal),
        (right.at[:, col], sides),
        (factor, blocks),
        (pattern, pats),
    ]
    copies = [
        pltpu.make_async_copy(source, target, sems.at[i])
        for i, (source, target) in enumerate(loads)
    ]
    for c in copies:
        c.start()
    wide[...] = jnp.zeros(wide.shape, F32)
    copies[0].wait()
    slots = [locate(plan, k, sizes)[0] for k in range(plan.levels)]
    copies[1].wait()
    copies[2].wait()
    segment = lax.dot_general(
        sides[0], diagonal[0], NT, preferred_element_type=F32
    ).astype(BF16)
    out[...] = jnp.broadcast_to(segment[None], out.shape)
    for k in range(plan.levels):
        rights[k] = sides[slots[k]]
        inverses[k] = diagonal[slots[k]]
    copies[3].wait()
    copies[4].wait()
    for target, levels in ((near, plan.near), (far, plan.far)):
        for i, k in enumerate(levels):
            at = pl.multiple_of(slots[k] * plan.deep, plan.deep)
            target[pl.ds(i * plan.deep, plan.deep), :] = blocks[
                pl.ds(at, plan.deep), :
            ]
    for k in range(1, plan.levels):
        wide[pl.ds(k, 1), pl.ds(0, plan.entries)] = pats[slots[k]].astype(F32)
    near[pl.ds(len(plan.near) * plan.deep, CODE_ROWS), :] = wide[...].astype(BF16)


def fill_table(plan, sizes, near, table):
    core = lax.rem(lax.axis_index("chain"), PAIR)
    split = len(plan.near) * plan.deep
    shape = (TABLE_ROWS, plan.width)
    row_level = lax.broadcasted_iota(jnp.int32, shape, 0)
    entry = lax.broadcasted_iota(jnp.int32, shape, 1)
    alive = jnp.zeros(shape, jnp.int32)
    ends = []
    for k in range(plan.levels):
        ends.append((ends[-1] if ends else 0) + sizes[k])
        live = locate(plan, k, sizes)[1].astype(jnp.int32)
        alive = alive + jnp.where(row_level == k, live, 0)
    total = jnp.zeros(shape, jnp.int32)
    for s in range(plan.cols):
        columns = near[s][split : split + CODE_ROWS, :].astype(F32)[:TABLE_ROWS]
        columns = columns.astype(jnp.int32)
        level = jnp.zeros(shape, jnp.int32)
        for end in ends:
            level = level + (columns >= end).astype(jnp.int32)
        there = lax.rem(columns, plan.lanes)
        apart = lax.rem(there, PAIR) ^ core
        there = apart * (plan.lanes // PAIR) + there // PAIR
        place = jnp.where(
            (level < row_level) & (alive > 0),
            level * plan.lanes + there,
            row_level * plan.lanes,
        )
        place = jnp.where(entry < plan.entries, place, 0)
        total = total + (pltpu.roll(place, s * plan.entries, 1) if s else place)
    own = entry * plan.lanes + lax.axis_index("chain")
    own_level = jnp.zeros(shape, jnp.int32)
    for end in ends:
        own_level = own_level + (own >= end).astype(jnp.int32)
    table[...] = jnp.where(row_level == TABLE_ROWS - 1, own_level, total)


def after(far, segment, same):
    pass


def forward_second(plan, *refs):
    sizes, right, inverse = refs[:3]
    fronts = refs[3 : 3 + PAIR]
    near = refs[3 + PAIR : 3 + PAIR + plan.cols]
    out, table, draft, store, sem = refs[3 + PAIR + plan.cols :]
    fill_table(plan, sizes, near, draft)
    copy = pltpu.make_async_copy(draft, table, sem)
    copy.start()
    gather_store(plan, 1, fronts, store)
    copy.wait()
    segment = half_segment(plan, 1, table, right, inverse, near, store)
    out[...] = jnp.broadcast_to(segment[None], out.shape)


def forward_level(plan, level, *refs):
    table, right, inverse = refs[:3]
    sources = refs[3 : 3 + plan.cols]
    earlier = refs[3 + plan.cols : 3 + plan.cols + PAIR * level]
    out, store = refs[3 + plan.cols + PAIR * level :]
    gather_store(plan, level, earlier, store)
    segment = half_segment(plan, level, table, right, inverse, sources, store)
    out[...] = jnp.broadcast_to(segment[None], out.shape)


def turn_level(plan, level, *refs):
    table, right, inverse = refs[:3]
    sources = refs[3 : 3 + plan.cols]
    earlier = refs[3 + plan.cols : 3 + plan.cols + PAIR * level]
    half, solved, acc, out, store = refs[3 + plan.cols + PAIR * level :]
    gather_store(plan, level, earlier, store)
    acc[...] = jnp.zeros(acc.shape, F32)
    segment = half_segment(plan, level, table, right, inverse, sources, store)
    half[...] = segment
    segment = lax.dot_general(
        segment, inverse[level], NN, preferred_element_type=F32
    ).astype(BF16)
    solved[...] = segment
    add_terms(plan, level, table, segment, sources, acc)
    give_terms(plan, level - 1, acc, out)


def solve_back(half, inverse, arrived):
    summed = jnp.sum(arrived[...].astype(F32), axis=0)
    rest = (half.astype(F32) - summed).astype(BF16)
    return lax.dot_general(rest, inverse, NN, preferred_element_type=F32).astype(BF16)


def backward_level(plan, level, *refs):
    table, inverse, front, arrived, _ = refs[:5]
    sources = refs[5 : 5 + plan.cols]
    solved, acc, out = refs[5 + plan.cols :]
    segment = solve_back(front[lax.axis_index("chain") // PAIR], inverse[level], arrived)
    solved[...] = segment
    add_terms(plan, level, table, segment, sources, acc)
    give_terms(plan, level - 1, acc, out)


def finish(plan, *refs):
    levels = plan.levels
    table, inverse, arrived = refs[:3]
    fronts = refs[3 : 2 + levels]
    half_last = refs[2 + levels]
    done = refs[3 + levels : 2 + 2 * levels]
    out, hbuf, sbuf = refs[2 + 2 * levels :]
    lane = lax.axis_index("chain")
    for k in range(levels - 1):
        hbuf[k] = fronts[k][lane // PAIR]
        sbuf[k + 1] = done[k][...]
    hbuf[levels - 1] = half_last[...]
    sbuf[0] = solve_back(hbuf[0], inverse[0], arrived)
    for r in range(plan.rows):
        level = table[TABLE_ROWS - 1, r]
        h, s = hbuf[level], sbuf[level]
        for q in range(plan.cols):
            out[q, r] = h
            out[q, plan.rows + r] = s


def per_device(rhs, pattern, factor, inverse, level_size):
    lanes = lax.axis_size("chain")
    cols = lax.axis_size("col")
    rows, _, probes, width = rhs.shape
    entries = pattern.shape[2]
    levels = level_size.shape[0]
    share = probes // cols
    plan = Plan(lanes, cols, rows, entries, share, width, levels)

    smem = pl.BlockSpec(memory_space=pltpu.SMEM)
    hbm = pl.BlockSpec(memory_space=pltpu.HBM)
    vmem = pl.BlockSpec(memory_space=pltpu.VMEM)
    segment_shape = pltpu.VMEM((share, width), BF16)
    front_shape = pltpu.VMEM((lanes // PAIR, share, width), BF16)
    terms_shape = pltpu.VMEM((lanes // PAIR, PAIR, share, width), BF16)
    params = pltpu.CompilerParams(vmem_limit_bytes=12 * 1024 * 1024)

    def far_off(x):
        return pltpu.with_memory_space_constraint(x, pltpu.HBM)

    def held(x):
        return pltpu.with_memory_space_constraint(x, pltpu.VMEM)

    def scalars(x):
        return pltpu.with_memory_space_constraint(x, pltpu.SMEM)

    def store(level):
        return pltpu.VMEM((level * lanes + 1, share, width), BF16)

    def exchange(x):
        groups = [list(range(i, lanes, PAIR)) for i in range(PAIR)]
        own = lax.all_to_all(x, "chain", 0, 0, tiled=True, axis_index_groups=groups)
        other = lax.ppermute(own, "chain", [(i, i ^ 1) for i in range(lanes)])
        return [held(own), held(other)]

    def exchange_back(x):
        x = x.reshape(lanes, share, width)
        return held(lax.all_to_all(x, "chain", 0, 0, tiled=True))

    def around(x):
        return [held(x)] + [
            held(lax.ppermute(x, "col", [(i, i ^ s) for i in range(cols)]))
            for s in (1, 3, 2)
        ]

    factor = far_off(factor.reshape(rows * plan.entries * width, width))
    far_shape = pltpu.VMEM((len(plan.far) * plan.deep, width), BF16)
    first, own, later, rights, inverses, sizes = pl.pallas_call(
        functools.partial(forward_first, plan),
        out_shape=(
            front_shape,
            pltpu.VMEM((len(plan.near) * plan.deep + CODE_ROWS, width), BF16),
            far_shape,
            pltpu.VMEM((levels, share, width), BF16),
            pltpu.VMEM((levels, width, width), BF16),
            pltpu.SMEM((levels,), jnp.int32),
        ),
        in_specs=[hbm] * 5,
        out_specs=(vmem,) * 5 + (smem,),
        scratch_shapes=[
            pltpu.VMEM((rows, 1, entries), jnp.int32),
            pltpu.VMEM((rows * plan.deep, width), BF16),
            pltpu.VMEM((rows, share, width), BF16),
            pltpu.VMEM((rows, width, width), BF16),
            pltpu.VMEM((CODE_ROWS, width), F32),
            pltpu.SemaphoreType.DMA((5,)),
        ],
        compiler_params=params,
        name="forward_first",
    )(
        far_off(level_size),
        far_off(pattern),
        factor,
        far_off(rhs.reshape(rows, cols, share, width)),
        far_off(inverse.reshape(rows, width, width)),
    )
    rights, inverses, sizes = held(rights), held(inverses), scalars(sizes)
    near = around(own)
    fronts = exchange(first)
    mine, table = pl.pallas_call(
        functools.partial(forward_second, plan),
        out_shape=(
            front_shape,
            pltpu.SMEM((TABLE_ROWS, width), jnp.int32),
        ),
        in_specs=[smem] + [vmem] * (2 + PAIR + cols),
        out_specs=(vmem, smem),
        scratch_shapes=[
            pltpu.VMEM((TABLE_ROWS, width), jnp.int32),
            store(1),
            pltpu.SemaphoreType.DMA,
        ],
        compiler_params=params,
        name="forward_second",
    )(sizes, rights, inverses, *fronts, *near)
    table = scalars(table)
    later = pl.pallas_call(
        after,
        out_shape=far_shape,
        in_specs=[vmem, vmem],
        out_specs=vmem,
        input_output_aliases={0: 0},
        compiler_params=params,
        name="after",
    )(held(later), held(mine))
    far = around(later)
    fronts += exchange(mine)

    def sources(level):
        return near if level in plan.near else far

    for k in range(2, levels - 1):
        mine = pl.pallas_call(
            functools.partial(forward_level, plan, k),
            out_shape=front_shape,
            in_specs=[smem] + [vmem] * (2 + cols + PAIR * k),
            out_specs=vmem,
            scratch_shapes=[store(k)],
            compiler_params=params,
            name=f"forward_level_{k}",
        )(table, rights, inverses, *sources(k), *fronts)
        fronts += exchange(mine)

    last = levels - 1
    acc_shape = pltpu.VMEM((last * lanes + 1, share, width), F32)
    half_last, solved, acc, terms = pl.pallas_call(
        functools.partial(turn_level, plan, last),
        out_shape=(segment_shape, segment_shape, acc_shape, terms_shape),
        in_specs=[smem] + [vmem] * (2 + cols + PAIR * last),
        out_specs=(vmem,) * 4,
        scratch_shapes=[store(last)],
        compiler_params=params,
        name="turn_level",
    )(table, rights, inverses, *sources(last), *fronts)
    done = [held(solved)]
    for k in range(last - 1, 0, -1):
        solved, acc, terms = pl.pallas_call(
            functools.partial(backward_level, plan, k),
            out_shape=(segment_shape, acc_shape, terms_shape),
            in_specs=[smem] + [vmem] * (4 + cols),
            out_specs=(vmem,) * 3,
            input_output_aliases={4: 1},
            compiler_params=params,
            name=f"backward_level_{k}",
        )(
            table,
            inverses,
            fronts[PAIR * k],
            exchange_back(terms),
            held(acc),
            *sources(k),
        )
        done.insert(0, held(solved))
    shares = pl.pallas_call(
        functools.partial(finish, plan),
        out_shape=pltpu.VMEM((cols, 2 * rows, share, width), BF16),
        in_specs=[smem] + [vmem] * (1 + 2 * levels),
        out_specs=vmem,
        scratch_shapes=[
            pltpu.VMEM((levels, share, width), BF16),
            pltpu.VMEM((levels, share, width), BF16),
        ],
        compiler_params=params,
        name="finish",
    )(table, inverses, exchange_back(terms), *fronts[::PAIR], held(half_last), *done)
    whole = lax.all_to_all(shares, "col", 0, 0, tiled=True)
    whole = whole.transpose(1, 0, 2, 3).reshape(2, rows, 1, probes, width)
    return whole[0], whole[1]


def solution(mesh):
    return jax.shard_map(
        per_device,
        mesh=mesh,
        in_specs=(
            P(None, "chain", None, None),
            P(None, "chain", "col"),
            P(None, "chain", "col", None, None),
            P(None, "chain", None, None),
            P(),
        ),
        out_specs=(P(None, "chain", None, None), P(None, "chain", None, None)),
        check_vma=False,
    )
```

```python
import functools
import jax
import jax.numpy as jnp
from jax import lax
from jax.experimental import pallas as pl
from jax.experimental.pallas import tpu as pltpu
from jax.sharding import PartitionSpec as P

BF16 = jnp.bfloat16
F32 = jnp.float32
NT = (((1,), (1,)), ((), ()))
NN = (((1,), (0,)), ((), ()))
CODE_ROWS = 16
TABLE_ROWS = 8
PAIR = 2


class Plan:
    def __init__(self, lanes, cols, rows, entries, share, width, levels):
        self.lanes, self.cols, self.rows, self.entries = lanes, cols, rows, entries
        self.share, self.width, self.levels = share, width, levels
        self.deep = entries * width
        self.near = range(1, min(3, levels))
        self.far = range(min(3, levels), levels)

    def slots(self, level):
        return max(0, self.rows - (self.levels - level)), min(level, self.rows - 1)


def locate(plan, level, sizes):
    lane = lax.axis_index("chain")
    start = jnp.int32(0)
    for k in range(level):
        start = start + sizes[k]
    slot = (start - lane + (plan.lanes - 1)) // plan.lanes
    live = (slot < plan.rows) & (slot * plan.lanes + lane < start + sizes[level])
    low, high = plan.slots(level)
    return jnp.clip(slot, low, high), live


def weights_of(plan, level, sources):
    base = (level - (plan.near if level in plan.near else plan.far)[0]) * plan.deep
    return jnp.concatenate(
        [
            source[base + e * plan.width : base + (e + 1) * plan.width, :]
            for source in sources
            for e in range(plan.entries)
        ],
        axis=1,
    )


def places_of(plan, level, table):
    return [
        table[level, s * plan.entries + e]
        for s in range(plan.cols)
        for e in range(plan.entries)
    ]


def gather_store(plan, level, earlier, store):
    part = plan.lanes // PAIR
    for k in range(PAIR * level):
        store[pl.ds(k * part, part)] = earlier[k][...]
    store[level * plan.lanes] = jnp.zeros(store.shape[1:], BF16)


def half_segment(plan, level, table, right, inverse, sources, store):
    chosen = jnp.concatenate([store[at] for at in places_of(plan, level, table)], axis=1)
    weights = weights_of(plan, level, sources)
    summed = lax.dot_general(chosen, weights, NT, preferred_element_type=F32)
    rest = (right[level].astype(F32) - summed).astype(BF16)
    return lax.dot_general(
        rest, inverse[level], NT, preferred_element_type=F32
    ).astype(BF16)


def add_terms(plan, level, table, segment, sources, acc):
    weights = weights_of(plan, level, sources)
    terms = lax.dot_general(segment, weights, NN, preferred_element_type=F32)
    for j, at in enumerate(places_of(plan, level, table)):
        acc[at] = acc[at] + terms[:, j * plan.width : (j + 1) * plan.width]


def give_terms(plan, level, acc, own, other):
    part = plan.lanes // PAIR
    own[...] = acc[pl.ds(level * plan.lanes, part)]
    other[...] = acc[pl.ds(level * plan.lanes + part, part)].astype(BF16)


def add_other(own, other, out):
    out[...] = (own[...] + other[...].astype(F32)).astype(BF16)


def forward_first(plan, *refs):
    level_size, pattern, factor, right, inverse = refs[:5]
    out, near, far, rights, inverses, sizes = refs[5:11]
    pats, blocks, sides, diagonal, wide, sems = refs[11:]
    col = lax.axis_index("col")
    loads = [
        (level_size, sizes),
        (inverse, diagonal),
        (right.at[:, col], sides),
        (factor, blocks),
        (pattern, pats),
    ]
    copies = [
        pltpu.make_async_copy(source, target, sems.at[i])
        for i, (source, target) in enumerate(loads)
    ]
    for c in copies:
        c.start()
    wide[...] = jnp.zeros(wide.shape, F32)
    copies[0].wait()
    slots = [locate(plan, k, sizes)[0] for k in range(plan.levels)]
    copies[1].wait()
    copies[2].wait()
    segment = lax.dot_general(
        sides[0], diagonal[0], NT, preferred_element_type=F32
    ).astype(BF16)
    out[...] = jnp.broadcast_to(segment[None], out.shape)
    for k in range(plan.levels):
        rights[k] = sides[slots[k]]
        inverses[k] = diagonal[slots[k]]
    copies[3].wait()
    copies[4].wait()
    for target, levels in ((near, plan.near), (far, plan.far)):
        for i, k in enumerate(levels):
            at = pl.multiple_of(slots[k] * plan.deep, plan.deep)
            target[pl.ds(i * plan.deep, plan.deep), :] = blocks[
                pl.ds(at, plan.deep), :
            ]
    for k in range(1, plan.levels):
        wide[pl.ds(k, 1), pl.ds(0, plan.entries)] = pats[slots[k]].astype(F32)
    near[pl.ds(len(plan.near) * plan.deep, CODE_ROWS), :] = wide[...].astype(BF16)


def fill_table(plan, sizes, near, table):
    core = lax.rem(lax.axis_index("chain"), PAIR)
    split = len(plan.near) * plan.deep
    shape = (TABLE_ROWS, plan.width)
    row_level = lax.broadcasted_iota(jnp.int32, shape, 0)
    entry = lax.broadcasted_iota(jnp.int32, shape, 1)
    alive = jnp.zeros(shape, jnp.int32)
    ends = []
    for k in range(plan.levels):
        ends.append((ends[-1] if ends else 0) + sizes[k])
        live = locate(plan, k, sizes)[1].astype(jnp.int32)
        alive = alive + jnp.where(row_level == k, live, 0)
    total = jnp.zeros(shape, jnp.int32)
    for s in range(plan.cols):
        columns = near[s][split : split + CODE_ROWS, :].astype(F32)[:TABLE_ROWS]
        columns = columns.astype(jnp.int32)
        level = jnp.zeros(shape, jnp.int32)
        for end in ends:
            level = level + (columns >= end).astype(jnp.int32)
        there = lax.rem(columns, plan.lanes)
        apart = lax.rem(there, PAIR) ^ core
        there = apart * (plan.lanes // PAIR) + there // PAIR
        place = jnp.where(
            (level < row_level) & (alive > 0),
            level * plan.lanes + there,
            row_level * plan.lanes,
        )
        place = jnp.where(entry < plan.entries, place, 0)
        total = total + (pltpu.roll(place, s * plan.entries, 1) if s else place)
    own = entry * plan.lanes + lax.axis_index("chain")
    own_level = jnp.zeros(shape, jnp.int32)
    for end in ends:
        own_level = own_level + (own >= end).astype(jnp.int32)
    table[...] = jnp.where(row_level == TABLE_ROWS - 1, own_level, total)


def after(far, segment, same):
    pass


def forward_second(plan, *refs):
    sizes, right, inverse = refs[:3]
    fronts = refs[3 : 3 + PAIR]
    near = refs[3 + PAIR : 3 + PAIR + plan.cols]
    out, table, draft, store, sem = refs[3 + PAIR + plan.cols :]
    fill_table(plan, sizes, near, draft)
    copy = pltpu.make_async_copy(draft, table, sem)
    copy.start()
    gather_store(plan, 1, fronts, store)
    copy.wait()
    segment = half_segment(plan, 1, table, right, inverse, near, store)
    out[...] = jnp.broadcast_to(segment[None], out.shape)


def forward_level(plan, level, *refs):
    table, right, inverse = refs[:3]
    sources = refs[3 : 3 + plan.cols]
    earlier = refs[3 + plan.cols : 3 + plan.cols + PAIR * level]
    out, store = refs[3 + plan.cols + PAIR * level :]
    gather_store(plan, level, earlier, store)
    segment = half_segment(plan, level, table, right, inverse, sources, store)
    out[...] = jnp.broadcast_to(segment[None], out.shape)


def turn_level(plan, level, *refs):
    table, right, inverse = refs[:3]
    sources = refs[3 : 3 + plan.cols]
    earlier = refs[3 + plan.cols : 3 + plan.cols + PAIR * level]
    half, solved, acc, own, other, store = refs[3 + plan.cols + PAIR * level :]
    gather_store(plan, level, earlier, store)
    acc[...] = jnp.zeros(acc.shape, F32)
    segment = half_segment(plan, level, table, right, inverse, sources, store)
    half[...] = segment
    segment = lax.dot_general(
        segment, inverse[level], NN, preferred_element_type=F32
    ).astype(BF16)
    solved[...] = segment
    add_terms(plan, level, table, segment, sources, acc)
    give_terms(plan, level - 1, acc, own, other)


def solve_back(half, inverse, arrived):
    summed = jnp.sum(arrived[...].astype(F32), axis=0)
    rest = (half.astype(F32) - summed).astype(BF16)
    return lax.dot_general(rest, inverse, NN, preferred_element_type=F32).astype(BF16)


def backward_level(plan, level, *refs):
    table, inverse, front, arrived, _ = refs[:5]
    sources = refs[5 : 5 + plan.cols]
    solved, acc, own, other = refs[5 + plan.cols :]
    segment = solve_back(front[lax.axis_index("chain") // PAIR], inverse[level], arrived)
    solved[...] = segment
    add_terms(plan, level, table, segment, sources, acc)
    give_terms(plan, level - 1, acc, own, other)


def finish(plan, *refs):
    levels = plan.levels
    table, inverse, arrived = refs[:3]
    fronts = refs[3 : 2 + levels]
    half_last = refs[2 + levels]
    done = refs[3 + levels : 2 + 2 * levels]
    out, hbuf, sbuf = refs[2 + 2 * levels :]
    lane = lax.axis_index("chain")
    for k in range(levels - 1):
        hbuf[k] = fronts[k][lane // PAIR]
        sbuf[k + 1] = done[k][...]
    hbuf[levels - 1] = half_last[...]
    sbuf[0] = solve_back(hbuf[0], inverse[0], arrived)
    for r in range(plan.rows):
        level = table[TABLE_ROWS - 1, r]
        h, s = hbuf[level], sbuf[level]
        for q in range(plan.cols):
            out[q, r] = h
            out[q, plan.rows + r] = s


def per_device(rhs, pattern, factor, inverse, level_size):
    lanes = lax.axis_size("chain")
    cols = lax.axis_size("col")
    rows, _, probes, width = rhs.shape
    entries = pattern.shape[2]
    levels = level_size.shape[0]
    share = probes // cols
    plan = Plan(lanes, cols, rows, entries, share, width, levels)

    smem = pl.BlockSpec(memory_space=pltpu.SMEM)
    hbm = pl.BlockSpec(memory_space=pltpu.HBM)
    vmem = pl.BlockSpec(memory_space=pltpu.VMEM)
    segment_shape = pltpu.VMEM((share, width), BF16)
    front_shape = pltpu.VMEM((lanes // PAIR, share, width), BF16)
    own_shape = pltpu.VMEM((lanes // PAIR, share, width), F32)
    params = pltpu.CompilerParams(vmem_limit_bytes=12 * 1024 * 1024)

    def far_off(x):
        return pltpu.with_memory_space_constraint(x, pltpu.HBM)

    def held(x):
        return pltpu.with_memory_space_constraint(x, pltpu.VMEM)

    def scalars(x):
        return pltpu.with_memory_space_constraint(x, pltpu.SMEM)

    def store(level):
        return pltpu.VMEM((level * lanes + 1, share, width), BF16)

    def across(x):
        return held(lax.ppermute(x, "chain", [(i, i ^ 1) for i in range(lanes)]))

    def among(x):
        groups = [list(range(i, lanes, PAIR)) for i in range(PAIR)]
        return held(
            lax.all_to_all(x, "chain", 0, 0, tiled=True, axis_index_groups=groups)
        )

    def exchange(x):
        own = among(x)
        return [own, across(own)]

    def exchange_back(own, other):
        whole = pl.pallas_call(
            add_other,
            out_shape=front_shape,
            in_specs=[vmem, vmem],
            out_specs=vmem,
            compiler_params=params,
            name="add_other",
        )(held(own), across(other))
        return among(whole)

    def around(x):
        return [held(x)] + [
            held(lax.ppermute(x, "col", [(i, i ^ s) for i in range(cols)]))
            for s in (1, 3, 2)
        ]

    factor = far_off(factor.reshape(rows * plan.entries * width, width))
    far_shape = pltpu.VMEM((len(plan.far) * plan.deep, width), BF16)
    first, own, later, rights, inverses, sizes = pl.pallas_call(
        functools.partial(forward_first, plan),
        out_shape=(
            front_shape,
            pltpu.VMEM((len(plan.near) * plan.deep + CODE_ROWS, width), BF16),
            far_shape,
            pltpu.VMEM((levels, share, width), BF16),
            pltpu.VMEM((levels, width, width), BF16),
            pltpu.SMEM((levels,), jnp.int32),
        ),
        in_specs=[hbm] * 5,
        out_specs=(vmem,) * 5 + (smem,),
        scratch_shapes=[
            pltpu.VMEM((rows, 1, entries), jnp.int32),
            pltpu.VMEM((rows * plan.deep, width), BF16),
            pltpu.VMEM((rows, share, width), BF16),
            pltpu.VMEM((rows, width, width), BF16),
            pltpu.VMEM((CODE_ROWS, width), F32),
            pltpu.SemaphoreType.DMA((5,)),
        ],
        compiler_params=params,
        name="forward_first",
    )(
        far_off(level_size),
        far_off(pattern),
        factor,
        far_off(rhs.reshape(rows, cols, share, width)),
        far_off(inverse.reshape(rows, width, width)),
    )
    rights, inverses, sizes = held(rights), held(inverses), scalars(sizes)
    near = around(own)
    fronts = exchange(first)
    mine, table = pl.pallas_call(
        functools.partial(forward_second, plan),
        out_shape=(
            front_shape,
            pltpu.SMEM((TABLE_ROWS, width), jnp.int32),
        ),
        in_specs=[smem] + [vmem] * (2 + PAIR + cols),
        out_specs=(vmem, smem),
        scratch_shapes=[
            pltpu.VMEM((TABLE_ROWS, width), jnp.int32),
            store(1),
            pltpu.SemaphoreType.DMA,
        ],
        compiler_params=params,
        name="forward_second",
    )(sizes, rights, inverses, *fronts, *near)
    table = scalars(table)
    later = pl.pallas_call(
        after,
        out_shape=far_shape,
        in_specs=[vmem, vmem],
        out_specs=vmem,
        input_output_aliases={0: 0},
        compiler_params=params,
        name="after",
    )(held(later), held(mine))
    far = around(later)
    fronts += exchange(mine)

    def sources(level):
        return near if level in plan.near else far

    for k in range(2, levels - 1):
        mine = pl.pallas_call(
            functools.partial(forward_level, plan, k),
            out_shape=front_shape,
            in_specs=[smem] + [vmem] * (2 + cols + PAIR * k),
            out_specs=vmem,
            scratch_shapes=[store(k)],
            compiler_params=params,
            name=f"forward_level_{k}",
        )(table, rights, inverses, *sources(k), *fronts)
        fronts += exchange(mine)

    last = levels - 1
    acc_shape = pltpu.VMEM((last * lanes + 1, share, width), F32)
    half_last, solved, acc, *terms = pl.pallas_call(
        functools.partial(turn_level, plan, last),
        out_shape=(segment_shape, segment_shape, acc_shape, own_shape, front_shape),
        in_specs=[smem] + [vmem] * (2 + cols + PAIR * last),
        out_specs=(vmem,) * 5,
        scratch_shapes=[store(last)],
        compiler_params=params,
        name="turn_level",
    )(table, rights, inverses, *sources(last), *fronts)
    done = [held(solved)]
    for k in range(last - 1, 0, -1):
        solved, acc, *terms = pl.pallas_call(
            functools.partial(backward_level, plan, k),
            out_shape=(segment_shape, acc_shape, own_shape, front_shape),
            in_specs=[smem] + [vmem] * (4 + cols),
            out_specs=(vmem,) * 4,
            input_output_aliases={4: 1},
            compiler_params=params,
            name=f"backward_level_{k}",
        )(
            table,
            inverses,
            fronts[PAIR * k],
            exchange_back(*terms),
            held(acc),
            *sources(k),
        )
        done.insert(0, held(solved))
    shares = pl.pallas_call(
        functools.partial(finish, plan),
        out_shape=pltpu.VMEM((cols, 2 * rows, share, width), BF16),
        in_specs=[smem] + [vmem] * (1 + 2 * levels),
        out_specs=vmem,
        scratch_shapes=[
            pltpu.VMEM((levels, share, width), BF16),
            pltpu.VMEM((levels, share, width), BF16),
        ],
        compiler_params=params,
        name="finish",
    )(table, inverses, exchange_back(*terms), *fronts[::PAIR], held(half_last), *done)
    whole = lax.all_to_all(shares, "col", 0, 0, tiled=True)
    whole = whole.transpose(1, 0, 2, 3).reshape(2, rows, 1, probes, width)
    return whole[0], whole[1]


def solution(mesh):
    return jax.shard_map(
        per_device,
        mesh=mesh,
        in_specs=(
            P(None, "chain", None, None),
            P(None, "chain", "col"),
            P(None, "chain", "col", None, None),
            P(None, "chain", None, None),
            P(),
        ),
        out_specs=(P(None, "chain", None, None), P(None, "chain", None, None)),
        check_vma=False,
    )
```

```python
import functools
import jax
import jax.numpy as jnp
from jax import lax
from jax.experimental import pallas as pl
from jax.experimental.pallas import tpu as pltpu
from jax.sharding import PartitionSpec as P

BF16 = jnp.bfloat16
F32 = jnp.float32
NT = (((1,), (1,)), ((), ()))
NN = (((1,), (0,)), ((), ()))
CODE_ROWS = 16
TABLE_ROWS = 8
PAIR = 2


class Plan:
    def __init__(self, lanes, cols, rows, entries, share, width, levels):
        self.lanes, self.cols, self.rows, self.entries = lanes, cols, rows, entries
        self.share, self.width, self.levels = share, width, levels
        self.deep = entries * width
        self.near = range(1, min(3, levels))
        self.far = range(min(3, levels), levels)

    def slots(self, level):
        return max(0, self.rows - (self.levels - level)), min(level, self.rows - 1)


def locate(plan, level, sizes):
    lane = lax.axis_index("chain")
    start = jnp.int32(0)
    for k in range(level):
        start = start + sizes[k]
    slot = (start - lane + (plan.lanes - 1)) // plan.lanes
    live = (slot < plan.rows) & (slot * plan.lanes + lane < start + sizes[level])
    low, high = plan.slots(level)
    return jnp.clip(slot, low, high), live


def weights_of(plan, level, sources):
    base = (level - (plan.near if level in plan.near else plan.far)[0]) * plan.deep
    return jnp.concatenate(
        [
            source[base + e * plan.width : base + (e + 1) * plan.width, :]
            for source in sources
            for e in range(plan.entries)
        ],
        axis=1,
    )


def places_of(plan, level, table):
    return [
        table[level, s * plan.entries + e]
        for s in range(plan.cols)
        for e in range(plan.entries)
    ]


def gather_store(plan, level, earlier, store):
    part = plan.lanes // PAIR
    for k in range(PAIR * level):
        store[pl.ds(k * part, part)] = earlier[k][...]
    store[level * plan.lanes] = jnp.zeros(store.shape[1:], BF16)


def half_segment(plan, level, table, right, inverse, sources, store):
    chosen = jnp.concatenate([store[at] for at in places_of(plan, level, table)], axis=1)
    weights = weights_of(plan, level, sources)
    summed = lax.dot_general(chosen, weights, NT, preferred_element_type=F32)
    rest = (right[level].astype(F32) - summed).astype(BF16)
    return lax.dot_general(
        rest, inverse[level], NT, preferred_element_type=F32
    ).astype(BF16)


def add_terms(plan, level, table, segment, sources, acc):
    weights = weights_of(plan, level, sources)
    terms = lax.dot_general(segment, weights, NN, preferred_element_type=F32)
    for j, at in enumerate(places_of(plan, level, table)):
        acc[at] = acc[at] + terms[:, j * plan.width : (j + 1) * plan.width]


def give_terms(plan, level, acc, own, other):
    part = plan.lanes // PAIR
    own[...] = acc[pl.ds(level * plan.lanes, part)]
    other[...] = acc[pl.ds(level * plan.lanes + part, part)].astype(BF16)


def add_other(own, other, out):
    out[...] = (own[...] + other[...].astype(F32)).astype(BF16)


def forward_first(plan, *refs):
    level_size, pattern, factor, right, inverse = refs[:5]
    out, near, far, rights, inverses, sizes = refs[5:11]
    pats, blocks, sides, diagonal, wide, sems = refs[11:]
    col = lax.axis_index("col")
    loads = [
        (level_size, sizes),
        (inverse, diagonal),
        (right.at[:, col], sides),
        (factor, blocks),
        (pattern, pats),
    ]
    copies = [
        pltpu.make_async_copy(source, target, sems.at[i])
        for i, (source, target) in enumerate(loads)
    ]
    for c in copies:
        c.start()
    wide[...] = jnp.zeros(wide.shape, F32)
    copies[0].wait()
    slots = [locate(plan, k, sizes)[0] for k in range(plan.levels)]
    copies[1].wait()
    copies[2].wait()
    segment = lax.dot_general(
        sides[0], diagonal[0], NT, preferred_element_type=F32
    ).astype(BF16)
    out[...] = jnp.broadcast_to(segment[None], out.shape)
    for k in range(plan.levels):
        rights[k] = sides[slots[k]]
        inverses[k] = diagonal[slots[k]]
    copies[3].wait()
    copies[4].wait()
    for target, levels in ((near, plan.near), (far, plan.far)):
        for i, k in enumerate(levels):
            at = pl.multiple_of(slots[k] * plan.deep, plan.deep)
            target[pl.ds(i * plan.deep, plan.deep), :] = blocks[
                pl.ds(at, plan.deep), :
            ]
    for k in range(1, plan.levels):
        wide[pl.ds(k, 1), pl.ds(0, plan.entries)] = pats[slots[k]].astype(F32)
    near[pl.ds(len(plan.near) * plan.deep, CODE_ROWS), :] = wide[...].astype(BF16)


def fill_table(plan, sizes, near, table):
    core = lax.rem(lax.axis_index("chain"), PAIR)
    split = len(plan.near) * plan.deep
    shape = (TABLE_ROWS, plan.width)
    row_level = lax.broadcasted_iota(jnp.int32, shape, 0)
    entry = lax.broadcasted_iota(jnp.int32, shape, 1)
    alive = jnp.zeros(shape, jnp.int32)
    ends = []
    for k in range(plan.levels):
        ends.append((ends[-1] if ends else 0) + sizes[k])
        live = locate(plan, k, sizes)[1].astype(jnp.int32)
        alive = alive + jnp.where(row_level == k, live, 0)
    total = jnp.zeros(shape, jnp.int32)
    for s in range(plan.cols):
        columns = near[s][split : split + CODE_ROWS, :].astype(F32)[:TABLE_ROWS]
        columns = columns.astype(jnp.int32)
        level = jnp.zeros(shape, jnp.int32)
        for end in ends:
            level = level + (columns >= end).astype(jnp.int32)
        there = lax.rem(columns, plan.lanes)
        apart = lax.rem(there, PAIR) ^ core
        there = apart * (plan.lanes // PAIR) + there // PAIR
        place = jnp.where(
            (level < row_level) & (alive > 0),
            level * plan.lanes + there,
            row_level * plan.lanes,
        )
        place = jnp.where(entry < plan.entries, place, 0)
        total = total + (pltpu.roll(place, s * plan.entries, 1) if s else place)
    own = entry * plan.lanes + lax.axis_index("chain")
    own_level = jnp.zeros(shape, jnp.int32)
    for end in ends:
        own_level = own_level + (own >= end).astype(jnp.int32)
    table[...] = jnp.where(row_level == TABLE_ROWS - 1, own_level, total)


def after(far, segment, same):
    pass


def forward_second(plan, *refs):
    sizes, right, inverse = refs[:3]
    fronts = refs[3 : 3 + PAIR]
    near = refs[3 + PAIR : 3 + PAIR + plan.cols]
    out, table, draft, store, sem = refs[3 + PAIR + plan.cols :]
    fill_table(plan, sizes, near, draft)
    copy = pltpu.make_async_copy(draft, table, sem)
    copy.start()
    gather_store(plan, 1, fronts, store)
    copy.wait()
    segment = half_segment(plan, 1, table, right, inverse, near, store)
    out[...] = jnp.broadcast_to(segment[None], out.shape)


def forward_level(plan, level, *refs):
    table, right, inverse = refs[:3]
    sources = refs[3 : 3 + plan.cols]
    earlier = refs[3 + plan.cols : 3 + plan.cols + PAIR * level]
    out, store = refs[3 + plan.cols + PAIR * level :]
    gather_store(plan, level, earlier, store)
    segment = half_segment(plan, level, table, right, inverse, sources, store)
    out[...] = jnp.broadcast_to(segment[None], out.shape)


def turn_level(plan, level, *refs):
    table, right, inverse = refs[:3]
    sources = refs[3 : 3 + plan.cols]
    earlier = refs[3 + plan.cols : 3 + plan.cols + PAIR * level]
    half, solved, acc, own, other, store = refs[3 + plan.cols + PAIR * level :]
    gather_store(plan, level, earlier, store)
    acc[...] = jnp.zeros(acc.shape, F32)
    segment = half_segment(plan, level, table, right, inverse, sources, store)
    half[...] = segment
    segment = lax.dot_general(
        segment, inverse[level], NN, preferred_element_type=F32
    ).astype(BF16)
    solved[...] = segment
    add_terms(plan, level, table, segment, sources, acc)
    give_terms(plan, level - 1, acc, own, other)


def solve_back(half, inverse, arrived):
    summed = jnp.sum(arrived[...].astype(F32), axis=0)
    rest = (half.astype(F32) - summed).astype(BF16)
    return lax.dot_general(rest, inverse, NN, preferred_element_type=F32).astype(BF16)


def backward_level(plan, level, *refs):
    table, inverse, front, arrived, _ = refs[:5]
    sources = refs[5 : 5 + plan.cols]
    solved, acc, own, other = refs[5 + plan.cols :]
    segment = solve_back(front[lax.axis_index("chain") // PAIR], inverse[level], arrived)
    solved[...] = segment
    add_terms(plan, level, table, segment, sources, acc)
    give_terms(plan, level - 1, acc, own, other)


def finish(plan, *refs):
    levels = plan.levels
    table, inverse, arrived = refs[:3]
    fronts = refs[3 : 2 + levels]
    half_last = refs[2 + levels]
    done = refs[3 + levels : 2 + 2 * levels]
    out, hbuf, sbuf = refs[2 + 2 * levels :]
    lane = lax.axis_index("chain")
    for k in range(levels - 1):
        hbuf[k] = fronts[k][lane // PAIR]
        sbuf[k + 1] = done[k][...]
    hbuf[levels - 1] = half_last[...]
    sbuf[0] = solve_back(hbuf[0], inverse[0], arrived)
    for r in range(plan.rows):
        level = table[TABLE_ROWS - 1, r]
        h, s = hbuf[level], sbuf[level]
        for q in range(plan.cols):
            out[q, r] = h
            out[q, plan.rows + r] = s


def per_device(rhs, pattern, factor, inverse, level_size):
    lanes = lax.axis_size("chain")
    cols = lax.axis_size("col")
    rows, _, probes, width = rhs.shape
    entries = pattern.shape[2]
    levels = level_size.shape[0]
    share = probes // cols
    plan = Plan(lanes, cols, rows, entries, share, width, levels)

    smem = pl.BlockSpec(memory_space=pltpu.SMEM)
    hbm = pl.BlockSpec(memory_space=pltpu.HBM)
    vmem = pl.BlockSpec(memory_space=pltpu.VMEM)
    segment_shape = pltpu.VMEM((share, width), BF16)
    front_shape = pltpu.VMEM((lanes // PAIR, share, width), BF16)
    own_shape = pltpu.VMEM((lanes // PAIR, share, width), F32)
    params = pltpu.CompilerParams(vmem_limit_bytes=12 * 1024 * 1024)

    def far_off(x):
        return pltpu.with_memory_space_constraint(x, pltpu.HBM)

    def held(x):
        return pltpu.with_memory_space_constraint(x, pltpu.VMEM)

    def scalars(x):
        return pltpu.with_memory_space_constraint(x, pltpu.SMEM)

    def store(level):
        return pltpu.VMEM((level * lanes + 1, share, width), BF16)

    def across(x):
        return held(lax.ppermute(x, "chain", [(i, i ^ 1) for i in range(lanes)]))

    def among(x):
        groups = [list(range(i, lanes, PAIR)) for i in range(PAIR)]
        return held(
            lax.all_to_all(x, "chain", 0, 0, tiled=True, axis_index_groups=groups)
        )

    def exchange(x):
        own = among(x)
        return [own, across(own)]

    def exchange_back(own, other):
        whole = pl.pallas_call(
            add_other,
            out_shape=front_shape,
            in_specs=[vmem, vmem],
            out_specs=vmem,
            compiler_params=params,
            name="add_other",
        )(held(own), across(other))
        return among(whole)

    def around(x):
        return [held(x)] + [
            held(lax.ppermute(x, "col", [(i, i ^ s) for i in range(cols)]))
            for s in (1, 3, 2)
        ]

    factor = far_off(factor.reshape(rows * plan.entries * width, width))
    far_shape = pltpu.VMEM((len(plan.far) * plan.deep, width), BF16)
    first, own, later, rights, inverses, sizes = pl.pallas_call(
        functools.partial(forward_first, plan),
        out_shape=(
            front_shape,
            pltpu.VMEM((len(plan.near) * plan.deep + CODE_ROWS, width), BF16),
            far_shape,
            pltpu.VMEM((levels, share, width), BF16),
            pltpu.VMEM((levels, width, width), BF16),
            pltpu.SMEM((levels,), jnp.int32),
        ),
        in_specs=[hbm] * 5,
        out_specs=(vmem,) * 5 + (smem,),
        scratch_shapes=[
            pltpu.VMEM((rows, 1, entries), jnp.int32),
            pltpu.VMEM((rows * plan.deep, width), BF16),
            pltpu.VMEM((rows, share, width), BF16),
            pltpu.VMEM((rows, width, width), BF16),
            pltpu.VMEM((CODE_ROWS, width), F32),
            pltpu.SemaphoreType.DMA((5,)),
        ],
        compiler_params=params,
        name="forward_first",
    )(
        far_off(level_size),
        far_off(pattern),
        factor,
        far_off(rhs.reshape(rows, cols, share, width)),
        far_off(inverse.reshape(rows, width, width)),
    )
    rights, inverses, sizes = held(rights), held(inverses), scalars(sizes)
    near = around(own)
    fronts = exchange(first)
    later = pl.pallas_call(
        after,
        out_shape=far_shape,
        in_specs=[vmem, vmem],
        out_specs=vmem,
        input_output_aliases={0: 0},
        compiler_params=params,
        name="after",
    )(held(later), fronts[0])
    far = around(later)

    mine, table = pl.pallas_call(
        functools.partial(forward_second, plan),
        out_shape=(
            front_shape,
            pltpu.SMEM((TABLE_ROWS, width), jnp.int32),
        ),
        in_specs=[smem] + [vmem] * (2 + PAIR + cols),
        out_specs=(vmem, smem),
        scratch_shapes=[
            pltpu.VMEM((TABLE_ROWS, width), jnp.int32),
            store(1),
            pltpu.SemaphoreType.DMA,
        ],
        compiler_params=params,
        name="forward_second",
    )(sizes, rights, inverses, *fronts, *near)
    table = scalars(table)
    fronts += exchange(mine)

    def sources(level):
        return near if level in plan.near else far

    for k in range(2, levels - 1):
        mine = pl.pallas_call(
            functools.partial(forward_level, plan, k),
            out_shape=front_shape,
            in_specs=[smem] + [vmem] * (2 + cols + PAIR * k),
            out_specs=vmem,
            scratch_shapes=[store(k)],
            compiler_params=params,
            name=f"forward_level_{k}",
        )(table, rights, inverses, *sources(k), *fronts)
        fronts += exchange(mine)

    last = levels - 1
    acc_shape = pltpu.VMEM((last * lanes + 1, share, width), F32)
    half_last, solved, acc, *terms = pl.pallas_call(
        functools.partial(turn_level, plan, last),
        out_shape=(segment_shape, segment_shape, acc_shape, own_shape, front_shape),
        in_specs=[smem] + [vmem] * (2 + cols + PAIR * last),
        out_specs=(vmem,) * 5,
        scratch_shapes=[store(last)],
        compiler_params=params,
        name="turn_level",
    )(table, rights, inverses, *sources(last), *fronts)
    done = [held(solved)]
    for k in range(last - 1, 0, -1):
        solved, acc, *terms = pl.pallas_call(
            functools.partial(backward_level, plan, k),
            out_shape=(segment_shape, acc_shape, own_shape, front_shape),
            in_specs=[smem] + [vmem] * (4 + cols),
            out_specs=(vmem,) * 4,
            input_output_aliases={4: 1},
            compiler_params=params,
            name=f"backward_level_{k}",
        )(
            table,
            inverses,
            fronts[PAIR * k],
            exchange_back(*terms),
            held(acc),
            *sources(k),
        )
        done.insert(0, held(solved))
    shares = pl.pallas_call(
        functools.partial(finish, plan),
        out_shape=pltpu.VMEM((cols, 2 * rows, share, width), BF16),
        in_specs=[smem] + [vmem] * (1 + 2 * levels),
        out_specs=vmem,
        scratch_shapes=[
            pltpu.VMEM((levels, share, width), BF16),
            pltpu.VMEM((levels, share, width), BF16),
        ],
        compiler_params=params,
        name="finish",
    )(table, inverses, exchange_back(*terms), *fronts[::PAIR], held(half_last), *done)
    whole = lax.all_to_all(shares, "col", 0, 0, tiled=True)
    whole = whole.transpose(1, 0, 2, 3).reshape(2, rows, 1, probes, width)
    return whole[0], whole[1]


def solution(mesh):
    return jax.shard_map(
        per_device,
        mesh=mesh,
        in_specs=(
            P(None, "chain", None, None),
            P(None, "chain", "col"),
            P(None, "chain", "col", None, None),
            P(None, "chain", None, None),
            P(),
        ),
        out_specs=(P(None, "chain", None, None), P(None, "chain", None, None)),
        check_vma=False,
    )
```

```python
import functools
import jax
import jax.numpy as jnp
from jax import lax
from jax.experimental import pallas as pl
from jax.experimental.pallas import tpu as pltpu
from jax.sharding import PartitionSpec as P

BF16 = jnp.bfloat16
F32 = jnp.float32
NT = (((1,), (1,)), ((), ()))
NN = (((1,), (0,)), ((), ()))
CODE_ROWS = 16
TABLE_ROWS = 8
PAIR = 2


class Plan:
    def __init__(self, lanes, cols, rows, entries, share, width, levels):
        self.lanes, self.cols, self.rows, self.entries = lanes, cols, rows, entries
        self.share, self.width, self.levels = share, width, levels
        self.deep = entries * width
        self.near = range(1, min(3, levels))
        self.far = range(min(3, levels), levels)

    def slots(self, level):
        return max(0, self.rows - (self.levels - level)), min(level, self.rows - 1)


def locate(plan, level, sizes):
    lane = lax.axis_index("chain")
    start = jnp.int32(0)
    for k in range(level):
        start = start + sizes[k]
    slot = (start - lane + (plan.lanes - 1)) // plan.lanes
    live = (slot < plan.rows) & (slot * plan.lanes + lane < start + sizes[level])
    low, high = plan.slots(level)
    return jnp.clip(slot, low, high), live


def weights_of(plan, level, sources):
    base = (level - (plan.near if level in plan.near else plan.far)[0]) * plan.deep
    return jnp.concatenate(
        [
            source[base + e * plan.width : base + (e + 1) * plan.width, :]
            for source in sources
            for e in range(plan.entries)
        ],
        axis=1,
    )


def places_of(plan, level, table):
    return [
        table[level, s * plan.entries + e]
        for s in range(plan.cols)
        for e in range(plan.entries)
    ]


def gather_store(plan, level, earlier, store):
    part = plan.lanes // PAIR
    for k in range(PAIR * level):
        store[pl.ds(k * part, part)] = earlier[k][...]
    store[level * plan.lanes] = jnp.zeros(store.shape[1:], BF16)


def half_segment(plan, level, table, right, inverse, sources, store):
    chosen = jnp.concatenate([store[at] for at in places_of(plan, level, table)], axis=1)
    weights = weights_of(plan, level, sources)
    summed = lax.dot_general(chosen, weights, NT, preferred_element_type=F32)
    rest = (right[level].astype(F32) - summed).astype(BF16)
    return lax.dot_general(
        rest, inverse[level], NT, preferred_element_type=F32
    ).astype(BF16)


def add_terms(plan, level, table, segment, sources, acc):
    weights = weights_of(plan, level, sources)
    terms = lax.dot_general(segment, weights, NN, preferred_element_type=F32)
    for j, at in enumerate(places_of(plan, level, table)):
        acc[at] = acc[at] + terms[:, j * plan.width : (j + 1) * plan.width]


def give_terms(plan, level, acc, own, other):
    part = plan.lanes // PAIR
    own[...] = acc[pl.ds(level * plan.lanes, part)]
    other[...] = acc[pl.ds(level * plan.lanes + part, part)].astype(BF16)


def add_other(own, other, out):
    out[...] = (own[...] + other[...].astype(F32)).astype(BF16)


def forward_first(plan, *refs):
    level_size, pattern, factor, right, inverse = refs[:5]
    out, near, far, rights, inverses, sizes = refs[5:11]
    pats, blocks, sides, diagonal, wide, sems = refs[11:]
    col = lax.axis_index("col")
    loads = [
        (level_size, sizes),
        (inverse, diagonal),
        (right.at[:, col], sides),
        (factor, blocks),
        (pattern, pats),
    ]
    copies = [
        pltpu.make_async_copy(source, target, sems.at[i])
        for i, (source, target) in enumerate(loads)
    ]
    for c in copies:
        c.start()
    wide[...] = jnp.zeros(wide.shape, F32)
    copies[0].wait()
    slots = [locate(plan, k, sizes)[0] for k in range(plan.levels)]
    copies[1].wait()
    copies[2].wait()
    segment = lax.dot_general(
        sides[0], diagonal[0], NT, preferred_element_type=F32
    ).astype(BF16)
    out[...] = jnp.broadcast_to(segment[None], out.shape)
    for k in range(plan.levels):
        rights[k] = sides[slots[k]]
        inverses[k] = diagonal[slots[k]]
    copies[3].wait()
    copies[4].wait()
    for target, levels in ((near, plan.near), (far, plan.far)):
        for i, k in enumerate(levels):
            at = pl.multiple_of(slots[k] * plan.deep, plan.deep)
            target[pl.ds(i * plan.deep, plan.deep), :] = blocks[
                pl.ds(at, plan.deep), :
            ]
    for k in range(1, plan.levels):
        wide[pl.ds(k, 1), pl.ds(0, plan.entries)] = pats[slots[k]].astype(F32)
    near[pl.ds(len(plan.near) * plan.deep, CODE_ROWS), :] = wide[...].astype(BF16)


def fill_table(plan, sizes, near, table):
    core = lax.rem(lax.axis_index("chain"), PAIR)
    split = len(plan.near) * plan.deep
    shape = (TABLE_ROWS, plan.width)
    row_level = lax.broadcasted_iota(jnp.int32, shape, 0)
    entry = lax.broadcasted_iota(jnp.int32, shape, 1)
    alive = jnp.zeros(shape, jnp.int32)
    ends = []
    for k in range(plan.levels):
        ends.append((ends[-1] if ends else 0) + sizes[k])
        live = locate(plan, k, sizes)[1].astype(jnp.int32)
        alive = alive + jnp.where(row_level == k, live, 0)
    total = jnp.zeros(shape, jnp.int32)
    for s in range(plan.cols):
        columns = near[s][split : split + CODE_ROWS, :].astype(F32)[:TABLE_ROWS]
        columns = columns.astype(jnp.int32)
        level = jnp.zeros(shape, jnp.int32)
        for end in ends:
            level = level + (columns >= end).astype(jnp.int32)
        there = lax.rem(columns, plan.lanes)
        apart = lax.rem(there, PAIR) ^ core
        there = apart * (plan.lanes // PAIR) + there // PAIR
        place = jnp.where(
            (level < row_level) & (alive > 0),
            level * plan.lanes + there,
            row_level * plan.lanes,
        )
        place = jnp.where(entry < plan.entries, place, 0)
        total = total + (pltpu.roll(place, s * plan.entries, 1) if s else place)
    own = entry * plan.lanes + lax.axis_index("chain")
    own_level = jnp.zeros(shape, jnp.int32)
    for end in ends:
        own_level = own_level + (own >= end).astype(jnp.int32)
    table[...] = jnp.where(row_level == TABLE_ROWS - 1, own_level, total)


def after(far, segment, same):
    pass


def forward_second(plan, *refs):
    sizes, right, inverse = refs[:3]
    fronts = refs[3 : 3 + PAIR]
    near = refs[3 + PAIR : 3 + PAIR + plan.cols]
    out, table, draft, store, sem = refs[3 + PAIR + plan.cols :]
    fill_table(plan, sizes, near, draft)
    copy = pltpu.make_async_copy(draft, table, sem)
    copy.start()
    gather_store(plan, 1, fronts, store)
    copy.wait()
    segment = half_segment(plan, 1, table, right, inverse, near, store)
    out[...] = jnp.broadcast_to(segment[None], out.shape)


def forward_level(plan, level, *refs):
    table, right, inverse = refs[:3]
    sources = refs[3 : 3 + plan.cols]
    earlier = refs[3 + plan.cols : 3 + plan.cols + PAIR * level]
    out, store = refs[3 + plan.cols + PAIR * level :]
    gather_store(plan, level, earlier, store)
    segment = half_segment(plan, level, table, right, inverse, sources, store)
    out[...] = jnp.broadcast_to(segment[None], out.shape)


def turn_level(plan, level, *refs):
    table, right, inverse = refs[:3]
    sources = refs[3 : 3 + plan.cols]
    earlier = refs[3 + plan.cols : 3 + plan.cols + PAIR * level]
    half, solved, acc, own, other, store = refs[3 + plan.cols + PAIR * level :]
    gather_store(plan, level, earlier, store)
    acc[...] = jnp.zeros(acc.shape, F32)
    segment = half_segment(plan, level, table, right, inverse, sources, store)
    half[...] = segment
    segment = lax.dot_general(
        segment, inverse[level], NN, preferred_element_type=F32
    ).astype(BF16)
    solved[...] = segment
    add_terms(plan, level, table, segment, sources, acc)
    give_terms(plan, level - 1, acc, own, other)


def solve_back(half, inverse, arrived):
    summed = jnp.sum(arrived[...].astype(F32), axis=0)
    rest = (half.astype(F32) - summed).astype(BF16)
    return lax.dot_general(rest, inverse, NN, preferred_element_type=F32).astype(BF16)


def backward_level(plan, level, *refs):
    table, inverse, front, arrived, _ = refs[:5]
    sources = refs[5 : 5 + plan.cols]
    solved, acc, own, other = refs[5 + plan.cols :]
    segment = solve_back(front[lax.axis_index("chain") // PAIR], inverse[level], arrived)
    solved[...] = segment
    add_terms(plan, level, table, segment, sources, acc)
    give_terms(plan, level - 1, acc, own, other)


def finish(plan, *refs):
    levels = plan.levels
    table, inverse, arrived = refs[:3]
    fronts = refs[3 : 2 + levels]
    half_last = refs[2 + levels]
    done = refs[3 + levels : 2 + 2 * levels]
    out, hbuf, sbuf = refs[2 + 2 * levels :]
    lane = lax.axis_index("chain")
    for k in range(levels - 1):
        hbuf[k] = fronts[k][lane // PAIR]
        sbuf[k + 1] = done[k][...]
    hbuf[levels - 1] = half_last[...]
    sbuf[0] = solve_back(hbuf[0], inverse[0], arrived)
    for r in range(plan.rows):
        level = table[TABLE_ROWS - 1, r]
        h, s = hbuf[level], sbuf[level]
        for q in range(plan.cols):
            out[q, r] = h
            out[q, plan.rows + r] = s


def per_device(rhs, pattern, factor, inverse, level_size):
    lanes = lax.axis_size("chain")
    cols = lax.axis_size("col")
    rows, _, probes, width = rhs.shape
    entries = pattern.shape[2]
    levels = level_size.shape[0]
    share = probes // cols
    plan = Plan(lanes, cols, rows, entries, share, width, levels)

    smem = pl.BlockSpec(memory_space=pltpu.SMEM)
    hbm = pl.BlockSpec(memory_space=pltpu.HBM)
    vmem = pl.BlockSpec(memory_space=pltpu.VMEM)
    segment_shape = pltpu.VMEM((share, width), BF16)
    front_shape = pltpu.VMEM((lanes // PAIR, share, width), BF16)
    own_shape = pltpu.VMEM((lanes // PAIR, share, width), F32)
    params = pltpu.CompilerParams(vmem_limit_bytes=12 * 1024 * 1024)

    def far_off(x):
        return pltpu.with_memory_space_constraint(x, pltpu.HBM)

    def held(x):
        return pltpu.with_memory_space_constraint(x, pltpu.VMEM)

    def scalars(x):
        return pltpu.with_memory_space_constraint(x, pltpu.SMEM)

    def store(level):
        return pltpu.VMEM((level * lanes + 1, share, width), BF16)

    def across(x):
        return held(lax.ppermute(x, "chain", [(i, i ^ 1) for i in range(lanes)]))

    def among(x):
        groups = [list(range(i, lanes, PAIR)) for i in range(PAIR)]
        return held(
            lax.all_to_all(x, "chain", 0, 0, tiled=True, axis_index_groups=groups)
        )

    def exchange(x):
        own = among(x)
        return [own, across(own)]

    def exchange_back(own, other):
        whole = pl.pallas_call(
            add_other,
            out_shape=front_shape,
            in_specs=[vmem, vmem],
            out_specs=vmem,
            compiler_params=params,
            name="add_other",
        )(held(own), across(other))
        return among(whole)

    def around(x):
        return [held(x)] + [
            held(lax.ppermute(x, "col", [(i, i ^ s) for i in range(cols)]))
            for s in (2, 3, 1)
        ]

    factor = far_off(factor.reshape(rows * plan.entries * width, width))
    far_shape = pltpu.VMEM((len(plan.far) * plan.deep, width), BF16)
    first, own, later, rights, inverses, sizes = pl.pallas_call(
        functools.partial(forward_first, plan),
        out_shape=(
            front_shape,
            pltpu.VMEM((len(plan.near) * plan.deep + CODE_ROWS, width), BF16),
            far_shape,
            pltpu.VMEM((levels, share, width), BF16),
            pltpu.VMEM((levels, width, width), BF16),
            pltpu.SMEM((levels,), jnp.int32),
        ),
        in_specs=[hbm] * 5,
        out_specs=(vmem,) * 5 + (smem,),
        scratch_shapes=[
            pltpu.VMEM((rows, 1, entries), jnp.int32),
            pltpu.VMEM((rows * plan.deep, width), BF16),
            pltpu.VMEM((rows, share, width), BF16),
            pltpu.VMEM((rows, width, width), BF16),
            pltpu.VMEM((CODE_ROWS, width), F32),
            pltpu.SemaphoreType.DMA((5,)),
        ],
        compiler_params=params,
        name="forward_first",
    )(
        far_off(level_size),
        far_off(pattern),
        factor,
        far_off(rhs.reshape(rows, cols, share, width)),
        far_off(inverse.reshape(rows, width, width)),
    )
    rights, inverses, sizes = held(rights), held(inverses), scalars(sizes)
    near = around(own)
    fronts = exchange(first)
    later = pl.pallas_call(
        after,
        out_shape=far_shape,
        in_specs=[vmem, vmem],
        out_specs=vmem,
        input_output_aliases={0: 0},
        compiler_params=params,
        name="after",
    )(held(later), fronts[0])
    far = around(later)

    mine, table = pl.pallas_call(
        functools.partial(forward_second, plan),
        out_shape=(
            front_shape,
            pltpu.SMEM((TABLE_ROWS, width), jnp.int32),
        ),
        in_specs=[smem] + [vmem] * (2 + PAIR + cols),
        out_specs=(vmem, smem),
        scratch_shapes=[
            pltpu.VMEM((TABLE_ROWS, width), jnp.int32),
            store(1),
            pltpu.SemaphoreType.DMA,
        ],
        compiler_params=params,
        name="forward_second",
    )(sizes, rights, inverses, *fronts, *near)
    table = scalars(table)
    fronts += exchange(mine)

    def sources(level):
        return near if level in plan.near else far

    for k in range(2, levels - 1):
        mine = pl.pallas_call(
            functools.partial(forward_level, plan, k),
            out_shape=front_shape,
            in_specs=[smem] + [vmem] * (2 + cols + PAIR * k),
            out_specs=vmem,
            scratch_shapes=[store(k)],
            compiler_params=params,
            name=f"forward_level_{k}",
        )(table, rights, inverses, *sources(k), *fronts)
        fronts += exchange(mine)

    last = levels - 1
    acc_shape = pltpu.VMEM((last * lanes + 1, share, width), F32)
    half_last, solved, acc, *terms = pl.pallas_call(
        functools.partial(turn_level, plan, last),
        out_shape=(segment_shape, segment_shape, acc_shape, own_shape, front_shape),
        in_specs=[smem] + [vmem] * (2 + cols + PAIR * last),
        out_specs=(vmem,) * 5,
        scratch_shapes=[store(last)],
        compiler_params=params,
        name="turn_level",
    )(table, rights, inverses, *sources(last), *fronts)
    done = [held(solved)]
    for k in range(last - 1, 0, -1):
        solved, acc, *terms = pl.pallas_call(
            functools.partial(backward_level, plan, k),
            out_shape=(segment_shape, acc_shape, own_shape, front_shape),
            in_specs=[smem] + [vmem] * (4 + cols),
            out_specs=(vmem,) * 4,
            input_output_aliases={4: 1},
            compiler_params=params,
            name=f"backward_level_{k}",
        )(
            table,
            inverses,
            fronts[PAIR * k],
            exchange_back(*terms),
            held(acc),
            *sources(k),
        )
        done.insert(0, held(solved))
    shares = pl.pallas_call(
        functools.partial(finish, plan),
        out_shape=pltpu.VMEM((cols, 2 * rows, share, width), BF16),
        in_specs=[smem] + [vmem] * (1 + 2 * levels),
        out_specs=vmem,
        scratch_shapes=[
            pltpu.VMEM((levels, share, width), BF16),
            pltpu.VMEM((levels, share, width), BF16),
        ],
        compiler_params=params,
        name="finish",
    )(table, inverses, exchange_back(*terms), *fronts[::PAIR], held(half_last), *done)
    whole = lax.all_to_all(shares, "col", 0, 0, tiled=True)
    whole = whole.transpose(1, 0, 2, 3).reshape(2, rows, 1, probes, width)
    return whole[0], whole[1]


def solution(mesh):
    return jax.shard_map(
        per_device,
        mesh=mesh,
        in_specs=(
            P(None, "chain", None, None),
            P(None, "chain", "col"),
            P(None, "chain", "col", None, None),
            P(None, "chain", None, None),
            P(),
        ),
        out_specs=(P(None, "chain", None, None), P(None, "chain", None, None)),
        check_vma=False,
    )
```

```python
import functools
import jax
import jax.numpy as jnp
from jax import lax
from jax.experimental import pallas as pl
from jax.experimental.pallas import tpu as pltpu
from jax.sharding import PartitionSpec as P

BF16 = jnp.bfloat16
F32 = jnp.float32
NT = (((1,), (1,)), ((), ()))
NN = (((1,), (0,)), ((), ()))
CODE_ROWS = 16
TABLE_ROWS = 8
PAIR = 2


class Plan:
    def __init__(self, lanes, cols, rows, entries, share, width, levels):
        self.lanes, self.cols, self.rows, self.entries = lanes, cols, rows, entries
        self.share, self.width, self.levels = share, width, levels
        self.deep = entries * width
        self.near = range(1, min(3, levels))
        self.far = range(min(3, levels), levels)

    def slots(self, level):
        return max(0, self.rows - (self.levels - level)), min(level, self.rows - 1)


def locate(plan, level, sizes):
    lane = lax.axis_index("chain")
    start = jnp.int32(0)
    for k in range(level):
        start = start + sizes[k]
    slot = (start - lane + (plan.lanes - 1)) // plan.lanes
    live = (slot < plan.rows) & (slot * plan.lanes + lane < start + sizes[level])
    low, high = plan.slots(level)
    return jnp.clip(slot, low, high), live


def weights_of(plan, level, sources):
    base = (level - (plan.near if level in plan.near else plan.far)[0]) * plan.deep
    return jnp.concatenate(
        [
            source[base + e * plan.width : base + (e + 1) * plan.width, :]
            for source in sources
            for e in range(plan.entries)
        ],
        axis=1,
    )


def places_of(plan, level, table):
    return [
        table[level, s * plan.entries + e]
        for s in range(plan.cols)
        for e in range(plan.entries)
    ]


def gather_store(plan, level, earlier, store):
    part = plan.lanes // PAIR
    for k in range(PAIR * level):
        store[pl.ds(k * part, part)] = earlier[k][...]
    store[level * plan.lanes] = jnp.zeros(store.shape[1:], BF16)


def half_segment(plan, level, table, right, inverse, sources, store):
    chosen = jnp.concatenate([store[at] for at in places_of(plan, level, table)], axis=1)
    weights = weights_of(plan, level, sources)
    summed = lax.dot_general(chosen, weights, NT, preferred_element_type=F32)
    rest = (right[level].astype(F32) - summed).astype(BF16)
    return lax.dot_general(
        rest, inverse[level], NT, preferred_element_type=F32
    ).astype(BF16)


def add_terms(plan, level, table, segment, sources, acc):
    weights = weights_of(plan, level, sources)
    terms = lax.dot_general(segment, weights, NN, preferred_element_type=F32)
    for j, at in enumerate(places_of(plan, level, table)):
        acc[at] = acc[at] + terms[:, j * plan.width : (j + 1) * plan.width]


def give_terms(plan, level, acc, own, other):
    part = plan.lanes // PAIR
    own[...] = acc[pl.ds(level * plan.lanes, part)]
    other[...] = acc[pl.ds(level * plan.lanes + part, part)].astype(BF16)


def add_other(own, other, out):
    out[...] = (own[...] + other[...].astype(F32)).astype(BF16)


def forward_first(plan, *refs):
    level_size, pattern, factor, right, inverse = refs[:5]
    out, near, far, rights, inverses, sizes = refs[5:11]
    pats, blocks, sides, diagonal, wide, sems = refs[11:]
    col = lax.axis_index("col")
    loads = [
        (level_size, sizes),
        (inverse, diagonal),
        (right.at[:, col], sides),
        (factor, blocks),
        (pattern, pats),
    ]
    copies = [
        pltpu.make_async_copy(source, target, sems.at[i])
        for i, (source, target) in enumerate(loads)
    ]
    for c in copies:
        c.start()
    wide[...] = jnp.zeros(wide.shape, F32)
    copies[0].wait()
    slots = [locate(plan, k, sizes)[0] for k in range(plan.levels)]
    copies[1].wait()
    copies[2].wait()
    segment = lax.dot_general(
        sides[0], diagonal[0], NT, preferred_element_type=F32
    ).astype(BF16)
    out[...] = jnp.broadcast_to(segment[None], out.shape)
    for k in range(plan.levels):
        rights[k] = sides[slots[k]]
        inverses[k] = diagonal[slots[k]]
    copies[3].wait()
    copies[4].wait()
    for target, levels in ((near, plan.near), (far, plan.far)):
        for i, k in enumerate(levels):
            at = pl.multiple_of(slots[k] * plan.deep, plan.deep)
            target[pl.ds(i * plan.deep, plan.deep), :] = blocks[
                pl.ds(at, plan.deep), :
            ]
    for k in range(1, plan.levels):
        wide[pl.ds(k, 1), pl.ds(0, plan.entries)] = pats[slots[k]].astype(F32)
    near[pl.ds(len(plan.near) * plan.deep, CODE_ROWS), :] = wide[...].astype(BF16)


def fill_table(plan, sizes, near, table):
    core = lax.rem(lax.axis_index("chain"), PAIR)
    split = len(plan.near) * plan.deep
    shape = (TABLE_ROWS, plan.width)
    row_level = lax.broadcasted_iota(jnp.int32, shape, 0)
    entry = lax.broadcasted_iota(jnp.int32, shape, 1)
    alive = jnp.zeros(shape, jnp.int32)
    ends = []
    for k in range(plan.levels):
        ends.append((ends[-1] if ends else 0) + sizes[k])
        live = locate(plan, k, sizes)[1].astype(jnp.int32)
        alive = alive + jnp.where(row_level == k, live, 0)
    total = jnp.zeros(shape, jnp.int32)
    for s in range(plan.cols):
        columns = near[s][split : split + CODE_ROWS, :].astype(F32)[:TABLE_ROWS]
        columns = columns.astype(jnp.int32)
        level = jnp.zeros(shape, jnp.int32)
        for end in ends:
            level = level + (columns >= end).astype(jnp.int32)
        there = lax.rem(columns, plan.lanes)
        apart = lax.rem(there, PAIR) ^ core
        there = apart * (plan.lanes // PAIR) + there // PAIR
        place = jnp.where(
            (level < row_level) & (alive > 0),
            level * plan.lanes + there,
            row_level * plan.lanes,
        )
        place = jnp.where(entry < plan.entries, place, 0)
        total = total + (pltpu.roll(place, s * plan.entries, 1) if s else place)
    own = entry * plan.lanes + lax.axis_index("chain")
    own_level = jnp.zeros(shape, jnp.int32)
    for end in ends:
        own_level = own_level + (own >= end).astype(jnp.int32)
    table[...] = jnp.where(row_level == TABLE_ROWS - 1, own_level, total)


def after(far, segment, same):
    pass


def forward_second(plan, *refs):
    sizes, right, inverse = refs[:3]
    fronts = refs[3 : 3 + PAIR]
    near = refs[3 + PAIR : 3 + PAIR + plan.cols]
    out, table, draft, store, sem = refs[3 + PAIR + plan.cols :]
    fill_table(plan, sizes, near, draft)
    copy = pltpu.make_async_copy(draft, table, sem)
    copy.start()
    gather_store(plan, 1, fronts, store)
    copy.wait()
    segment = half_segment(plan, 1, table, right, inverse, near, store)
    out[...] = jnp.broadcast_to(segment[None], out.shape)


def forward_level(plan, level, *refs):
    table, right, inverse = refs[:3]
    sources = refs[3 : 3 + plan.cols]
    earlier = refs[3 + plan.cols : 3 + plan.cols + PAIR * level]
    out, store = refs[3 + plan.cols + PAIR * level :]
    gather_store(plan, level, earlier, store)
    segment = half_segment(plan, level, table, right, inverse, sources, store)
    out[...] = jnp.broadcast_to(segment[None], out.shape)


def clear(front, acc):
    acc[...] = jnp.zeros(acc.shape, F32)


def turn_level(plan, level, *refs):
    table, right, inverse = refs[:3]
    sources = refs[3 : 3 + plan.cols]
    earlier = refs[3 + plan.cols : 3 + plan.cols + PAIR * level]
    refs = refs[1:]
    half, solved, acc, own, other, store = refs[3 + plan.cols + PAIR * level :]
    gather_store(plan, level, earlier, store)
    segment = half_segment(plan, level, table, right, inverse, sources, store)
    half[...] = segment
    segment = lax.dot_general(
        segment, inverse[level], NN, preferred_element_type=F32
    ).astype(BF16)
    solved[...] = segment
    add_terms(plan, level, table, segment, sources, acc)
    give_terms(plan, level - 1, acc, own, other)


def solve_back(half, inverse, arrived):
    summed = jnp.sum(arrived[...].astype(F32), axis=0)
    rest = (half.astype(F32) - summed).astype(BF16)
    return lax.dot_general(rest, inverse, NN, preferred_element_type=F32).astype(BF16)


def backward_level(plan, level, *refs):
    table, inverse, front, arrived, _ = refs[:5]
    sources = refs[5 : 5 + plan.cols]
    solved, acc, own, other = refs[5 + plan.cols :]
    segment = solve_back(front[lax.axis_index("chain") // PAIR], inverse[level], arrived)
    solved[...] = segment
    add_terms(plan, level, table, segment, sources, acc)
    give_terms(plan, level - 1, acc, own, other)


def finish(plan, *refs):
    levels = plan.levels
    table, inverse, arrived = refs[:3]
    fronts = refs[3 : 2 + levels]
    half_last = refs[2 + levels]
    done = refs[3 + levels : 2 + 2 * levels]
    out, hbuf, sbuf = refs[2 + 2 * levels :]
    lane = lax.axis_index("chain")
    for k in range(levels - 1):
        hbuf[k] = fronts[k][lane // PAIR]
        sbuf[k + 1] = done[k][...]
    hbuf[levels - 1] = half_last[...]
    sbuf[0] = solve_back(hbuf[0], inverse[0], arrived)
    for r in range(plan.rows):
        level = table[TABLE_ROWS - 1, r]
        h, s = hbuf[level], sbuf[level]
        for q in range(plan.cols):
            out[q, r] = h
            out[q, plan.rows + r] = s


def per_device(rhs, pattern, factor, inverse, level_size):
    lanes = lax.axis_size("chain")
    cols = lax.axis_size("col")
    rows, _, probes, width = rhs.shape
    entries = pattern.shape[2]
    levels = level_size.shape[0]
    share = probes // cols
    plan = Plan(lanes, cols, rows, entries, share, width, levels)

    smem = pl.BlockSpec(memory_space=pltpu.SMEM)
    hbm = pl.BlockSpec(memory_space=pltpu.HBM)
    vmem = pl.BlockSpec(memory_space=pltpu.VMEM)
    segment_shape = pltpu.VMEM((share, width), BF16)
    front_shape = pltpu.VMEM((lanes // PAIR, share, width), BF16)
    own_shape = pltpu.VMEM((lanes // PAIR, share, width), F32)
    params = pltpu.CompilerParams(vmem_limit_bytes=12 * 1024 * 1024)

    def far_off(x):
        return pltpu.with_memory_space_constraint(x, pltpu.HBM)

    def held(x):
        return pltpu.with_memory_space_constraint(x, pltpu.VMEM)

    def scalars(x):
        return pltpu.with_memory_space_constraint(x, pltpu.SMEM)

    def store(level):
        return pltpu.VMEM((level * lanes + 1, share, width), BF16)

    def across(x):
        return held(lax.ppermute(x, "chain", [(i, i ^ 1) for i in range(lanes)]))

    def among(x):
        groups = [list(range(i, lanes, PAIR)) for i in range(PAIR)]
        return held(
            lax.all_to_all(x, "chain", 0, 0, tiled=True, axis_index_groups=groups)
        )

    def exchange(x):
        own = among(x)
        return [own, across(own)]

    def exchange_back(own, other):
        whole = pl.pallas_call(
            add_other,
            out_shape=front_shape,
            in_specs=[vmem, vmem],
            out_specs=vmem,
            compiler_params=params,
            name="add_other",
        )(held(own), across(other))
        return among(whole)

    def around(x):
        return [held(x)] + [
            held(lax.ppermute(x, "col", [(i, i ^ s) for i in range(cols)]))
            for s in (2, 3, 1)
        ]

    factor = far_off(factor.reshape(rows * plan.entries * width, width))
    far_shape = pltpu.VMEM((len(plan.far) * plan.deep, width), BF16)
    first, own, later, rights, inverses, sizes = pl.pallas_call(
        functools.partial(forward_first, plan),
        out_shape=(
            front_shape,
            pltpu.VMEM((len(plan.near) * plan.deep + CODE_ROWS, width), BF16),
            far_shape,
            pltpu.VMEM((levels, share, width), BF16),
            pltpu.VMEM((levels, width, width), BF16),
            pltpu.SMEM((levels,), jnp.int32),
        ),
        in_specs=[hbm] * 5,
        out_specs=(vmem,) * 5 + (smem,),
        scratch_shapes=[
            pltpu.VMEM((rows, 1, entries), jnp.int32),
            pltpu.VMEM((rows * plan.deep, width), BF16),
            pltpu.VMEM((rows, share, width), BF16),
            pltpu.VMEM((rows, width, width), BF16),
            pltpu.VMEM((CODE_ROWS, width), F32),
            pltpu.SemaphoreType.DMA((5,)),
        ],
        compiler_params=params,
        name="forward_first",
    )(
        far_off(level_size),
        far_off(pattern),
        factor,
        far_off(rhs.reshape(rows, cols, share, width)),
        far_off(inverse.reshape(rows, width, width)),
    )
    rights, inverses, sizes = held(rights), held(inverses), scalars(sizes)
    near = around(own)
    fronts = exchange(first)
    later = pl.pallas_call(
        after,
        out_shape=far_shape,
        in_specs=[vmem, vmem],
        out_specs=vmem,
        input_output_aliases={0: 0},
        compiler_params=params,
        name="after",
    )(held(later), fronts[0])
    far = around(later)

    mine, table = pl.pallas_call(
        functools.partial(forward_second, plan),
        out_shape=(
            front_shape,
            pltpu.SMEM((TABLE_ROWS, width), jnp.int32),
        ),
        in_specs=[smem] + [vmem] * (2 + PAIR + cols),
        out_specs=(vmem, smem),
        scratch_shapes=[
            pltpu.VMEM((TABLE_ROWS, width), jnp.int32),
            store(1),
            pltpu.SemaphoreType.DMA,
        ],
        compiler_params=params,
        name="forward_second",
    )(sizes, rights, inverses, *fronts, *near)
    table = scalars(table)
    fronts += exchange(mine)

    def sources(level):
        return near if level in plan.near else far

    for k in range(2, levels - 1):
        mine = pl.pallas_call(
            functools.partial(forward_level, plan, k),
            out_shape=front_shape,
            in_specs=[smem] + [vmem] * (2 + cols + PAIR * k),
            out_specs=vmem,
            scratch_shapes=[store(k)],
            compiler_params=params,
            name=f"forward_level_{k}",
        )(table, rights, inverses, *sources(k), *fronts)
        fronts += exchange(mine)

    last = levels - 1
    acc_shape = pltpu.VMEM((last * lanes + 1, share, width), F32)
    cleared = pl.pallas_call(
        clear,
        out_shape=acc_shape,
        in_specs=[vmem],
        out_specs=vmem,
        compiler_params=params,
        name="clear",
    )(fronts[PAIR * (last - 1)])
    half_last, solved, acc, *terms = pl.pallas_call(
        functools.partial(turn_level, plan, last),
        out_shape=(segment_shape, segment_shape, acc_shape, own_shape, front_shape),
        in_specs=[smem] + [vmem] * (3 + cols + PAIR * last),
        out_specs=(vmem,) * 5,
        input_output_aliases={3 + cols + PAIR * last: 2},
        scratch_shapes=[store(last)],
        compiler_params=params,
        name="turn_level",
    )(table, rights, inverses, *sources(last), *fronts, held(cleared))
    done = [held(solved)]
    for k in range(last - 1, 0, -1):
        solved, acc, *terms = pl.pallas_call(
            functools.partial(backward_level, plan, k),
            out_shape=(segment_shape, acc_shape, own_shape, front_shape),
            in_specs=[smem] + [vmem] * (4 + cols),
            out_specs=(vmem,) * 4,
            input_output_aliases={4: 1},
            compiler_params=params,
            name=f"backward_level_{k}",
        )(
            table,
            inverses,
            fronts[PAIR * k],
            exchange_back(*terms),
            held(acc),
            *sources(k),
        )
        done.insert(0, held(solved))
    shares = pl.pallas_call(
        functools.partial(finish, plan),
        out_shape=pltpu.VMEM((cols, 2 * rows, share, width), BF16),
        in_specs=[smem] + [vmem] * (1 + 2 * levels),
        out_specs=vmem,
        scratch_shapes=[
            pltpu.VMEM((levels, share, width), BF16),
            pltpu.VMEM((levels, share, width), BF16),
        ],
        compiler_params=params,
        name="finish",
    )(table, inverses, exchange_back(*terms), *fronts[::PAIR], held(half_last), *done)
    whole = lax.all_to_all(shares, "col", 0, 0, tiled=True)
    whole = whole.transpose(1, 0, 2, 3).reshape(2, rows, 1, probes, width)
    return whole[0], whole[1]


def solution(mesh):
    return jax.shard_map(
        per_device,
        mesh=mesh,
        in_specs=(
            P(None, "chain", None, None),
            P(None, "chain", "col"),
            P(None, "chain", "col", None, None),
            P(None, "chain", None, None),
            P(),
        ),
        out_specs=(P(None, "chain", None, None), P(None, "chain", None, None)),
        check_vma=False,
    )
```

```python
import functools
import jax
import jax.numpy as jnp
from jax import lax
from jax.experimental import pallas as pl
from jax.experimental.pallas import tpu as pltpu
from jax.sharding import PartitionSpec as P

BF16 = jnp.bfloat16
F32 = jnp.float32
NT = (((1,), (1,)), ((), ()))
NN = (((1,), (0,)), ((), ()))
CODE_ROWS = 16
TABLE_ROWS = 8
PAIR = 2


class Plan:
    def __init__(self, lanes, cols, rows, entries, share, width, levels):
        self.lanes, self.cols, self.rows, self.entries = lanes, cols, rows, entries
        self.share, self.width, self.levels = share, width, levels
        self.deep = entries * width
        self.near = range(1, min(3, levels))
        self.far = range(min(3, levels), levels)

    def slots(self, level):
        return max(0, self.rows - (self.levels - level)), min(level, self.rows - 1)


def locate(plan, level, sizes):
    lane = lax.axis_index("chain")
    start = jnp.int32(0)
    for k in range(level):
        start = start + sizes[k]
    slot = (start - lane + (plan.lanes - 1)) // plan.lanes
    live = (slot < plan.rows) & (slot * plan.lanes + lane < start + sizes[level])
    low, high = plan.slots(level)
    return jnp.clip(slot, low, high), live


def weights_of(plan, level, sources):
    base = (level - (plan.near if level in plan.near else plan.far)[0]) * plan.deep
    return jnp.concatenate(
        [
            source[base + e * plan.width : base + (e + 1) * plan.width, :]
            for source in sources
            for e in range(plan.entries)
        ],
        axis=1,
    )


def places_of(plan, level, table):
    return [
        table[level, s * plan.entries + e]
        for s in range(plan.cols)
        for e in range(plan.entries)
    ]


def gather_store(plan, level, earlier, store):
    part = plan.lanes // PAIR
    for k in range(PAIR * level):
        store[pl.ds(k * part, part)] = earlier[k][...]
    store[level * plan.lanes] = jnp.zeros(store.shape[1:], BF16)


def half_segment(plan, level, table, right, inverse, sources, store):
    chosen = jnp.concatenate([store[at] for at in places_of(plan, level, table)], axis=1)
    weights = weights_of(plan, level, sources)
    summed = lax.dot_general(chosen, weights, NT, preferred_element_type=F32)
    rest = (right[level].astype(F32) - summed).astype(BF16)
    return lax.dot_general(
        rest, inverse[level], NT, preferred_element_type=F32
    ).astype(BF16)


def add_terms(plan, level, table, segment, sources, acc):
    weights = weights_of(plan, level, sources)
    terms = lax.dot_general(segment, weights, NN, preferred_element_type=F32)
    for j, at in enumerate(places_of(plan, level, table)):
        acc[at] = acc[at] + terms[:, j * plan.width : (j + 1) * plan.width]


def give_terms(plan, level, acc, own, other):
    part = plan.lanes // PAIR
    own[...] = acc[pl.ds(level * plan.lanes, part)]
    other[...] = acc[pl.ds(level * plan.lanes + part, part)].astype(BF16)


def add_other(own, other, out):
    out[...] = (own[...] + other[...].astype(F32)).astype(BF16)


def forward_first(plan, *refs):
    level_size, pattern, factor, right, inverse = refs[:5]
    out, near, far, rights, inverses, sizes = refs[5:11]
    pats, blocks, sides, diagonal, wide, sems = refs[11:]
    col = lax.axis_index("col")
    loads = [
        (level_size, sizes),
        (inverse, diagonal),
        (right.at[:, col], sides),
        (factor, blocks),
        (pattern, pats),
    ]
    copies = [
        pltpu.make_async_copy(source, target, sems.at[i])
        for i, (source, target) in enumerate(loads)
    ]
    for c in copies:
        c.start()
    wide[...] = jnp.zeros(wide.shape, F32)
    copies[0].wait()
    slots = [locate(plan, k, sizes)[0] for k in range(plan.levels)]
    copies[1].wait()
    copies[2].wait()
    segment = lax.dot_general(
        sides[0], diagonal[0], NT, preferred_element_type=F32
    ).astype(BF16)
    out[...] = jnp.broadcast_to(segment[None], out.shape)
    for k in range(plan.levels):
        rights[k] = sides[slots[k]]
        inverses[k] = diagonal[slots[k]]
    copies[3].wait()
    copies[4].wait()
    for target, levels in ((near, plan.near), (far, plan.far)):
        for i, k in enumerate(levels):
            at = pl.multiple_of(slots[k] * plan.deep, plan.deep)
            target[pl.ds(i * plan.deep, plan.deep), :] = blocks[
                pl.ds(at, plan.deep), :
            ]
    for k in range(1, plan.levels):
        wide[pl.ds(k, 1), pl.ds(0, plan.entries)] = pats[slots[k]].astype(F32)
    near[pl.ds(len(plan.near) * plan.deep, CODE_ROWS), :] = wide[...].astype(BF16)


def fill_table(plan, sizes, near, table):
    core = lax.rem(lax.axis_index("chain"), PAIR)
    split = len(plan.near) * plan.deep
    shape = (TABLE_ROWS, plan.width)
    row_level = lax.broadcasted_iota(jnp.int32, shape, 0)
    entry = lax.broadcasted_iota(jnp.int32, shape, 1)
    alive = jnp.zeros(shape, jnp.int32)
    ends = []
    for k in range(plan.levels):
        ends.append((ends[-1] if ends else 0) + sizes[k])
        live = locate(plan, k, sizes)[1].astype(jnp.int32)
        alive = alive + jnp.where(row_level == k, live, 0)
    total = jnp.zeros(shape, jnp.int32)
    for s in range(plan.cols):
        columns = near[s][split : split + CODE_ROWS, :].astype(F32)[:TABLE_ROWS]
        columns = columns.astype(jnp.int32)
        level = jnp.zeros(shape, jnp.int32)
        for end in ends:
            level = level + (columns >= end).astype(jnp.int32)
        there = lax.rem(columns, plan.lanes)
        apart = lax.rem(there, PAIR) ^ core
        there = apart * (plan.lanes // PAIR) + there // PAIR
        place = jnp.where(
            (level < row_level) & (alive > 0),
            level * plan.lanes + there,
            row_level * plan.lanes,
        )
        place = jnp.where(entry < plan.entries, place, 0)
        total = total + (pltpu.roll(place, s * plan.entries, 1) if s else place)
    own = entry * plan.lanes + lax.axis_index("chain")
    own_level = jnp.zeros(shape, jnp.int32)
    for end in ends:
        own_level = own_level + (own >= end).astype(jnp.int32)
    table[...] = jnp.where(row_level == TABLE_ROWS - 1, own_level, total)


def after(far, segment, same):
    pass


def forward_second(plan, *refs):
    sizes, right, inverse = refs[:3]
    fronts = refs[3 : 3 + PAIR]
    near = refs[3 + PAIR : 3 + PAIR + plan.cols]
    out, table, draft, store, sem = refs[3 + PAIR + plan.cols :]
    fill_table(plan, sizes, near, draft)
    copy = pltpu.make_async_copy(draft, table, sem)
    copy.start()
    gather_store(plan, 1, fronts, store)
    copy.wait()
    segment = half_segment(plan, 1, table, right, inverse, near, store)
    out[...] = jnp.broadcast_to(segment[None], out.shape)


def forward_level(plan, level, *refs):
    table, right, inverse = refs[:3]
    sources = refs[3 : 3 + plan.cols]
    earlier = refs[3 + plan.cols : 3 + plan.cols + PAIR * level]
    out, store = refs[3 + plan.cols + PAIR * level :]
    gather_store(plan, level, earlier, store)
    segment = half_segment(plan, level, table, right, inverse, sources, store)
    out[...] = jnp.broadcast_to(segment[None], out.shape)


def clear(front, acc):
    acc[...] = jnp.zeros(acc.shape, F32)


def turn_level(plan, level, *refs):
    table, right, inverse = refs[:3]
    sources = refs[3 : 3 + plan.cols]
    earlier = refs[3 + plan.cols : 3 + plan.cols + PAIR * level]
    refs = refs[1:]
    half, solved, acc, own, other, store = refs[3 + plan.cols + PAIR * level :]
    gather_store(plan, level, earlier, store)
    segment = half_segment(plan, level, table, right, inverse, sources, store)
    half[...] = segment
    segment = lax.dot_general(
        segment, inverse[level], NN, preferred_element_type=F32
    ).astype(BF16)
    solved[...] = segment
    add_terms(plan, level, table, segment, sources, acc)
    give_terms(plan, level - 1, acc, own, other)


def solve_back(half, inverse, arrived):
    summed = jnp.sum(arrived[...].astype(F32), axis=0)
    rest = (half.astype(F32) - summed).astype(BF16)
    return lax.dot_general(rest, inverse, NN, preferred_element_type=F32).astype(BF16)


def backward_level(plan, level, *refs):
    table, inverse, front, arrived, _ = refs[:5]
    sources = refs[5 : 5 + plan.cols]
    solved, acc, own, other = refs[5 + plan.cols :]
    segment = solve_back(front[lax.axis_index("chain") // PAIR], inverse[level], arrived)
    solved[...] = segment
    add_terms(plan, level, table, segment, sources, acc)
    give_terms(plan, level - 1, acc, own, other)


def finish(plan, *refs):
    levels = plan.levels
    table, inverse, arrived = refs[:3]
    fronts = refs[3 : 2 + levels]
    half_last = refs[2 + levels]
    done = refs[3 + levels : 2 + 2 * levels]
    out, hbuf, sbuf = refs[2 + 2 * levels :]
    lane = lax.axis_index("chain")
    for k in range(levels - 1):
        hbuf[k] = fronts[k][lane // PAIR]
        sbuf[k + 1] = done[k][...]
    hbuf[levels - 1] = half_last[...]
    sbuf[0] = solve_back(hbuf[0], inverse[0], arrived)
    for r in range(plan.rows):
        level = table[TABLE_ROWS - 1, r]
        h, s = hbuf[level], sbuf[level]
        for q in range(plan.cols):
            out[q, r] = h
            out[q, plan.rows + r] = s


def per_device(rhs, pattern, factor, inverse, level_size):
    lanes = lax.axis_size("chain")
    cols = lax.axis_size("col")
    rows, _, probes, width = rhs.shape
    entries = pattern.shape[2]
    levels = level_size.shape[0]
    share = probes // cols
    plan = Plan(lanes, cols, rows, entries, share, width, levels)

    smem = pl.BlockSpec(memory_space=pltpu.SMEM)
    hbm = pl.BlockSpec(memory_space=pltpu.HBM)
    vmem = pl.BlockSpec(memory_space=pltpu.VMEM)
    segment_shape = pltpu.VMEM((share, width), BF16)
    front_shape = pltpu.VMEM((lanes // PAIR, share, width), BF16)
    own_shape = pltpu.VMEM((lanes // PAIR, share, width), F32)
    params = pltpu.CompilerParams(vmem_limit_bytes=12 * 1024 * 1024)

    def far_off(x):
        return pltpu.with_memory_space_constraint(x, pltpu.HBM)

    def held(x):
        return pltpu.with_memory_space_constraint(x, pltpu.VMEM)

    def scalars(x):
        return pltpu.with_memory_space_constraint(x, pltpu.SMEM)

    def store(level):
        return pltpu.VMEM((level * lanes + 1, share, width), BF16)

    def across(x):
        return held(lax.ppermute(x, "chain", [(i, i ^ 1) for i in range(lanes)]))

    def among(x):
        groups = [list(range(i, lanes, PAIR)) for i in range(PAIR)]
        return held(
            lax.all_to_all(x, "chain", 0, 0, tiled=True, axis_index_groups=groups)
        )

    def exchange(x):
        own = among(x)
        return [own, across(own)]

    def exchange_back(own, other):
        whole = pl.pallas_call(
            add_other,
            out_shape=front_shape,
            in_specs=[vmem, vmem],
            out_specs=vmem,
            compiler_params=params,
            name="add_other",
        )(held(own), across(other))
        return among(whole)

    def around(x):
        return [held(x)] + [
            held(lax.ppermute(x, "col", [(i, i ^ s) for i in range(cols)]))
            for s in (2, 1, 3)
        ]

    factor = far_off(factor.reshape(rows * plan.entries * width, width))
    far_shape = pltpu.VMEM((len(plan.far) * plan.deep, width), BF16)
    first, own, later, rights, inverses, sizes = pl.pallas_call(
        functools.partial(forward_first, plan),
        out_shape=(
            front_shape,
            pltpu.VMEM((len(plan.near) * plan.deep + CODE_ROWS, width), BF16),
            far_shape,
            pltpu.VMEM((levels, share, width), BF16),
            pltpu.VMEM((levels, width, width), BF16),
            pltpu.SMEM((levels,), jnp.int32),
        ),
        in_specs=[hbm] * 5,
        out_specs=(vmem,) * 5 + (smem,),
        scratch_shapes=[
            pltpu.VMEM((rows, 1, entries), jnp.int32),
            pltpu.VMEM((rows * plan.deep, width), BF16),
            pltpu.VMEM((rows, share, width), BF16),
            pltpu.VMEM((rows, width, width), BF16),
            pltpu.VMEM((CODE_ROWS, width), F32),
            pltpu.SemaphoreType.DMA((5,)),
        ],
        compiler_params=params,
        name="forward_first",
    )(
        far_off(level_size),
        far_off(pattern),
        factor,
        far_off(rhs.reshape(rows, cols, share, width)),
        far_off(inverse.reshape(rows, width, width)),
    )
    rights, inverses, sizes = held(rights), held(inverses), scalars(sizes)
    near = around(own)
    fronts = exchange(first)
    later = pl.pallas_call(
        after,
        out_shape=far_shape,
        in_specs=[vmem, vmem],
        out_specs=vmem,
        input_output_aliases={0: 0},
        compiler_params=params,
        name="after",
    )(held(later), fronts[0])
    far = around(later)

    mine, table = pl.pallas_call(
        functools.partial(forward_second, plan),
        out_shape=(
            front_shape,
            pltpu.SMEM((TABLE_ROWS, width), jnp.int32),
        ),
        in_specs=[smem] + [vmem] * (2 + PAIR + cols),
        out_specs=(vmem, smem),
        scratch_shapes=[
            pltpu.VMEM((TABLE_ROWS, width), jnp.int32),
            store(1),
            pltpu.SemaphoreType.DMA,
        ],
        compiler_params=params,
        name="forward_second",
    )(sizes, rights, inverses, *fronts, *near)
    table = scalars(table)
    fronts += exchange(mine)

    def sources(level):
        return near if level in plan.near else far

    for k in range(2, levels - 1):
        mine = pl.pallas_call(
            functools.partial(forward_level, plan, k),
            out_shape=front_shape,
            in_specs=[smem] + [vmem] * (2 + cols + PAIR * k),
            out_specs=vmem,
            scratch_shapes=[store(k)],
            compiler_params=params,
            name=f"forward_level_{k}",
        )(table, rights, inverses, *sources(k), *fronts)
        fronts += exchange(mine)

    last = levels - 1
    acc_shape = pltpu.VMEM((last * lanes + 1, share, width), F32)
    cleared = pl.pallas_call(
        clear,
        out_shape=acc_shape,
        in_specs=[vmem],
        out_specs=vmem,
        compiler_params=params,
        name="clear",
    )(fronts[PAIR * (last - 1)])
    half_last, solved, acc, *terms = pl.pallas_call(
        functools.partial(turn_level, plan, last),
        out_shape=(segment_shape, segment_shape, acc_shape, own_shape, front_shape),
        in_specs=[smem] + [vmem] * (3 + cols + PAIR * last),
        out_specs=(vmem,) * 5,
        input_output_aliases={3 + cols + PAIR * last: 2},
        scratch_shapes=[store(last)],
        compiler_params=params,
        name="turn_level",
    )(table, rights, inverses, *sources(last), *fronts, held(cleared))
    done = [held(solved)]
    for k in range(last - 1, 0, -1):
        solved, acc, *terms = pl.pallas_call(
            functools.partial(backward_level, plan, k),
            out_shape=(segment_shape, acc_shape, own_shape, front_shape),
            in_specs=[smem] + [vmem] * (4 + cols),
            out_specs=(vmem,) * 4,
            input_output_aliases={4: 1},
            compiler_params=params,
            name=f"backward_level_{k}",
        )(
            table,
            inverses,
            fronts[PAIR * k],
            exchange_back(*terms),
            held(acc),
            *sources(k),
        )
        done.insert(0, held(solved))
    shares = pl.pallas_call(
        functools.partial(finish, plan),
        out_shape=pltpu.VMEM((cols, 2 * rows, share, width), BF16),
        in_specs=[smem] + [vmem] * (1 + 2 * levels),
        out_specs=vmem,
        scratch_shapes=[
            pltpu.VMEM((levels, share, width), BF16),
            pltpu.VMEM((levels, share, width), BF16),
        ],
        compiler_params=params,
        name="finish",
    )(table, inverses, exchange_back(*terms), *fronts[::PAIR], held(half_last), *done)
    whole = lax.all_to_all(shares, "col", 0, 0, tiled=True)
    whole = whole.transpose(1, 0, 2, 3).reshape(2, rows, 1, probes, width)
    return whole[0], whole[1]


def solution(mesh):
    return jax.shard_map(
        per_device,
        mesh=mesh,
        in_specs=(
            P(None, "chain", None, None),
            P(None, "chain", "col"),
            P(None, "chain", "col", None, None),
            P(None, "chain", None, None),
            P(),
        ),
        out_specs=(P(None, "chain", None, None), P(None, "chain", None, None)),
        check_vma=False,
    )
```

```python
import functools
import jax
import jax.numpy as jnp
from jax import lax
from jax.experimental import pallas as pl
from jax.experimental.pallas import tpu as pltpu
from jax.sharding import PartitionSpec as P

BF16 = jnp.bfloat16
F32 = jnp.float32
NT = (((1,), (1,)), ((), ()))
NN = (((1,), (0,)), ((), ()))
CODE_ROWS = 16
TABLE_ROWS = 8
PAIR = 2


class Plan:
    def __init__(self, lanes, cols, rows, entries, share, width, levels):
        self.lanes, self.cols, self.rows, self.entries = lanes, cols, rows, entries
        self.share, self.width, self.levels = share, width, levels
        self.deep = entries * width
        self.near = range(1, min(3, levels))
        self.far = range(min(3, levels), levels)

    def slots(self, level):
        return max(0, self.rows - (self.levels - level)), min(level, self.rows - 1)


def locate(plan, level, sizes):
    lane = lax.axis_index("chain")
    start = jnp.int32(0)
    for k in range(level):
        start = start + sizes[k]
    slot = (start - lane + (plan.lanes - 1)) // plan.lanes
    live = (slot < plan.rows) & (slot * plan.lanes + lane < start + sizes[level])
    low, high = plan.slots(level)
    return jnp.clip(slot, low, high), live


def weights_of(plan, level, sources):
    base = (level - (plan.near if level in plan.near else plan.far)[0]) * plan.deep
    return jnp.concatenate(
        [
            source[base + e * plan.width : base + (e + 1) * plan.width, :]
            for source in sources
            for e in range(plan.entries)
        ],
        axis=1,
    )


def places_of(plan, level, table):
    return [
        table[level, s * plan.entries + e]
        for s in range(plan.cols)
        for e in range(plan.entries)
    ]


def gather_store(plan, level, earlier, store):
    part = plan.lanes // PAIR
    for k in range(PAIR * level):
        store[pl.ds(k * part, part)] = earlier[k][...]
    store[level * plan.lanes] = jnp.zeros(store.shape[1:], BF16)


def half_segment(plan, level, table, right, inverse, sources, store):
    chosen = jnp.concatenate([store[at] for at in places_of(plan, level, table)], axis=1)
    weights = weights_of(plan, level, sources)
    summed = lax.dot_general(chosen, weights, NT, preferred_element_type=F32)
    rest = (right[level].astype(F32) - summed).astype(BF16)
    return lax.dot_general(
        rest, inverse[level], NT, preferred_element_type=F32
    ).astype(BF16)


def add_terms(plan, level, table, segment, sources, acc):
    weights = weights_of(plan, level, sources)
    terms = lax.dot_general(segment, weights, NN, preferred_element_type=F32)
    for j, at in enumerate(places_of(plan, level, table)):
        acc[at] = acc[at] + terms[:, j * plan.width : (j + 1) * plan.width]


def give_terms(plan, level, acc, own, other):
    part = plan.lanes // PAIR
    own[...] = acc[pl.ds(level * plan.lanes, part)]
    other[...] = acc[pl.ds(level * plan.lanes + part, part)].astype(BF16)


def add_other(own, other, out):
    out[...] = (own[...] + other[...].astype(F32)).astype(BF16)


def forward_first(plan, *refs):
    level_size, pattern, factor, right, inverse = refs[:5]
    out, near, far, rights, inverses, sizes = refs[5:11]
    pats, blocks, sides, diagonal, wide, sems = refs[11:]
    col = lax.axis_index("col")
    loads = [
        (level_size, sizes),
        (inverse, diagonal),
        (right.at[:, col], sides),
        (factor, blocks),
        (pattern, pats),
    ]
    copies = [
        pltpu.make_async_copy(source, target, sems.at[i])
        for i, (source, target) in enumerate(loads)
    ]
    for c in copies:
        c.start()
    wide[...] = jnp.zeros(wide.shape, F32)
    copies[0].wait()
    slots = [locate(plan, k, sizes)[0] for k in range(plan.levels)]
    copies[1].wait()
    copies[2].wait()
    segment = lax.dot_general(
        sides[0], diagonal[0], NT, preferred_element_type=F32
    ).astype(BF16)
    out[...] = jnp.broadcast_to(segment[None], out.shape)
    for k in range(plan.levels):
        rights[k] = sides[slots[k]]
        inverses[k] = diagonal[slots[k]]
    copies[3].wait()
    copies[4].wait()
    for target, levels in ((near, plan.near), (far, plan.far)):
        for i, k in enumerate(levels):
            at = pl.multiple_of(slots[k] * plan.deep, plan.deep)
            target[pl.ds(i * plan.deep, plan.deep), :] = blocks[
                pl.ds(at, plan.deep), :
            ]
    for k in range(1, plan.levels):
        wide[pl.ds(k, 1), pl.ds(0, plan.entries)] = pats[slots[k]].astype(F32)
    near[pl.ds(len(plan.near) * plan.deep, CODE_ROWS), :] = wide[...].astype(BF16)


def fill_table(plan, sizes, near, table):
    core = lax.rem(lax.axis_index("chain"), PAIR)
    split = len(plan.near) * plan.deep
    shape = (TABLE_ROWS, plan.width)
    row_level = lax.broadcasted_iota(jnp.int32, shape, 0)
    entry = lax.broadcasted_iota(jnp.int32, shape, 1)
    alive = jnp.zeros(shape, jnp.int32)
    ends = []
    for k in range(plan.levels):
        ends.append((ends[-1] if ends else 0) + sizes[k])
        live = locate(plan, k, sizes)[1].astype(jnp.int32)
        alive = alive + jnp.where(row_level == k, live, 0)
    total = jnp.zeros(shape, jnp.int32)
    for s in range(plan.cols):
        columns = near[s][split : split + CODE_ROWS, :].astype(F32)[:TABLE_ROWS]
        columns = columns.astype(jnp.int32)
        level = jnp.zeros(shape, jnp.int32)
        for end in ends:
            level = level + (columns >= end).astype(jnp.int32)
        there = lax.rem(columns, plan.lanes)
        apart = lax.rem(there, PAIR) ^ core
        there = apart * (plan.lanes // PAIR) + there // PAIR
        place = jnp.where(
            (level < row_level) & (alive > 0),
            level * plan.lanes + there,
            row_level * plan.lanes,
        )
        place = jnp.where(entry < plan.entries, place, 0)
        total = total + (pltpu.roll(place, s * plan.entries, 1) if s else place)
    own = entry * plan.lanes + lax.axis_index("chain")
    own_level = jnp.zeros(shape, jnp.int32)
    for end in ends:
        own_level = own_level + (own >= end).astype(jnp.int32)
    table[...] = jnp.where(row_level == TABLE_ROWS - 1, own_level, total)


def after(far, segment, same):
    pass


def forward_second(plan, *refs):
    sizes, right, inverse = refs[:3]
    fronts = refs[3 : 3 + PAIR]
    near = refs[3 + PAIR : 3 + PAIR + plan.cols]
    out, table, draft, store, sem = refs[3 + PAIR + plan.cols :]
    fill_table(plan, sizes, near, draft)
    copy = pltpu.make_async_copy(draft, table, sem)
    copy.start()
    gather_store(plan, 1, fronts, store)
    copy.wait()
    segment = half_segment(plan, 1, table, right, inverse, near, store)
    out[...] = jnp.broadcast_to(segment[None], out.shape)


def forward_level(plan, level, *refs):
    table, right, inverse = refs[:3]
    sources = refs[3 : 3 + plan.cols]
    earlier = refs[3 + plan.cols : 3 + plan.cols + PAIR * level]
    out, store = refs[3 + plan.cols + PAIR * level :]
    gather_store(plan, level, earlier, store)
    segment = half_segment(plan, level, table, right, inverse, sources, store)
    out[...] = jnp.broadcast_to(segment[None], out.shape)


def clear(front, acc):
    acc[...] = jnp.zeros(acc.shape, F32)


def turn_level(plan, level, *refs):
    table, right, inverse = refs[:3]
    sources = refs[3 : 3 + plan.cols]
    earlier = refs[3 + plan.cols : 3 + plan.cols + PAIR * level]
    refs = refs[1:]
    half, solved, acc, own, other, store = refs[3 + plan.cols + PAIR * level :]
    gather_store(plan, level, earlier, store)
    segment = half_segment(plan, level, table, right, inverse, sources, store)
    half[...] = segment
    segment = lax.dot_general(
        segment, inverse[level], NN, preferred_element_type=F32
    ).astype(BF16)
    solved[...] = segment
    add_terms(plan, level, table, segment, sources, acc)
    give_terms(plan, level - 1, acc, own, other)


def solve_back(half, inverse, arrived):
    summed = jnp.sum(arrived[...].astype(F32), axis=0)
    rest = (half.astype(F32) - summed).astype(BF16)
    return lax.dot_general(rest, inverse, NN, preferred_element_type=F32).astype(BF16)


def backward_level(plan, level, *refs):
    table, inverse, front, arrived, _ = refs[:5]
    sources = refs[5 : 5 + plan.cols]
    solved, acc, own, other = refs[5 + plan.cols :]
    segment = solve_back(front[lax.axis_index("chain") // PAIR], inverse[level], arrived)
    solved[...] = segment
    add_terms(plan, level, table, segment, sources, acc)
    give_terms(plan, level - 1, acc, own, other)


def finish(plan, *refs):
    levels = plan.levels
    table, inverse, arrived = refs[:3]
    fronts = refs[3 : 2 + levels]
    half_last = refs[2 + levels]
    done = refs[3 + levels : 2 + 2 * levels]
    out, hbuf, sbuf = refs[2 + 2 * levels :]
    lane = lax.axis_index("chain")
    for k in range(levels - 1):
        hbuf[k] = fronts[k][lane // PAIR]
        sbuf[k + 1] = done[k][...]
    hbuf[levels - 1] = half_last[...]
    sbuf[0] = solve_back(hbuf[0], inverse[0], arrived)
    for r in range(plan.rows):
        level = table[TABLE_ROWS - 1, r]
        h, s = hbuf[level], sbuf[level]
        for q in range(plan.cols):
            out[q, r] = h
            out[q, plan.rows + r] = s


def per_device(rhs, pattern, factor, inverse, level_size):
    lanes = lax.axis_size("chain")
    cols = lax.axis_size("col")
    rows, _, probes, width = rhs.shape
    entries = pattern.shape[2]
    levels = level_size.shape[0]
    share = probes // cols
    plan = Plan(lanes, cols, rows, entries, share, width, levels)

    smem = pl.BlockSpec(memory_space=pltpu.SMEM)
    hbm = pl.BlockSpec(memory_space=pltpu.HBM)
    vmem = pl.BlockSpec(memory_space=pltpu.VMEM)
    segment_shape = pltpu.VMEM((share, width), BF16)
    front_shape = pltpu.VMEM((lanes // PAIR, share, width), BF16)
    own_shape = pltpu.VMEM((lanes // PAIR, share, width), F32)
    params = pltpu.CompilerParams(vmem_limit_bytes=12 * 1024 * 1024)

    def far_off(x):
        return pltpu.with_memory_space_constraint(x, pltpu.HBM)

    def held(x):
        return pltpu.with_memory_space_constraint(x, pltpu.VMEM)

    def scalars(x):
        return pltpu.with_memory_space_constraint(x, pltpu.SMEM)

    def store(level):
        return pltpu.VMEM((level * lanes + 1, share, width), BF16)

    def across(x):
        return held(lax.ppermute(x, "chain", [(i, i ^ 1) for i in range(lanes)]))

    def among(x):
        groups = [list(range(i, lanes, PAIR)) for i in range(PAIR)]
        return held(
            lax.all_to_all(x, "chain", 0, 0, tiled=True, axis_index_groups=groups)
        )

    def exchange(x):
        own = among(x)
        return [own, across(own)]

    def exchange_back(own, other):
        whole = pl.pallas_call(
            add_other,
            out_shape=front_shape,
            in_specs=[vmem, vmem],
            out_specs=vmem,
            compiler_params=params,
            name="add_other",
        )(held(own), across(other))
        return among(whole)

    def around(x, order):
        got = {
            s: held(lax.ppermute(x, "col", [(i, i ^ s) for i in range(cols)]))
            for s in order
        }
        return [held(x), got[2], got[3], got[1]]

    factor = far_off(factor.reshape(rows * plan.entries * width, width))
    far_shape = pltpu.VMEM((len(plan.far) * plan.deep, width), BF16)
    first, own, later, rights, inverses, sizes = pl.pallas_call(
        functools.partial(forward_first, plan),
        out_shape=(
            front_shape,
            pltpu.VMEM((len(plan.near) * plan.deep + CODE_ROWS, width), BF16),
            far_shape,
            pltpu.VMEM((levels, share, width), BF16),
            pltpu.VMEM((levels, width, width), BF16),
            pltpu.SMEM((levels,), jnp.int32),
        ),
        in_specs=[hbm] * 5,
        out_specs=(vmem,) * 5 + (smem,),
        scratch_shapes=[
            pltpu.VMEM((rows, 1, entries), jnp.int32),
            pltpu.VMEM((rows * plan.deep, width), BF16),
            pltpu.VMEM((rows, share, width), BF16),
            pltpu.VMEM((rows, width, width), BF16),
            pltpu.VMEM((CODE_ROWS, width), F32),
            pltpu.SemaphoreType.DMA((5,)),
        ],
        compiler_params=params,
        name="forward_first",
    )(
        far_off(level_size),
        far_off(pattern),
        factor,
        far_off(rhs.reshape(rows, cols, share, width)),
        far_off(inverse.reshape(rows, width, width)),
    )
    rights, inverses, sizes = held(rights), held(inverses), scalars(sizes)
    near = around(own, (2, 3, 1))
    fronts = exchange(first)
    later = pl.pallas_call(
        after,
        out_shape=far_shape,
        in_specs=[vmem, vmem],
        out_specs=vmem,
        input_output_aliases={0: 0},
        compiler_params=params,
        name="after",
    )(held(later), fronts[0])
    far = around(later, (1, 3, 2))

    mine, table = pl.pallas_call(
        functools.partial(forward_second, plan),
        out_shape=(
            front_shape,
            pltpu.SMEM((TABLE_ROWS, width), jnp.int32),
        ),
        in_specs=[smem] + [vmem] * (2 + PAIR + cols),
        out_specs=(vmem, smem),
        scratch_shapes=[
            pltpu.VMEM((TABLE_ROWS, width), jnp.int32),
            store(1),
            pltpu.SemaphoreType.DMA,
        ],
        compiler_params=params,
        name="forward_second",
    )(sizes, rights, inverses, *fronts, *near)
    table = scalars(table)
    fronts += exchange(mine)

    def sources(level):
        return near if level in plan.near else far

    for k in range(2, levels - 1):
        mine = pl.pallas_call(
            functools.partial(forward_level, plan, k),
            out_shape=front_shape,
            in_specs=[smem] + [vmem] * (2 + cols + PAIR * k),
            out_specs=vmem,
            scratch_shapes=[store(k)],
            compiler_params=params,
            name=f"forward_level_{k}",
        )(table, rights, inverses, *sources(k), *fronts)
        fronts += exchange(mine)

    last = levels - 1
    acc_shape = pltpu.VMEM((last * lanes + 1, share, width), F32)
    cleared = pl.pallas_call(
        clear,
        out_shape=acc_shape,
        in_specs=[vmem],
        out_specs=vmem,
        compiler_params=params,
        name="clear",
    )(fronts[PAIR * (last - 1)])
    half_last, solved, acc, *terms = pl.pallas_call(
        functools.partial(turn_level, plan, last),
        out_shape=(segment_shape, segment_shape, acc_shape, own_shape, front_shape),
        in_specs=[smem] + [vmem] * (3 + cols + PAIR * last),
        out_specs=(vmem,) * 5,
        input_output_aliases={3 + cols + PAIR * last: 2},
        scratch_shapes=[store(last)],
        compiler_params=params,
        name="turn_level",
    )(table, rights, inverses, *sources(last), *fronts, held(cleared))
    done = [held(solved)]
    for k in range(last - 1, 0, -1):
        solved, acc, *terms = pl.pallas_call(
            functools.partial(backward_level, plan, k),
            out_shape=(segment_shape, acc_shape, own_shape, front_shape),
            in_specs=[smem] + [vmem] * (4 + cols),
            out_specs=(vmem,) * 4,
            input_output_aliases={4: 1},
            compiler_params=params,
            name=f"backward_level_{k}",
        )(
            table,
            inverses,
            fronts[PAIR * k],
            exchange_back(*terms),
            held(acc),
            *sources(k),
        )
        done.insert(0, held(solved))
    shares = pl.pallas_call(
        functools.partial(finish, plan),
        out_shape=pltpu.VMEM((cols, 2 * rows, share, width), BF16),
        in_specs=[smem] + [vmem] * (1 + 2 * levels),
        out_specs=vmem,
        scratch_shapes=[
            pltpu.VMEM((levels, share, width), BF16),
            pltpu.VMEM((levels, share, width), BF16),
        ],
        compiler_params=params,
        name="finish",
    )(table, inverses, exchange_back(*terms), *fronts[::PAIR], held(half_last), *done)
    whole = lax.all_to_all(shares, "col", 0, 0, tiled=True)
    whole = whole.transpose(1, 0, 2, 3).reshape(2, rows, 1, probes, width)
    return whole[0], whole[1]


def solution(mesh):
    return jax.shard_map(
        per_device,
        mesh=mesh,
        in_specs=(
            P(None, "chain", None, None),
            P(None, "chain", "col"),
            P(None, "chain", "col", None, None),
            P(None, "chain", None, None),
            P(),
        ),
        out_specs=(P(None, "chain", None, None), P(None, "chain", None, None)),
        check_vma=False,
    )
```

```python
import functools
import jax
import jax.numpy as jnp
from jax import lax
from jax.experimental import pallas as pl
from jax.experimental.pallas import tpu as pltpu
from jax.sharding import PartitionSpec as P

BF16 = jnp.bfloat16
F32 = jnp.float32
NT = (((1,), (1,)), ((), ()))
NN = (((1,), (0,)), ((), ()))
CODE_ROWS = 16
TABLE_ROWS = 8
PAIR = 2


class Plan:
    def __init__(self, lanes, cols, rows, entries, share, width, levels):
        self.lanes, self.cols, self.rows, self.entries = lanes, cols, rows, entries
        self.share, self.width, self.levels = share, width, levels
        self.deep = entries * width
        self.near = range(1, min(3, levels))
        self.far = range(min(3, levels), levels)

    def slots(self, level):
        return max(0, self.rows - (self.levels - level)), min(level, self.rows - 1)


def locate(plan, level, sizes):
    lane = lax.axis_index("chain")
    start = jnp.int32(0)
    for k in range(level):
        start = start + sizes[k]
    slot = (start - lane + (plan.lanes - 1)) // plan.lanes
    live = (slot < plan.rows) & (slot * plan.lanes + lane < start + sizes[level])
    low, high = plan.slots(level)
    return jnp.clip(slot, low, high), live


def weights_of(plan, level, sources):
    base = (level - (plan.near if level in plan.near else plan.far)[0]) * plan.deep
    return jnp.concatenate(
        [
            source[base + e * plan.width : base + (e + 1) * plan.width, :]
            for source in sources
            for e in range(plan.entries)
        ],
        axis=1,
    )


def places_of(plan, level, table):
    return [
        table[level, s * plan.entries + e]
        for s in range(plan.cols)
        for e in range(plan.entries)
    ]


def gather_store(plan, level, earlier, store):
    part = plan.lanes // PAIR
    for k in range(PAIR * level):
        store[pl.ds(k * part, part)] = earlier[k][...]
    store[level * plan.lanes] = jnp.zeros(store.shape[1:], BF16)


def half_segment(plan, level, table, right, inverse, sources, store):
    chosen = jnp.concatenate([store[at] for at in places_of(plan, level, table)], axis=1)
    weights = weights_of(plan, level, sources)
    summed = lax.dot_general(chosen, weights, NT, preferred_element_type=F32)
    rest = (right[level].astype(F32) - summed).astype(BF16)
    return lax.dot_general(
        rest, inverse[level], NT, preferred_element_type=F32
    ).astype(BF16)


def add_terms(plan, level, table, segment, sources, acc):
    weights = weights_of(plan, level, sources)
    terms = lax.dot_general(segment, weights, NN, preferred_element_type=F32)
    for j, at in enumerate(places_of(plan, level, table)):
        acc[at] = acc[at] + terms[:, j * plan.width : (j + 1) * plan.width]


def give_terms(plan, level, acc, own, other):
    part = plan.lanes // PAIR
    own[...] = acc[pl.ds(level * plan.lanes, part)]
    other[...] = acc[pl.ds(level * plan.lanes + part, part)].astype(BF16)


def add_other(own, other, out):
    out[...] = (own[...] + other[...].astype(F32)).astype(BF16)


def forward_first(plan, *refs):
    level_size, pattern, factor, right, inverse = refs[:5]
    out, near, far, rights, inverses, sizes = refs[5:11]
    pats, blocks, sides, diagonal, wide, sems = refs[11:]
    col = lax.axis_index("col")
    loads = [
        (level_size, sizes),
        (factor, blocks),
        (inverse, diagonal),
        (right.at[:, col], sides),
        (pattern, pats),
    ]
    copies = [
        pltpu.make_async_copy(source, target, sems.at[i])
        for i, (source, target) in enumerate(loads)
    ]
    for c in copies:
        c.start()
    wide[...] = jnp.zeros(wide.shape, F32)
    copies[0].wait()
    slots = [locate(plan, k, sizes)[0] for k in range(plan.levels)]
    copies[2].wait()
    copies[3].wait()
    segment = lax.dot_general(
        sides[0], diagonal[0], NT, preferred_element_type=F32
    ).astype(BF16)
    out[...] = jnp.broadcast_to(segment[None], out.shape)
    for k in range(plan.levels):
        rights[k] = sides[slots[k]]
        inverses[k] = diagonal[slots[k]]
    copies[1].wait()
    copies[4].wait()
    for target, levels in ((near, plan.near), (far, plan.far)):
        for i, k in enumerate(levels):
            at = pl.multiple_of(slots[k] * plan.deep, plan.deep)
            target[pl.ds(i * plan.deep, plan.deep), :] = blocks[
                pl.ds(at, plan.deep), :
            ]
    for k in range(1, plan.levels):
        wide[pl.ds(k, 1), pl.ds(0, plan.entries)] = pats[slots[k]].astype(F32)
    near[pl.ds(len(plan.near) * plan.deep, CODE_ROWS), :] = wide[...].astype(BF16)


def fill_table(plan, sizes, near, table):
    core = lax.rem(lax.axis_index("chain"), PAIR)
    split = len(plan.near) * plan.deep
    shape = (TABLE_ROWS, plan.width)
    row_level = lax.broadcasted_iota(jnp.int32, shape, 0)
    entry = lax.broadcasted_iota(jnp.int32, shape, 1)
    alive = jnp.zeros(shape, jnp.int32)
    ends = []
    for k in range(plan.levels):
        ends.append((ends[-1] if ends else 0) + sizes[k])
        live = locate(plan, k, sizes)[1].astype(jnp.int32)
        alive = alive + jnp.where(row_level == k, live, 0)
    total = jnp.zeros(shape, jnp.int32)
    for s in range(plan.cols):
        columns = near[s][split : split + CODE_ROWS, :].astype(F32)[:TABLE_ROWS]
        columns = columns.astype(jnp.int32)
        level = jnp.zeros(shape, jnp.int32)
        for end in ends:
            level = level + (columns >= end).astype(jnp.int32)
        there = lax.rem(columns, plan.lanes)
        apart = lax.rem(there, PAIR) ^ core
        there = apart * (plan.lanes // PAIR) + there // PAIR
        place = jnp.where(
            (level < row_level) & (alive > 0),
            level * plan.lanes + there,
            row_level * plan.lanes,
        )
        place = jnp.where(entry < plan.entries, place, 0)
        total = total + (pltpu.roll(place, s * plan.entries, 1) if s else place)
    own = entry * plan.lanes + lax.axis_index("chain")
    own_level = jnp.zeros(shape, jnp.int32)
    for end in ends:
        own_level = own_level + (own >= end).astype(jnp.int32)
    table[...] = jnp.where(row_level == TABLE_ROWS - 1, own_level, total)


def after(far, segment, same):
    pass


def forward_second(plan, *refs):
    sizes, right, inverse = refs[:3]
    fronts = refs[3 : 3 + PAIR]
    near = refs[3 + PAIR : 3 + PAIR + plan.cols]
    out, table, draft, store, sem = refs[3 + PAIR + plan.cols :]
    fill_table(plan, sizes, near, draft)
    copy = pltpu.make_async_copy(draft, table, sem)
    copy.start()
    gather_store(plan, 1, fronts, store)
    copy.wait()
    segment = half_segment(plan, 1, table, right, inverse, near, store)
    out[...] = jnp.broadcast_to(segment[None], out.shape)


def forward_level(plan, level, *refs):
    table, right, inverse = refs[:3]
    sources = refs[3 : 3 + plan.cols]
    earlier = refs[3 + plan.cols : 3 + plan.cols + PAIR * level]
    out, store = refs[3 + plan.cols + PAIR * level :]
    gather_store(plan, level, earlier, store)
    segment = half_segment(plan, level, table, right, inverse, sources, store)
    out[...] = jnp.broadcast_to(segment[None], out.shape)


def clear(front, acc):
    acc[...] = jnp.zeros(acc.shape, F32)


def turn_level(plan, level, *refs):
    table, right, inverse = refs[:3]
    sources = refs[3 : 3 + plan.cols]
    earlier = refs[3 + plan.cols : 3 + plan.cols + PAIR * level]
    refs = refs[1:]
    half, solved, acc, own, other, store = refs[3 + plan.cols + PAIR * level :]
    gather_store(plan, level, earlier, store)
    segment = half_segment(plan, level, table, right, inverse, sources, store)
    half[...] = segment
    segment = lax.dot_general(
        segment, inverse[level], NN, preferred_element_type=F32
    ).astype(BF16)
    solved[...] = segment
    add_terms(plan, level, table, segment, sources, acc)
    give_terms(plan, level - 1, acc, own, other)


def solve_back(half, inverse, arrived):
    summed = jnp.sum(arrived[...].astype(F32), axis=0)
    rest = (half.astype(F32) - summed).astype(BF16)
    return lax.dot_general(rest, inverse, NN, preferred_element_type=F32).astype(BF16)


def backward_level(plan, level, *refs):
    table, inverse, front, arrived, _ = refs[:5]
    sources = refs[5 : 5 + plan.cols]
    solved, acc, own, other = refs[5 + plan.cols :]
    segment = solve_back(front[lax.axis_index("chain") // PAIR], inverse[level], arrived)
    solved[...] = segment
    add_terms(plan, level, table, segment, sources, acc)
    give_terms(plan, level - 1, acc, own, other)


def finish(plan, *refs):
    levels = plan.levels
    table, inverse, arrived = refs[:3]
    fronts = refs[3 : 2 + levels]
    half_last = refs[2 + levels]
    done = refs[3 + levels : 2 + 2 * levels]
    out, hbuf, sbuf = refs[2 + 2 * levels :]
    lane = lax.axis_index("chain")
    for k in range(levels - 1):
        hbuf[k] = fronts[k][lane // PAIR]
        sbuf[k + 1] = done[k][...]
    hbuf[levels - 1] = half_last[...]
    sbuf[0] = solve_back(hbuf[0], inverse[0], arrived)
    for r in range(plan.rows):
        level = table[TABLE_ROWS - 1, r]
        h, s = hbuf[level], sbuf[level]
        for q in range(plan.cols):
            out[q, r] = h
            out[q, plan.rows + r] = s


def per_device(rhs, pattern, factor, inverse, level_size):
    lanes = lax.axis_size("chain")
    cols = lax.axis_size("col")
    rows, _, probes, width = rhs.shape
    entries = pattern.shape[2]
    levels = level_size.shape[0]
    share = probes // cols
    plan = Plan(lanes, cols, rows, entries, share, width, levels)

    smem = pl.BlockSpec(memory_space=pltpu.SMEM)
    hbm = pl.BlockSpec(memory_space=pltpu.HBM)
    vmem = pl.BlockSpec(memory_space=pltpu.VMEM)
    segment_shape = pltpu.VMEM((share, width), BF16)
    front_shape = pltpu.VMEM((lanes // PAIR, share, width), BF16)
    own_shape = pltpu.VMEM((lanes // PAIR, share, width), F32)
    params = pltpu.CompilerParams(vmem_limit_bytes=12 * 1024 * 1024)

    def far_off(x):
        return pltpu.with_memory_space_constraint(x, pltpu.HBM)

    def held(x):
        return pltpu.with_memory_space_constraint(x, pltpu.VMEM)

    def scalars(x):
        return pltpu.with_memory_space_constraint(x, pltpu.SMEM)

    def store(level):
        return pltpu.VMEM((level * lanes + 1, share, width), BF16)

    def across(x):
        return held(lax.ppermute(x, "chain", [(i, i ^ 1) for i in range(lanes)]))

    def among(x):
        groups = [list(range(i, lanes, PAIR)) for i in range(PAIR)]
        return held(
            lax.all_to_all(x, "chain", 0, 0, tiled=True, axis_index_groups=groups)
        )

    def exchange(x):
        own = among(x)
        return [own, across(own)]

    def exchange_back(own, other):
        whole = pl.pallas_call(
            add_other,
            out_shape=front_shape,
            in_specs=[vmem, vmem],
            out_specs=vmem,
            compiler_params=params,
            name="add_other",
        )(held(own), across(other))
        return among(whole)

    def around(x):
        return [held(x)] + [
            held(lax.ppermute(x, "col", [(i, i ^ s) for i in range(cols)]))
            for s in (2, 3, 1)
        ]

    factor = far_off(factor.reshape(rows * plan.entries * width, width))
    far_shape = pltpu.VMEM((len(plan.far) * plan.deep, width), BF16)
    first, own, later, rights, inverses, sizes = pl.pallas_call(
        functools.partial(forward_first, plan),
        out_shape=(
            front_shape,
            pltpu.VMEM((len(plan.near) * plan.deep + CODE_ROWS, width), BF16),
            far_shape,
            pltpu.VMEM((levels, share, width), BF16),
            pltpu.VMEM((levels, width, width), BF16),
            pltpu.SMEM((levels,), jnp.int32),
        ),
        in_specs=[hbm] * 5,
        out_specs=(vmem,) * 5 + (smem,),
        scratch_shapes=[
            pltpu.VMEM((rows, 1, entries), jnp.int32),
            pltpu.VMEM((rows * plan.deep, width), BF16),
            pltpu.VMEM((rows, share, width), BF16),
            pltpu.VMEM((rows, width, width), BF16),
            pltpu.VMEM((CODE_ROWS, width), F32),
            pltpu.SemaphoreType.DMA((5,)),
        ],
        compiler_params=params,
        name="forward_first",
    )(
        far_off(level_size),
        far_off(pattern),
        factor,
        far_off(rhs.reshape(rows, cols, share, width)),
        far_off(inverse.reshape(rows, width, width)),
    )
    rights, inverses, sizes = held(rights), held(inverses), scalars(sizes)
    near = around(own)
    fronts = exchange(first)
    later = pl.pallas_call(
        after,
        out_shape=far_shape,
        in_specs=[vmem, vmem],
        out_specs=vmem,
        input_output_aliases={0: 0},
        compiler_params=params,
        name="after",
    )(held(later), fronts[0])
    far = around(later)

    mine, table = pl.pallas_call(
        functools.partial(forward_second, plan),
        out_shape=(
            front_shape,
            pltpu.SMEM((TABLE_ROWS, width), jnp.int32),
        ),
        in_specs=[smem] + [vmem] * (2 + PAIR + cols),
        out_specs=(vmem, smem),
        scratch_shapes=[
            pltpu.VMEM((TABLE_ROWS, width), jnp.int32),
            store(1),
            pltpu.SemaphoreType.DMA,
        ],
        compiler_params=params,
        name="forward_second",
    )(sizes, rights, inverses, *fronts, *near)
    table = scalars(table)
    fronts += exchange(mine)

    def sources(level):
        return near if level in plan.near else far

    for k in range(2, levels - 1):
        mine = pl.pallas_call(
            functools.partial(forward_level, plan, k),
            out_shape=front_shape,
            in_specs=[smem] + [vmem] * (2 + cols + PAIR * k),
            out_specs=vmem,
            scratch_shapes=[store(k)],
            compiler_params=params,
            name=f"forward_level_{k}",
        )(table, rights, inverses, *sources(k), *fronts)
        fronts += exchange(mine)

    last = levels - 1
    acc_shape = pltpu.VMEM((last * lanes + 1, share, width), F32)
    cleared = pl.pallas_call(
        clear,
        out_shape=acc_shape,
        in_specs=[vmem],
        out_specs=vmem,
        compiler_params=params,
        name="clear",
    )(fronts[PAIR * (last - 1)])
    half_last, solved, acc, *terms = pl.pallas_call(
        functools.partial(turn_level, plan, last),
        out_shape=(segment_shape, segment_shape, acc_shape, own_shape, front_shape),
        in_specs=[smem] + [vmem] * (3 + cols + PAIR * last),
        out_specs=(vmem,) * 5,
        input_output_aliases={3 + cols + PAIR * last: 2},
        scratch_shapes=[store(last)],
        compiler_params=params,
        name="turn_level",
    )(table, rights, inverses, *sources(last), *fronts, held(cleared))
    done = [held(solved)]
    for k in range(last - 1, 0, -1):
        solved, acc, *terms = pl.pallas_call(
            functools.partial(backward_level, plan, k),
            out_shape=(segment_shape, acc_shape, own_shape, front_shape),
            in_specs=[smem] + [vmem] * (4 + cols),
            out_specs=(vmem,) * 4,
            input_output_aliases={4: 1},
            compiler_params=params,
            name=f"backward_level_{k}",
        )(
            table,
            inverses,
            fronts[PAIR * k],
            exchange_back(*terms),
            held(acc),
            *sources(k),
        )
        done.insert(0, held(solved))
    shares = pl.pallas_call(
        functools.partial(finish, plan),
        out_shape=pltpu.VMEM((cols, 2 * rows, share, width), BF16),
        in_specs=[smem] + [vmem] * (1 + 2 * levels),
        out_specs=vmem,
        scratch_shapes=[
            pltpu.VMEM((levels, share, width), BF16),
            pltpu.VMEM((levels, share, width), BF16),
        ],
        compiler_params=params,
        name="finish",
    )(table, inverses, exchange_back(*terms), *fronts[::PAIR], held(half_last), *done)
    whole = lax.all_to_all(shares, "col", 0, 0, tiled=True)
    whole = whole.transpose(1, 0, 2, 3).reshape(2, rows, 1, probes, width)
    return whole[0], whole[1]


def solution(mesh):
    return jax.shard_map(
        per_device,
        mesh=mesh,
        in_specs=(
            P(None, "chain", None, None),
            P(None, "chain", "col"),
            P(None, "chain", "col", None, None),
            P(None, "chain", None, None),
            P(),
        ),
        out_specs=(P(None, "chain", None, None), P(None, "chain", None, None)),
        check_vma=False,
    )
```
